128 devices in a mesh: child: 8 (over z, core), grp: 16 (over y, x).
Axes of the slice: x: 4, y: 4, z: 4, core: 2. Of those that a mesh axis runs over, the one named last changes fastest.
Arguments:
- front_child: float32 [8, 4096, 4096], P('child', 'grp'), may hold values from -6 to 6
- left_factor: float32 [8, 4096, 1280], P('child', 'grp'), may hold values from -0.15625 to 0.15625
- right_factor: float32 [8, 1280, 4096], P('child', None, 'grp'), may hold values from -6 to 6
- child_map: int32 [8, 32], replicated, may hold values from 0 to 127, as said below
- parent_diag: float32 [16384], replicated, may hold values from 1 to 8
- lead_block: float32 [128, 128], replicated, may hold values from -4 to 304
- pivots: int32 [128], replicated, may hold values from 0 to 127, as said below
Outputs:
- front: float32 [8, 2048, 16, 1024], P('child', None, 'grp')
The draws below stay inside these ranges and needn't reach their ends.
Inputs may be any that keep to these rules, and one draw needn't show every extreme that they name: `child_map`: row k names the parent tile of each of child k's tiles; one child's tiles are distinct; of one child's tiles at most 3 have one value modulo 16, and at most 6 one value modulo 8; both bounds are reached by every child. `pivots`: A permutation of the first 128 rows.
All inputs are finite; a program needn't handle non-finite values.
Results may differ from the reference program's by a relative error of at most 0.0001.
Values sent between devices are 32-bit elements; how exact they have to be, the bound alone decides.
A program may use at most 128 MiB of HBM per device.

```python
import math
import jax
import jax.numpy as jnp
from jax import lax

NB = 128
CB = 4096
PIV = 1280
NP = 16384
CHILDREN = 8
CBT = 32
PT = 128
TR_DEV = 16
TC_DEV = 8
N_CHILD = 8
N_GRP = 16


def shared_pivots(key):
    return jax.random.permutation(jax.random.fold_in(key, 11), NB).astype(jnp.int32)


def draw_pivots(key, part):
    pivot_order = shared_pivots(key)
    return pivot_order


def draw_lead_block(key, part):
    pivot_order = shared_pivots(key)
    key = jax.random.fold_in(key, 5)
    first_key, second_key = jax.random.split(key)
    off_part = jnp.clip(jax.random.normal(first_key, (NB, NB), jnp.float32), -4.0, 4.0)
    strong = jax.random.uniform(second_key, (NB,), jnp.float32, 150.0, 300.0)
    placed = pivot_order[None, :] == jnp.arange(NB)[:, None]
    return off_part + jnp.where(placed, strong[None, :], 0.0)


def draw_child_map(key, part):
    key = jax.random.fold_in(key, 7)

    def one_child(child_key):
        key_list = jax.random.split(child_key, 4)
        base_count = CBT // N_GRP
        heavy_class = jax.random.randint(key_list[0], (), 0, N_CHILD)
        light_class = (heavy_class + jax.random.randint(key_list[1], (), 1, N_CHILD)) % N_CHILD
        classes = jnp.arange(N_GRP) % N_CHILD
        counts = base_count + (classes == heavy_class).astype(jnp.int32) - (classes == light_class).astype(jnp.int32)
        per_class = PT // N_GRP
        orders = jax.vmap(lambda class_key: jax.random.permutation(class_key, per_class))(jax.random.split(key_list[2], N_GRP))
        tile_ids = jnp.arange(N_GRP)[:, None] + N_GRP * orders
        chosen = jnp.arange(per_class)[None, :] < counts[:, None]
        scores = jax.random.permutation(key_list[3], N_GRP * per_class).reshape(N_GRP, per_class)
        scores = jnp.where(chosen, scores, scores + N_GRP * per_class)
        picked_order = jnp.argsort(scores.reshape(-1), stable=True)[:CBT]
        return tile_ids.reshape(-1)[picked_order].astype(jnp.int32)
    return jax.vmap(one_child)(jax.random.split(key, N_CHILD))


def block_scale(rng, dims, shards, least, high):
    loudness = 1.0
    for dim, blocks in shards:
        heights = jax.random.uniform(jax.random.fold_in(jax.random.fold_in(rng, 6), dim), (blocks,), jnp.float32, least / len(shards), high / len(shards))
        loudness = loudness * jnp.repeat(jnp.exp(heights), dims[dim] // blocks).reshape((-1,) + (1,) * (len(dims) - 1 - dim))
    return loudness


def normal_values(rng, shape, width, reach, cuts=(), held_as=jnp.bfloat16):
    factor_of = block_scale(rng, shape, cuts, -0.22, 0.18) if cuts else 1.0
    drawn = jax.random.normal(rng, shape, jnp.float32) * width * factor_of
    return jnp.minimum(jnp.maximum(drawn, -reach), reach).astype(held_as)


def setup_inputs(seed: int = 0) -> dict:
    keys = jax.random.split(jax.random.key(seed), 8)
    return {
        "front_child": normal_values(keys[0], (CHILDREN, CB, CB), 1.0, 6.0, ((0, 8), (1, 16)), jnp.float32),
        "left_factor": normal_values(keys[1], (CHILDREN, CB, PIV), PIV ** -0.5, 0.15625, ((0, 8), (1, 16)), jnp.float32),
        "right_factor": normal_values(keys[2], (CHILDREN, PIV, CB), 1.0, 6.0, ((0, 8), (2, 16)), jnp.float32),
        "child_map": draw_child_map(jax.random.fold_in(keys[7], 71), 0),
        "parent_diag": jnp.clip(jnp.exp(jax.random.uniform(keys[4], (NP,), jnp.float32, math.log(1.0), math.log(8.0))), 1.0, 8.0),
        "lead_block": draw_lead_block(jax.random.fold_in(keys[7], 71), 0),
        "pivots": draw_pivots(jax.random.fold_in(keys[7], 71), 0),
    }


def factor_tile(square):
    order_n = square.shape[0]
    positions = jnp.arange(order_n)

    def eliminate(j, working):
        pivot_value = working[j, j]
        column = jnp.where(positions > j, working[:, j] / pivot_value, 0.0)
        row_part = jnp.where(positions > j, working[j, :], 0.0)
        working = working - column[:, None] * row_part[None, :]
        working = working.at[:, j].set(jnp.where(positions > j, column, working[:, j]))
        return working
    return lax.fori_loop(0, order_n, eliminate, square)

def reference(front_child, left_factor, right_factor, child_map, parent_diag, lead_block, pivots):
    parent_front = jnp.zeros((PT, NB, PT, NB), jnp.float32)
    for child_id in range(N_CHILD):
        contribution = front_child[child_id] - jnp.dot(left_factor[child_id].astype(jnp.float32), right_factor[child_id].astype(jnp.float32), precision=lax.Precision.HIGHEST, preferred_element_type=jnp.float32)
        tile_blocks = contribution.reshape(CBT, NB, CBT, NB).transpose(0, 2, 1, 3)
        where_to = child_map[child_id]
        parent_front = parent_front.at[where_to[:, None], :, where_to[None, :], :].add(tile_blocks)
    parent_front = parent_front.reshape(NP, NP)
    diagonal_ids = jnp.arange(NP)
    parent_front = parent_front.at[diagonal_ids, diagonal_ids].add(parent_diag)
    parent_front = parent_front.at[:NB, :NB].add(lead_block)
    parent_front = parent_front.at[:NB, :].set(parent_front[pivots, :])
    packed = factor_tile(parent_front[:NB, :NB])
    upper_part = jnp.triu(packed)
    lower_part = jnp.tril(packed, -1) + jnp.eye(NB, dtype=jnp.float32)
    left_panel = lax.linalg.triangular_solve(upper_part, parent_front[NB:, :NB], left_side=False, lower=False)
    right_panel = lax.linalg.triangular_solve(lower_part, parent_front[:NB, NB:], left_side=True, lower=True, unit_diagonal=True)
    trailing = parent_front[NB:, NB:] - jnp.dot(left_panel.astype(jnp.float32), right_panel.astype(jnp.float32), precision=lax.Precision.HIGHEST, preferred_element_type=jnp.float32)
    top_rows = jnp.concatenate([packed, right_panel], axis=1)
    bottom_rows = jnp.concatenate([left_panel, trailing], axis=1)
    parent_front = jnp.concatenate([top_rows, bottom_rows], axis=0)
    return parent_front.reshape(TR_DEV, N_CHILD, NB, TC_DEV, N_GRP, NB).transpose(1, 0, 2, 4, 3, 5).reshape(N_CHILD, TR_DEV * NB, N_GRP, TC_DEV * NB)
```

```python
import jax
import jax.numpy as jnp
from jax import lax
from jax.experimental import pallas as pl
from jax.sharding import PartitionSpec as P

NB = 128
CB = 4096
NP = 16384


full_precision = lax.Precision.HIGHEST


def from_root(shard, axis, root):
    mine = lax.axis_index(axis) == root
    return lax.psum(jnp.where(mine, shard, jnp.zeros_like(shard)), axis)


def factor_kernel(tile_ref, packed_ref, lower_ref, upper_ref):
    rows = lax.broadcasted_iota(jnp.int32, (NB, NB), 0)
    cols = lax.broadcasted_iota(jnp.int32, (NB, NB), 1)
    lane = lax.broadcasted_iota(jnp.int32, (1, NB), 1)
    eye = jnp.where(rows == cols, 1.0, 0.0)
    packed_ref[...] = tile_ref[...]
    lower_ref[...] = eye
    upper_ref[...] = eye

    def eliminate(j, carry):
        working = packed_ref[...]
        upper = upper_ref[...]
        row_part = packed_ref[pl.ds(j, 1), :]
        row_lower = lower_ref[pl.ds(j, 1), :]
        column = jnp.sum(jnp.where(cols == j, working, 0.0), axis=1, keepdims=True)
        column_upper = jnp.sum(jnp.where(cols == j, upper, 0.0), axis=1, keepdims=True)
        pivot_value = jnp.sum(jnp.where(lane == j, row_part, 0.0), axis=1, keepdims=True)
        multiplier = jnp.where(rows[:, :1] > j, column / pivot_value, 0.0)
        right = jnp.where(lane > j, row_part, 0.0)
        packed_ref[...] = jnp.where(
            (cols == j) & (rows > j), multiplier, working - multiplier * right
        )
        lower_ref[...] = lower_ref[...] - multiplier * row_lower
        scaled = column_upper / pivot_value
        upper_ref[...] = jnp.where(cols == j, scaled, upper - scaled * right)
        return carry

    lax.fori_loop(0, NB, eliminate, 0)


def factor_tile(square):
    tile = jax.ShapeDtypeStruct((NB, NB), jnp.float32)
    return pl.pallas_call(factor_kernel, out_shape=(tile, tile, tile))(square)


def slot_table(classes, groups, capacity):
    count_tiles = classes.shape[0]
    places = jnp.arange(count_tiles)
    same_class = classes[:, None] == classes[None, :]
    before = places[None, :] < places[:, None]
    ranked = jnp.sum((same_class & before).astype(jnp.int32), axis=1)
    matches = (classes[None, None, :] == jnp.arange(groups)[:, None, None]) & (
        ranked[None, None, :] == jnp.arange(capacity)[None, :, None]
    )
    picked = jnp.sum(jnp.where(matches, places[None, None, :], 0), axis=2)
    filled = jnp.any(matches, axis=2)
    return (picked, filled)


def body(front_child, left_factor, right_factor, child_map, parent_diag, lead_block, pivots):
    groups = lax.axis_size("grp")
    rowgroups = lax.axis_size("child")
    child_index = lax.axis_index("child")
    group_index = lax.axis_index("grp")
    tiles_child = CB // NB
    capacity_cols = tiles_child // groups + 1
    capacity_rows = capacity_cols * (groups // rowgroups)
    tile_rows = NP // NB // rowgroups
    tile_cols = NP // NB // groups
    local_front = front_child[0]
    local_left = left_factor[0]
    local_right = right_factor[0]
    slot_width = capacity_cols * NB
    cols_picked, cols_filled = jax.vmap(
        lambda tile_map: slot_table(tile_map % groups, groups, capacity_cols)
    )(child_map)
    rows_picked, rows_filled = jax.vmap(
        lambda tile_map: slot_table(tile_map % rowgroups, rowgroups, capacity_rows)
    )(child_map)
    col_pick = lax.dynamic_index_in_dim(cols_picked, child_index, 0, keepdims=False)
    col_fill = lax.dynamic_index_in_dim(cols_filled, child_index, 0, keepdims=False)
    contribution = local_front - jnp.dot(
        local_left,
        lax.all_gather(local_right, "grp", axis=1, tiled=True),
        precision=full_precision,
        preferred_element_type=jnp.float32,
    )
    tile_view = contribution.reshape(contribution.shape[0], tiles_child, NB)
    chosen = jnp.take(tile_view, col_pick.reshape(-1), axis=1) * col_fill.reshape(1, -1, 1).astype(
        jnp.float32
    )
    by_column = lax.all_to_all(
        chosen.reshape(contribution.shape[0], groups, slot_width),
        "grp",
        split_axis=1,
        concat_axis=0,
        tiled=True,
    )
    by_column = by_column.reshape(tiles_child, NB, slot_width)
    row_pick = lax.dynamic_index_in_dim(rows_picked, child_index, 0, keepdims=False)
    row_fill = lax.dynamic_index_in_dim(rows_filled, child_index, 0, keepdims=False)
    second = jnp.take(by_column, row_pick.reshape(-1), axis=0) * row_fill.reshape(-1, 1, 1).astype(
        jnp.float32
    )
    second = second.reshape(rowgroups, capacity_rows * NB, slot_width)
    arrived = lax.all_to_all(second, "child", split_axis=0, concat_axis=0, tiled=True)
    col_pick_all = lax.dynamic_index_in_dim(cols_picked, group_index, 1, keepdims=False)
    col_fill_all = lax.dynamic_index_in_dim(cols_filled, group_index, 1, keepdims=False)
    row_pick_all = lax.dynamic_index_in_dim(rows_picked, child_index, 1, keepdims=False)
    row_fill_all = lax.dynamic_index_in_dim(rows_filled, child_index, 1, keepdims=False)
    col_tiles = jnp.take_along_axis(child_map, col_pick_all, axis=1) // groups
    row_tiles = jnp.take_along_axis(child_map, row_pick_all, axis=1) // rowgroups
    row_hot = (
        (row_tiles[:, None, :] == jnp.arange(tile_rows)[None, :, None]) & row_fill_all[:, None, :]
    ).astype(jnp.float32)
    col_hot = (
        (col_tiles[:, None, :] == jnp.arange(tile_cols)[None, :, None]) & col_fill_all[:, None, :]
    ).astype(jnp.float32)
    blocks = arrived.reshape(rowgroups, capacity_rows, NB, capacity_cols, NB)
    placed = jnp.einsum("kar,krisj->kaisj", row_hot, blocks, precision=full_precision)
    parent_front = jnp.einsum("kaisj,kbs->aibj", placed, col_hot, precision=full_precision).reshape(
        tile_rows * NB, tile_cols * NB
    )
    row_global = (
        (jnp.arange(tile_rows)[:, None] * rowgroups + child_index) * NB + jnp.arange(NB)[None, :]
    ).reshape(-1)
    col_global = (
        (jnp.arange(tile_cols)[:, None] * groups + group_index) * NB + jnp.arange(NB)[None, :]
    ).reshape(-1)
    on_diag = row_global[:, None] == col_global[None, :]
    parent_front = parent_front + jnp.where(
        on_diag, jnp.take(parent_diag, row_global)[:, None], 0.0
    )
    is_first_row = child_index == 0
    is_first_col = group_index == 0
    is_owner = is_first_row & is_first_col
    parent_front = parent_front.at[:NB, :NB].add(jnp.where(is_owner, lead_block, 0.0))
    top_rows = jnp.take(parent_front[:NB, :], pivots, axis=0)
    lead_tile = from_root(top_rows[:, :NB], ("child", "grp"), 0)
    packed_col, unit_inverse, upper_inverse = factor_tile(lead_tile)
    left_raw = jnp.dot(
        parent_front[:, :NB],
        upper_inverse,
        precision=full_precision,
        preferred_element_type=jnp.float32,
    )
    right_raw = jnp.dot(
        unit_inverse, top_rows, precision=full_precision, preferred_element_type=jnp.float32
    )
    row_lead = row_global < NB
    col_lead = col_global < NB
    left_send = jnp.where(row_lead[:, None], 0.0, left_raw)
    right_send = jnp.where(col_lead[None, :], 0.0, right_raw)
    left_all = from_root(left_send, "grp", 0)
    right_all = from_root(right_send, "child", 0)
    updated = parent_front - jnp.dot(
        left_all, right_all, precision=full_precision, preferred_element_type=jnp.float32
    )
    left_out = jnp.where(row_lead[:, None], updated[:, :NB], left_raw)
    updated = updated.at[:, :NB].set(jnp.where(is_first_col, left_out, updated[:, :NB]))
    top_out = right_raw.at[:, :NB].set(jnp.where(is_first_col, packed_col, right_raw[:, :NB]))
    updated = updated.at[:NB, :].set(jnp.where(is_first_row, top_out, updated[:NB, :]))
    return updated.reshape(1, tile_rows * NB, 1, tile_cols * NB)


def solution(mesh):
    in_specs = (
        P("child", "grp", None),
        P("child", "grp", None),
        P("child", None, "grp"),
        P(),
        P(),
        P(),
        P(),
    )
    out_specs = P("child", None, "grp", None)
    return jax.shard_map(body, mesh=mesh, in_specs=in_specs, out_specs=out_specs, check_vma=False)
```

```python
import jax
import jax.numpy as jnp
from jax import lax
from jax.experimental import pallas as pl
from jax.experimental.pallas import tpu as pltpu
from jax.sharding import PartitionSpec as P

NB = 128
CB = 4096
PIV = 1280
NP = 16384
CHILDREN = 8
GROUPS = 16
RING = 4
CBT = CB // NB
PT = NP // NB
TR = PT // CHILDREN
TC = PT // GROUPS
COL_SLOTS = 3
ROW_SLOTS = 6
ROWS = CB // GROUPS
HALF = PIV // 2
QUARTER = PIV // 4
MESH = pl.DeviceIdType.MESH
ANY = pl.BlockSpec(memory_space=pl.ANY)
VMEM = pl.BlockSpec(memory_space=pltpu.VMEM)
SMEM = pl.BlockSpec(memory_space=pltpu.SMEM)


def full_dot(a, b):
    return jnp.dot(a, b, precision=lax.Precision.HIGHEST, preferred_element_type=jnp.float32)


def gather_kernel(pick_ref, front_hbm, left_hbm, right_hbm, by_column,
                  factors, front, left, contribution, chosen,
                  load_sem, ring_send, ring_recv, col_send, col_recv, own_sem):
    child = lax.axis_index("child")
    group = lax.axis_index("grp")
    at_y, at_x = group // RING, group % RING

    load_right = pltpu.make_async_copy(right_hbm, factors.at[group], load_sem.at[0])
    load_left = pltpu.make_async_copy(left_hbm, left, load_sem.at[1])
    load_front = pltpu.make_async_copy(front_hbm, front, load_sem.at[2])
    load_right.start()
    load_left.start()
    load_front.start()

    barrier = pltpu.get_barrier_semaphore()

    def greet(i, carry):
        pl.semaphore_signal(
            barrier, inc=1, device_id=(child, lax.rem(group + i, GROUPS)), device_id_type=MESH
        )
        return carry

    lax.fori_loop(1, GROUPS, greet, 0)
    pl.semaphore_wait(barrier, GROUPS - 1)

    def place(half, first, second):
        return second * RING + first if half == 0 else first * RING + second

    def turn(position, by):
        return lax.rem(position + by + RING, RING)

    def piece(half, block, quarter):
        if quarter is None:
            return factors.at[block, pl.ds(half * HALF, HALF)]
        return factors.at[block, pl.ds(half * HALF + quarter * QUARTER, QUARTER)]

    copies = {}

    def make(key, half, block, quarter, target):
        number = len(copies)
        ref = piece(half, block, quarter)
        copies[key] = pltpu.make_async_remote_copy(
            src_ref=ref, dst_ref=ref, send_sem=ring_send.at[number], recv_sem=ring_recv.at[number],
            device_id=(child, target), device_id_type=MESH,
        )

    lines = (0, -1, 1, 2)
    for half in (0, 1):
        first, second = (at_x, at_y) if half == 0 else (at_y, at_x)
        for way in (1, -1):
            target = place(half, turn(first, way), second)
            make((half, "a", way), half, place(half, first, second), None, target)
            make((half, "af", way), half, place(half, turn(first, -way), second),
                 0 if way == 1 else 1, target)
        for line in lines:
            column = turn(first, line)
            for way in (1, -1):
                target = place(half, first, turn(second, way))
                make((half, line, way), half, place(half, column, second), None, target)
                make((half, line, "f", way), half, place(half, column, turn(second, -way)),
                     0 if way == 1 else 1, target)

    def start(*key):
        for half in (0, 1):
            for way in (1, -1):
                copies[(half,) + key + (way,)].start()

    def arrive(*key):
        for half in (0, 1):
            for way in (1, -1):
                copies[(half,) + key + (way,)].wait_recv()

    def multiply(offsets):
        def one(i, carry):
            block = jnp.int32(0)
            for number, (dy, dx) in enumerate(offsets):
                block = jnp.where(i == number, turn(at_y, dy) * RING + turn(at_x, dx), block)
            product = full_dot(left[...], factors[block])
            base = pl.multiple_of(block * ROWS, ROWS)
            result = front[:, pl.ds(base, ROWS)] - product
            contribution[2 * block] = result[:, :NB]
            contribution[2 * block + 1] = result[:, NB:]
            return carry

        lax.fori_loop(0, len(offsets), one, 0)

    load_right.wait()
    start("a")
    start(0)
    load_left.wait()
    load_front.wait()
    multiply([(0, 0)])
    arrive("a")
    start("af")
    start(-1)
    start(1)
    arrive(0)
    start(0, "f")
    multiply([(0, 1), (0, -1), (1, 0), (-1, 0)])
    arrive("af")
    start(2)
    arrive(0, "f")
    multiply([(0, 2), (2, 0)])
    arrive(-1)
    start(-1, "f")
    arrive(1)
    start(1, "f")
    multiply([(1, 1), (1, -1), (-1, 1), (-1, -1)])
    arrive(2)
    start(2, "f")
    arrive(-1, "f")
    arrive(1, "f")
    multiply([(1, 2), (-1, 2), (2, 1), (2, -1)])
    arrive(2, "f")
    multiply([(2, 2)])

    def column_copy(slot, i):
        target = lax.rem(group + i, GROUPS)
        return pltpu.make_async_remote_copy(
            src_ref=chosen.at[slot, target],
            dst_ref=by_column.at[slot, pl.ds(2 * group, 2)],
            send_sem=col_send.at[slot * GROUPS + i], recv_sem=col_recv.at[slot * GROUPS + i],
            device_id=(child, target), device_id_type=MESH,
        )

    def own_copy(slot):
        return pltpu.make_async_copy(
            chosen.at[slot, group], by_column.at[slot, pl.ds(2 * group, 2)], own_sem.at[slot]
        )

    def select(slot, target):
        tile = contribution[pick_ref[target * COL_SLOTS + slot]]
        chosen[slot, target] = tile.reshape(2, NB, NB)

    for slot in range(COL_SLOTS):
        def send(i, carry):
            select(slot, lax.rem(group + i, GROUPS))
            column_copy(slot, i).start()
            return carry

        lax.fori_loop(1, GROUPS, send, 0)
        select(slot, group)
        own_copy(slot).start()

    for key in copies:
        copies[key].wait_send()
    for slot in range(COL_SLOTS):
        def finish(i, carry):
            column_copy(slot, i).wait_recv()
            column_copy(slot, i).wait_send()
            return carry

        lax.fori_loop(1, GROUPS, finish, 0)
        own_copy(slot).wait()


def gather_columns(pick, front, left, right):
    return pl.pallas_call(
        gather_kernel,
        out_shape=jax.ShapeDtypeStruct((COL_SLOTS, CBT, NB, NB), jnp.float32),
        in_specs=[SMEM, ANY, ANY, ANY],
        out_specs=ANY,
        scratch_shapes=[
            pltpu.VMEM((GROUPS, PIV, ROWS), jnp.float32),
            pltpu.VMEM((ROWS, CB), jnp.float32),
            pltpu.VMEM((ROWS, PIV), jnp.float32),
            pltpu.VMEM((CBT, ROWS, NB), jnp.float32),
            pltpu.VMEM((COL_SLOTS, GROUPS, 2, NB, NB), jnp.float32),
            pltpu.SemaphoreType.DMA((3,)),
            pltpu.SemaphoreType.DMA((40,)),
            pltpu.SemaphoreType.DMA((40,)),
            pltpu.SemaphoreType.DMA((COL_SLOTS * GROUPS,)),
            pltpu.SemaphoreType.DMA((COL_SLOTS * GROUPS,)),
            pltpu.SemaphoreType.DMA((COL_SLOTS,)),
        ],
        compiler_params=pltpu.CompilerParams(
            collective_id=0, has_side_effects=True, vmem_limit_bytes=52 * 2**20
        ),
        name="gather_columns",
    )(pick, front, left, right)


def factor_tile(packed_ref, lower_ref, upper_ref):
    rows = lax.broadcasted_iota(jnp.int32, (NB, NB), 0)
    cols = lax.broadcasted_iota(jnp.int32, (NB, NB), 1)
    lane = lax.broadcasted_iota(jnp.int32, (1, NB), 1)
    eye = jnp.where(rows == cols, 1.0, 0.0)
    lower_ref[...] = eye
    upper_ref[...] = eye

    def eliminate(j, carry):
        working = packed_ref[...]
        upper = upper_ref[...]
        row_part = packed_ref[pl.ds(j, 1), :]
        row_lower = lower_ref[pl.ds(j, 1), :]
        column = jnp.sum(jnp.where(cols == j, working, 0.0), axis=1, keepdims=True)
        column_upper = jnp.sum(jnp.where(cols == j, upper, 0.0), axis=1, keepdims=True)
        pivot_value = jnp.sum(jnp.where(lane == j, row_part, 0.0), axis=1, keepdims=True)
        multiplier = jnp.where(rows[:, :1] > j, column / pivot_value, 0.0)
        right = jnp.where(lane > j, row_part, 0.0)
        packed_ref[...] = jnp.where(
            (cols == j) & (rows > j), multiplier, working - multiplier * right
        )
        lower_ref[...] = lower_ref[...] - multiplier * row_lower
        scaled = column_upper / pivot_value
        upper_ref[...] = jnp.where(cols == j, scaled, upper - scaled * right)
        return carry

    lax.fori_loop(0, NB, eliminate, 0)


def row_kernel(pick_ref, lead_ref, row_slot_ref, by_column, lead_block, lead_diag, pivots,
               arrived, left_panel, top_parts, packed, lower, upper,
               chosen, first_column, raw_lead,
               top_send, top_recv, row_send, row_recv, own_sem, lead_send, lead_recv,
               load_sem, spread_send, spread_recv, share_send, share_recv):
    child = lax.axis_index("child")
    group = lax.axis_index("grp")

    barrier = pltpu.get_barrier_semaphore()

    def greet_group(i, carry):
        pl.semaphore_signal(
            barrier, inc=1, device_id=(child, lax.rem(group + i, GROUPS)), device_id_type=MESH
        )
        return carry

    def greet_child(i, carry):
        pl.semaphore_signal(
            barrier, inc=1, device_id=(lax.rem(child + i, CHILDREN), group), device_id_type=MESH
        )
        return carry

    lax.fori_loop(1, GROUPS, greet_group, 0)
    lax.fori_loop(1, CHILDREN, greet_child, 0)
    pl.semaphore_wait(barrier, GROUPS + CHILDREN - 2)

    def top_copy(i):
        return pltpu.make_async_remote_copy(
            src_ref=top_parts.at[child], dst_ref=top_parts.at[child],
            send_sem=top_send.at[i], recv_sem=top_recv.at[i],
            device_id=(lax.rem(child + i, CHILDREN), group), device_id_type=MESH,
        )

    for slot in range(COL_SLOTS):
        top_parts[child, slot] = by_column[slot, pick_ref[0]]

    def send_top(i, carry):
        top_copy(i).start()
        return carry

    lax.fori_loop(1, CHILDREN, send_top, 0)

    def row_copy(slot, i):
        target = lax.rem(child + i, CHILDREN)
        return pltpu.make_async_remote_copy(
            src_ref=chosen.at[slot, target], dst_ref=arrived.at[slot, child],
            send_sem=row_send.at[slot * CHILDREN + i], recv_sem=row_recv.at[slot * CHILDREN + i],
            device_id=(target, group), device_id_type=MESH,
        )

    def own_copy(slot):
        return pltpu.make_async_copy(
            chosen.at[slot, child], arrived.at[slot, child], own_sem.at[slot]
        )

    def select(slot, target):
        for r in range(ROW_SLOTS):
            chosen[slot, target, r] = by_column[slot, pick_ref[target * ROW_SLOTS + r]]

    for slot in range(COL_SLOTS):
        def send(i, carry):
            select(slot, lax.rem(child + i, CHILDREN))
            row_copy(slot, i).start()
            return carry

        lax.fori_loop(1, CHILDREN, send, 0)
        select(slot, child)
        own_copy(slot).start()

    def arrive_top(i, carry):
        top_copy(i).wait_recv()
        return carry

    lax.fori_loop(1, CHILDREN, arrive_top, 0)

    def lead_copy(target):
        return pltpu.make_async_remote_copy(
            src_ref=raw_lead, dst_ref=raw_lead,
            send_sem=lead_send.at[target], recv_sem=lead_recv.at[0],
            device_id=(child, target), device_id_type=MESH,
        )

    rows = lax.broadcasted_iota(jnp.int32, (NB, NB), 0)
    cols = lax.broadcasted_iota(jnp.int32, (NB, NB), 1)

    @pl.when(group == 0)
    def _():
        total = lead_block[...] + jnp.where(rows == cols, lead_diag[...], 0.0)
        for k in range(CHILDREN):
            total = total + jnp.where(lead_ref[k] > 0, top_parts[k, 0], 0.0)
        chosen_rows = jnp.where(pivots[...] == cols, 1.0, 0.0)
        raw_lead[...] = full_dot(chosen_rows, total)

        def send_lead(i, carry):
            lead_copy(i).start()
            return carry

        lax.fori_loop(1, GROUPS, send_lead, 0)

    @pl.when(group != 0)
    def _():
        lead_copy(0).wait_recv()

    packed[...] = raw_lead[...]
    factor_tile(packed, lower, upper)

    def finish_rows(slot):
        def finish(i, carry):
            row_copy(slot, i).wait_recv()
            row_copy(slot, i).wait_send()
            return carry

        lax.fori_loop(1, CHILDREN, finish, 0)
        own_copy(slot).wait()

    def spread_copy(target):
        return pltpu.make_async_remote_copy(
            src_ref=left_panel.at[target], dst_ref=left_panel.at[target],
            send_sem=spread_send.at[target], recv_sem=spread_recv.at[0],
            device_id=(child, target), device_id_type=MESH,
        )

    def own_spread():
        return pltpu.make_async_remote_copy(
            src_ref=left_panel.at[group], dst_ref=left_panel.at[group],
            send_sem=spread_send.at[0], recv_sem=spread_recv.at[0],
            device_id=(child, 0), device_id_type=MESH,
        )

    def share_copy(i):
        return pltpu.make_async_remote_copy(
            src_ref=left_panel.at[group], dst_ref=left_panel.at[group],
            send_sem=share_send.at[i], recv_sem=share_recv.at[i],
            device_id=(child, lax.rem(group + i, GROUPS)), device_id_type=MESH,
        )

    finish_rows(0)

    @pl.when(group == 0)
    def _():
        load = pltpu.make_async_copy(arrived.at[0], first_column, load_sem.at[0])
        load.start()
        load.wait()

        def assemble(i, carry):
            a = lax.rem(i, TR)
            total = jnp.zeros((NB, NB), jnp.float32)
            for k in range(CHILDREN):
                slot = row_slot_ref[k * TR + a]
                held = (slot >= 0) & (lead_ref[k] > 0)
                tile = first_column[k, jnp.maximum(slot, 0)]
                total = total + jnp.where(held, tile, 0.0)
            left_panel[a] = total

            @pl.when(a > 0)
            def _():
                spread_copy(a).start()

            return carry

        lax.fori_loop(1, TR + 1, assemble, 0)

    @pl.when(group != 0)
    def _():
        own_spread().wait_recv()

    def send_share(i, carry):
        @pl.when(lax.rem(group + i, GROUPS) != 0)
        def _():
            share_copy(i).start()
        return carry

    lax.fori_loop(1, GROUPS, send_share, 0)

    def finish_top(i, carry):
        top_copy(i).wait_send()
        return carry

    lax.fori_loop(1, CHILDREN, finish_top, 0)

    def finish_share(i, carry):
        @pl.when(lax.rem(group + i, GROUPS) != 0)
        def _():
            share_copy(i).wait_send()

        @pl.when(group != 0)
        def _():
            share_copy(i).wait_recv()

        @pl.when(group == 0)
        def _():
            lead_copy(i).wait_send()
            spread_copy(i).wait_send()

        return carry

    lax.fori_loop(1, GROUPS, finish_share, 0)
    finish_rows(1)
    finish_rows(2)


def exchange_rows(pick, lead_held, row_slot, by_column, lead_block, lead_diag, pivots):
    tile = jax.ShapeDtypeStruct((NB, NB), jnp.float32)
    return pl.pallas_call(
        row_kernel,
        out_shape=(
            jax.ShapeDtypeStruct((COL_SLOTS, CHILDREN, ROW_SLOTS, NB, NB), jnp.float32),
            jax.ShapeDtypeStruct((TR, NB, NB), jnp.float32),
            jax.ShapeDtypeStruct((CHILDREN, COL_SLOTS, NB, NB), jnp.float32),
            tile, tile, tile,
        ),
        in_specs=[SMEM, SMEM, SMEM, VMEM, VMEM, VMEM, VMEM],
        out_specs=(ANY, VMEM, VMEM, VMEM, VMEM, VMEM),
        scratch_shapes=[
            pltpu.VMEM((COL_SLOTS, CHILDREN, ROW_SLOTS, NB, NB), jnp.float32),
            pltpu.VMEM((CHILDREN, ROW_SLOTS, NB, NB), jnp.float32),
            pltpu.VMEM((NB, NB), jnp.float32),
            pltpu.SemaphoreType.DMA((CHILDREN,)),
            pltpu.SemaphoreType.DMA((CHILDREN,)),
            pltpu.SemaphoreType.DMA((COL_SLOTS * CHILDREN,)),
            pltpu.SemaphoreType.DMA((COL_SLOTS * CHILDREN,)),
            pltpu.SemaphoreType.DMA((COL_SLOTS,)),
            pltpu.SemaphoreType.DMA((GROUPS,)),
            pltpu.SemaphoreType.DMA((1,)),
            pltpu.SemaphoreType.DMA((1,)),
            pltpu.SemaphoreType.DMA((GROUPS,)),
            pltpu.SemaphoreType.DMA((1,)),
            pltpu.SemaphoreType.DMA((GROUPS,)),
            pltpu.SemaphoreType.DMA((GROUPS,)),
        ],
        compiler_params=pltpu.CompilerParams(
            collective_id=1, has_side_effects=True, vmem_limit_bytes=52 * 2**20
        ),
        name="exchange_rows",
    )(pick, lead_held, row_slot, by_column, lead_block, lead_diag, pivots)


def update_kernel(place_ref, lead_ref, row_slot_ref, col_slot_ref, arrived, left_raw, top_parts,
                  packed, lower, upper, diag, pivots, out_ref, right):
    a = pl.program_id(0)
    child, group = place_ref[0], place_ref[1]
    rows = lax.broadcasted_iota(jnp.int32, (NB, NB), 0)
    cols = lax.broadcasted_iota(jnp.int32, (NB, NB), 1)

    @pl.when(a == 0)
    def _():
        right[...] = jnp.zeros_like(right)
        for k in range(CHILDREN):
            for b in range(TC):
                slot = col_slot_ref[k * TC + b]

                @pl.when((slot >= 0) & (lead_ref[k] > 0))
                def _():
                    span = pl.ds(b * NB, NB)
                    right[:, span] = right[:, span] + top_parts[k, slot]

        chosen_rows = jnp.where(pivots[...] == cols, 1.0, 0.0)
        right[...] = full_dot(lower[...], full_dot(chosen_rows, right[...]))

        @pl.when(group == 0)
        def _():
            right[:, :NB] = jnp.zeros((NB, NB), jnp.float32)

    top = (a == 0) & (child == 0)

    @pl.when(top)
    def _():
        out_ref[...] = right[...]

        @pl.when(group == 0)
        def _():
            out_ref[:, :NB] = packed[...]

    @pl.when(jnp.logical_not(top))
    def _():
        left = full_dot(left_raw[0], upper[...])
        out_ref[...] = -full_dot(left, right[...])
        for k in range(CHILDREN):
            row_slot = row_slot_ref[k * TR + a]

            @pl.when(row_slot >= 0)
            def _():
                for b in range(TC):
                    col_slot = col_slot_ref[k * TC + b]

                    @pl.when(col_slot >= 0)
                    def _():
                        span = pl.ds(b * NB, NB)
                        out_ref[:, span] = out_ref[:, span] + arrived[col_slot, k, row_slot]

        on_diag = (lax.rem(group, CHILDREN) == child) & (lax.rem(a, 2) == group // CHILDREN)

        @pl.when(on_diag)
        def _():
            span = pl.ds(pl.multiple_of((a // 2) * NB, NB), NB)
            out_ref[:, span] = out_ref[:, span] + jnp.where(rows == cols, diag[0], 0.0)

        @pl.when(group == 0)
        def _():
            out_ref[:, :NB] = left


def update_front(place, lead_held, row_slot, col_slot, arrived, left_raw, top_parts,
                 packed, lower, upper, diag, pivots):
    return pl.pallas_call(
        update_kernel,
        grid=(TR,),
        out_shape=jax.ShapeDtypeStruct((TR * NB, TC * NB), jnp.float32),
        in_specs=[
            SMEM, SMEM, SMEM, SMEM, VMEM,
            pl.BlockSpec((1, NB, NB), lambda a: (a, 0, 0)),
            VMEM, VMEM, VMEM, VMEM,
            pl.BlockSpec((1, 1, NB), lambda a: (a, 0, 0)),
            VMEM,
        ],
        out_specs=pl.BlockSpec((NB, TC * NB), lambda a: (a, 0)),
        scratch_shapes=[pltpu.VMEM((NB, TC * NB), jnp.float32)],
        compiler_params=pltpu.CompilerParams(vmem_limit_bytes=52 * 2**20),
        name="update_front",
    )(place, lead_held, row_slot, col_slot, arrived, left_raw, top_parts,
      packed, lower, upper, diag, pivots)


def slot_tables(child_map):
    tiles = jnp.arange(PT)
    hits = child_map[:, None, :] == tiles[None, :, None]
    present = jnp.any(hits, axis=2)
    source = jnp.sum(jnp.where(hits, jnp.arange(CBT)[None, None, :], 0), axis=2)

    def by_class(classes, capacity):
        count = PT // classes
        held = present.reshape(CHILDREN, count, classes).transpose(0, 2, 1)
        tile = source.reshape(CHILDREN, count, classes).transpose(0, 2, 1)
        earlier = jnp.arange(count)[None, :] < jnp.arange(count)[:, None]
        rank = jnp.sum((held[:, :, None, :] & earlier).astype(jnp.int32), axis=3)
        slot = jnp.where(held, rank, -1)
        wanted = slot[:, :, None, :] == jnp.arange(capacity)[None, None, :, None]
        pick = jnp.sum(jnp.where(wanted, tile[:, :, None, :], 0), axis=3)
        return slot, pick

    return present, by_class(GROUPS, COL_SLOTS), by_class(CHILDREN, ROW_SLOTS)


def body(front_child, left_factor, right_factor, child_map, parent_diag, lead_block, pivots):
    child = lax.axis_index("child")
    group = lax.axis_index("grp")
    present, (col_slot, col_pick), (row_slot, row_pick) = slot_tables(child_map)

    def mine(table, index, dim):
        return lax.dynamic_index_in_dim(table, index, dim, keepdims=False).reshape(-1)

    lead_held = present[:, 0].astype(jnp.int32)
    row_slots = mine(row_slot, child, 1)
    col_slots = mine(col_slot, group, 1)
    pivot_column = pivots.reshape(NB, 1)
    by_column = gather_columns(
        mine(col_pick, child, 0), front_child[0], left_factor[0], right_factor[0]
    )
    arrived, left_raw, top_parts, packed, lower, upper = exchange_rows(
        mine(row_pick, child, 0), lead_held, row_slots, by_column, lead_block,
        parent_diag[:NB].reshape(1, NB), pivot_column,
    )
    diag = lax.dynamic_index_in_dim(
        parent_diag.reshape(TR, CHILDREN, NB), child, 1, keepdims=True
    )
    front = update_front(
        jnp.stack([child, group]).astype(jnp.int32), lead_held, row_slots, col_slots,
        arrived, left_raw, top_parts, packed, lower, upper, diag, pivot_column,
    )
    return front.reshape(1, TR * NB, 1, TC * NB)


def solution(mesh):
    in_specs = (
        P("child", "grp", None),
        P("child", "grp", None),
        P("child", None, "grp"),
        P(),
        P(),
        P(),
        P(),
    )
    out_specs = P("child", None, "grp", None)
    return jax.shard_map(body, mesh=mesh, in_specs=in_specs, out_specs=out_specs, check_vma=False)
```

```python
import jax
import jax.numpy as jnp
from jax import lax
from jax.experimental import pallas as pl
from jax.experimental.pallas import tpu as pltpu
from jax.sharding import PartitionSpec as P

NB = 128
CB = 4096
PIV = 1280
NP = 16384
CHILDREN = 8
GROUPS = 16
RING = 4
CBT = CB // NB
PT = NP // NB
TR = PT // CHILDREN
TC = PT // GROUPS
COL_SLOTS = 3
ROW_SLOTS = 6
ROWS = CB // GROUPS
HALF = PIV // 2
QUARTER = PIV // 4
MESH = pl.DeviceIdType.MESH
ANY = pl.BlockSpec(memory_space=pl.ANY)
VMEM = pl.BlockSpec(memory_space=pltpu.VMEM)
SMEM = pl.BlockSpec(memory_space=pltpu.SMEM)


def full_dot(a, b):
    return jnp.dot(a, b, precision=lax.Precision.HIGHEST, preferred_element_type=jnp.float32)


def factor_tile(packed_ref, lower_ref, upper_ref):
    rows = lax.broadcasted_iota(jnp.int32, (NB, NB), 0)
    cols = lax.broadcasted_iota(jnp.int32, (NB, NB), 1)
    lane = lax.broadcasted_iota(jnp.int32, (1, NB), 1)
    eye = jnp.where(rows == cols, 1.0, 0.0)
    lower_ref[...] = eye
    upper_ref[...] = eye

    def eliminate(j, carry):
        working = packed_ref[...]
        upper = upper_ref[...]
        row_part = packed_ref[pl.ds(j, 1), :]
        row_lower = lower_ref[pl.ds(j, 1), :]
        column = jnp.sum(jnp.where(cols == j, working, 0.0), axis=1, keepdims=True)
        column_upper = jnp.sum(jnp.where(cols == j, upper, 0.0), axis=1, keepdims=True)
        pivot_value = jnp.sum(jnp.where(lane == j, row_part, 0.0), axis=1, keepdims=True)
        multiplier = jnp.where(rows[:, :1] > j, column / pivot_value, 0.0)
        right = jnp.where(lane > j, row_part, 0.0)
        packed_ref[...] = jnp.where(
            (cols == j) & (rows > j), multiplier, working - multiplier * right
        )
        lower_ref[...] = lower_ref[...] - multiplier * row_lower
        scaled = column_upper / pivot_value
        upper_ref[...] = jnp.where(cols == j, scaled, upper - scaled * right)
        return carry

    lax.fori_loop(0, NB, eliminate, 0)


def exchange_kernel(col_pick_ref, row_pick_ref, lead_ref, row_slot_ref,
                    front_hbm, left_hbm, right_hbm, lead_block, lead_diag, pivots,
                    arrived, left_panel, top_parts, packed, lower, upper,
                    factors, front, left, contribution, col_chosen, column_0, column_1, column_2,
                    first_column, raw_lead,
                    load_sem, ring_send, ring_recv, col_send, col_recv, own_col_sem,
                    top_send, top_recv, row_send, row_recv, own_row_sem, lead_send, lead_recv,
                    spread_send, spread_recv, share_send, share_recv):
    child = lax.axis_index("child")
    group = lax.axis_index("grp")
    at_y, at_x = group // RING, group % RING

    load_right = pltpu.make_async_copy(right_hbm, factors.at[group], load_sem.at[0])
    load_left = pltpu.make_async_copy(left_hbm, left, load_sem.at[1])
    load_front = pltpu.make_async_copy(front_hbm, front, load_sem.at[2])
    load_right.start()
    load_left.start()
    load_front.start()

    barrier = pltpu.get_barrier_semaphore()

    def greet_group(i, carry):
        pl.semaphore_signal(
            barrier, inc=1, device_id=(child, lax.rem(group + i, GROUPS)), device_id_type=MESH
        )
        return carry

    def greet_child(i, carry):
        pl.semaphore_signal(
            barrier, inc=1, device_id=(lax.rem(child + i, CHILDREN), group), device_id_type=MESH
        )
        return carry

    lax.fori_loop(1, GROUPS, greet_group, 0)
    lax.fori_loop(1, CHILDREN, greet_child, 0)
    pl.semaphore_wait(barrier, GROUPS + CHILDREN - 2)

    def place(half, first, second):
        return second * RING + first if half == 0 else first * RING + second

    def turn(position, by):
        return lax.rem(position + by + RING, RING)

    def piece(half, block, quarter):
        if quarter is None:
            return factors.at[block, pl.ds(half * HALF, HALF)]
        return factors.at[block, pl.ds(half * HALF + quarter * QUARTER, QUARTER)]

    copies = {}

    def make(key, half, block, quarter, target):
        number = len(copies)
        ref = piece(half, block, quarter)
        copies[key] = pltpu.make_async_remote_copy(
            src_ref=ref, dst_ref=ref, send_sem=ring_send.at[number], recv_sem=ring_recv.at[number],
            device_id=(child, target), device_id_type=MESH,
        )

    lines = (0, -1, 1, 2)
    for half in (0, 1):
        first, second = (at_x, at_y) if half == 0 else (at_y, at_x)
        for way in (1, -1):
            target = place(half, turn(first, way), second)
            make((half, "a", way), half, place(half, first, second), None, target)
            make((half, "af", way), half, place(half, turn(first, -way), second),
                 0 if way == 1 else 1, target)
        for line in lines:
            column = turn(first, line)
            for way in (1, -1):
                target = place(half, first, turn(second, way))
                make((half, line, way), half, place(half, column, second), None, target)
                make((half, line, "f", way), half, place(half, column, turn(second, -way)),
                     0 if way == 1 else 1, target)

    def start(*key):
        for half in (0, 1):
            for way in (1, -1):
                copies[(half,) + key + (way,)].start()

    def arrive(*key):
        for half in (0, 1):
            for way in (1, -1):
                copies[(half,) + key + (way,)].wait_recv()

    def multiply(offsets):
        def one(i, carry):
            block = jnp.int32(0)
            for number, (dy, dx) in enumerate(offsets):
                block = jnp.where(i == number, turn(at_y, dy) * RING + turn(at_x, dx), block)
            product = full_dot(left[...], factors[block])
            base = pl.multiple_of(block * ROWS, ROWS)
            result = front[:, pl.ds(base, ROWS)] - product
            contribution[2 * block] = result[:, :NB]
            contribution[2 * block + 1] = result[:, NB:]
            return carry

        lax.fori_loop(0, len(offsets), one, 0)

    load_right.wait()
    start("a")
    start(0)
    load_left.wait()
    load_front.wait()
    multiply([(0, 0)])
    arrive("a")
    start("af")
    start(-1)
    start(1)
    arrive(0)
    start(0, "f")
    multiply([(0, 1), (0, -1), (1, 0), (-1, 0)])
    arrive("af")
    start(2)
    arrive(0, "f")
    multiply([(0, 2), (2, 0)])
    arrive(-1)
    start(-1, "f")
    arrive(1)
    start(1, "f")
    multiply([(1, 1), (1, -1), (-1, 1), (-1, -1)])
    arrive(2)
    start(2, "f")
    arrive(-1, "f")
    arrive(1, "f")
    multiply([(1, 2), (-1, 2), (2, 1), (2, -1)])
    arrive(2, "f")
    multiply([(2, 2)])

    by_column = (column_0, column_1, column_2)

    def column_copy(slot, i):
        target = lax.rem(group + i, GROUPS)
        return pltpu.make_async_remote_copy(
            src_ref=col_chosen.at[slot, target],
            dst_ref=by_column[slot].at[pl.ds(2 * group, 2)],
            send_sem=col_send.at[slot * GROUPS + i], recv_sem=col_recv.at[slot * GROUPS + i],
            device_id=(child, target), device_id_type=MESH,
        )

    def own_column_copy(slot):
        return pltpu.make_async_copy(
            col_chosen.at[slot, group], by_column[slot].at[pl.ds(2 * group, 2)],
            own_col_sem.at[slot],
        )

    def select_column(slot, target):
        tile = contribution[col_pick_ref[target * COL_SLOTS + slot]]
        col_chosen[slot, target] = tile.reshape(2, NB, NB)

    for slot in range(COL_SLOTS):
        def send_column(i, carry):
            select_column(slot, lax.rem(group + i, GROUPS))
            column_copy(slot, i).start()
            return carry

        lax.fori_loop(1, GROUPS, send_column, 0)
        select_column(slot, group)
        own_column_copy(slot).start()

    for key in copies:
        copies[key].wait_send()

    def top_copy(slot, i):
        return pltpu.make_async_remote_copy(
            src_ref=top_parts.at[child, slot], dst_ref=top_parts.at[child, slot],
            send_sem=top_send.at[slot * CHILDREN + i], recv_sem=top_recv.at[slot * CHILDREN + i],
            device_id=(lax.rem(child + i, CHILDREN), group), device_id_type=MESH,
        )

    def row_buffer(slot, target):
        number = slot * CHILDREN + target
        lanes = pl.multiple_of(lax.rem(number, 2) * NB, NB)
        return factors.at[number // 2, pl.ds(0, ROW_SLOTS * NB), pl.ds(lanes, NB)]

    def row_copy(slot, i):
        target = lax.rem(child + i, CHILDREN)
        return pltpu.make_async_remote_copy(
            src_ref=row_buffer(slot, target), dst_ref=arrived.at[slot, child],
            send_sem=row_send.at[slot * CHILDREN + i], recv_sem=row_recv.at[slot * CHILDREN + i],
            device_id=(target, group), device_id_type=MESH,
        )

    def own_row_copy(slot):
        return pltpu.make_async_copy(
            row_buffer(slot, child), arrived.at[slot, child], own_row_sem.at[slot]
        )

    def select_rows(slot, target):
        number = slot * CHILDREN + target
        lanes = pl.multiple_of(lax.rem(number, 2) * NB, NB)
        for r in range(ROW_SLOTS):
            tile = by_column[slot][row_pick_ref[target * ROW_SLOTS + r]]
            factors[number // 2, pl.ds(r * NB, NB), pl.ds(lanes, NB)] = tile

    def pass_rows(slot):
        def finish(i, carry):
            column_copy(slot, i).wait_recv()
            return carry

        lax.fori_loop(1, GROUPS, finish, 0)
        own_column_copy(slot).wait()
        top_parts[child, slot] = by_column[slot][row_pick_ref[0]]

        def send_top(i, carry):
            top_copy(slot, i).start()
            return carry

        lax.fori_loop(1, CHILDREN, send_top, 0)

        def send_rows(i, carry):
            select_rows(slot, lax.rem(child + i, CHILDREN))
            row_copy(slot, i).start()
            return carry

        lax.fori_loop(1, CHILDREN, send_rows, 0)
        select_rows(slot, child)
        own_row_copy(slot).start()

    def finish_top(slot):
        def arrive_top(i, carry):
            top_copy(slot, i).wait_recv()
            return carry

        lax.fori_loop(1, CHILDREN, arrive_top, 0)

    def finish_rows(slot):
        def finish(i, carry):
            row_copy(slot, i).wait_recv()
            return carry

        lax.fori_loop(1, CHILDREN, finish, 0)
        own_row_copy(slot).wait()

    def lead_copy(target):
        return pltpu.make_async_remote_copy(
            src_ref=raw_lead, dst_ref=raw_lead,
            send_sem=lead_send.at[target], recv_sem=lead_recv.at[0],
            device_id=(child, target), device_id_type=MESH,
        )

    def spread_copy(target):
        return pltpu.make_async_remote_copy(
            src_ref=left_panel.at[target], dst_ref=left_panel.at[target],
            send_sem=spread_send.at[target], recv_sem=spread_recv.at[0],
            device_id=(child, target), device_id_type=MESH,
        )

    def own_spread():
        return pltpu.make_async_remote_copy(
            src_ref=left_panel.at[group], dst_ref=left_panel.at[group],
            send_sem=spread_send.at[0], recv_sem=spread_recv.at[0],
            device_id=(child, 0), device_id_type=MESH,
        )

    def share_copy(i):
        return pltpu.make_async_remote_copy(
            src_ref=left_panel.at[group], dst_ref=left_panel.at[group],
            send_sem=share_send.at[i], recv_sem=share_recv.at[i],
            device_id=(child, lax.rem(group + i, GROUPS)), device_id_type=MESH,
        )

    pass_rows(0)
    finish_top(0)
    rows = lax.broadcasted_iota(jnp.int32, (NB, NB), 0)
    cols = lax.broadcasted_iota(jnp.int32, (NB, NB), 1)

    @pl.when(group == 0)
    def _():
        total = lead_block[...] + jnp.where(rows == cols, lead_diag[...], 0.0)
        for k in range(CHILDREN):
            total = total + jnp.where(lead_ref[k] > 0, top_parts[k, 0], 0.0)
        chosen_rows = jnp.where(pivots[...] == cols, 1.0, 0.0)
        raw_lead[...] = full_dot(chosen_rows, total)

        def send_lead(i, carry):
            lead_copy(i).start()
            return carry

        lax.fori_loop(1, GROUPS, send_lead, 0)

    pass_rows(1)

    @pl.when(group != 0)
    def _():
        lead_copy(0).wait_recv()

    packed[...] = raw_lead[...]
    factor_tile(packed, lower, upper)
    pass_rows(2)

    finish_rows(0)

    @pl.when(group == 0)
    def _():
        loads = [
            pltpu.make_async_copy(
                arrived.at[0, :, pl.ds(r * NB, NB), :], first_column.at[:, r], load_sem.at[r]
            )
            for r in range(ROW_SLOTS)
        ]
        for load in loads:
            load.start()
        for load in loads:
            load.wait()

        def assemble(i, carry):
            a = lax.rem(i, TR)
            total = jnp.zeros((NB, NB), jnp.float32)
            for k in range(CHILDREN):
                slot = row_slot_ref[k * TR + a]
                held = (slot >= 0) & (lead_ref[k] > 0)
                tile = first_column[k, jnp.maximum(slot, 0)]
                total = total + jnp.where(held, tile, 0.0)
            left_panel[a] = total

            @pl.when(a > 0)
            def _():
                spread_copy(a).start()

            return carry

        lax.fori_loop(1, TR + 1, assemble, 0)

    @pl.when(group != 0)
    def _():
        own_spread().wait_recv()

    def send_share(i, carry):
        @pl.when(lax.rem(group + i, GROUPS) != 0)
        def _():
            share_copy(i).start()
        return carry

    lax.fori_loop(1, GROUPS, send_share, 0)
    finish_top(1)
    finish_top(2)

    def finish_share(i, carry):
        @pl.when(lax.rem(group + i, GROUPS) != 0)
        def _():
            share_copy(i).wait_send()

        @pl.when(group != 0)
        def _():
            share_copy(i).wait_recv()

        @pl.when(group == 0)
        def _():
            lead_copy(i).wait_send()
            spread_copy(i).wait_send()

        return carry

    lax.fori_loop(1, GROUPS, finish_share, 0)
    finish_rows(1)
    finish_rows(2)

    for slot in range(COL_SLOTS):
        def sent_columns(i, carry):
            column_copy(slot, i).wait_send()
            return carry

        def sent_rows(i, carry):
            top_copy(slot, i).wait_send()
            row_copy(slot, i).wait_send()
            return carry

        lax.fori_loop(1, GROUPS, sent_columns, 0)
        lax.fori_loop(1, CHILDREN, sent_rows, 0)


def exchange(col_pick, row_pick, lead_held, row_slot, front, left, right,
             lead_block, lead_diag, pivots):
    tile = jax.ShapeDtypeStruct((NB, NB), jnp.float32)
    dma = pltpu.SemaphoreType.DMA
    return pl.pallas_call(
        exchange_kernel,
        out_shape=(
            jax.ShapeDtypeStruct((COL_SLOTS, CHILDREN, ROW_SLOTS * NB, NB), jnp.float32),
            jax.ShapeDtypeStruct((TR, NB, NB), jnp.float32),
            jax.ShapeDtypeStruct((CHILDREN, COL_SLOTS, NB, NB), jnp.float32),
            tile, tile, tile,
        ),
        in_specs=[SMEM, SMEM, SMEM, SMEM, ANY, ANY, ANY, VMEM, VMEM, VMEM],
        out_specs=(ANY, VMEM, VMEM, VMEM, VMEM, VMEM),
        scratch_shapes=[
            pltpu.VMEM((GROUPS, PIV, ROWS), jnp.float32),
            pltpu.VMEM((ROWS, CB), jnp.float32),
            pltpu.VMEM((ROWS, PIV), jnp.float32),
            pltpu.VMEM((CBT, ROWS, NB), jnp.float32),
            pltpu.VMEM((COL_SLOTS, GROUPS, 2, NB, NB), jnp.float32),
            pltpu.VMEM((CBT, NB, NB), jnp.float32),
            pltpu.VMEM((CBT, NB, NB), jnp.float32),
            pltpu.VMEM((CBT, NB, NB), jnp.float32),
            pltpu.VMEM((CHILDREN, ROW_SLOTS, NB, NB), jnp.float32),
            pltpu.VMEM((NB, NB), jnp.float32),
            dma((ROW_SLOTS,)), dma((40,)), dma((40,)),
            dma((COL_SLOTS * GROUPS,)), dma((COL_SLOTS * GROUPS,)), dma((COL_SLOTS,)),
            dma((COL_SLOTS * CHILDREN,)), dma((COL_SLOTS * CHILDREN,)),
            dma((COL_SLOTS * CHILDREN,)), dma((COL_SLOTS * CHILDREN,)), dma((COL_SLOTS,)),
            dma((GROUPS,)), dma((1,)), dma((GROUPS,)), dma((1,)), dma((GROUPS,)), dma((GROUPS,)),
        ],
        compiler_params=pltpu.CompilerParams(
            collective_id=0, has_side_effects=True, vmem_limit_bytes=56 * 2**20
        ),
        name="exchange",
    )(col_pick, row_pick, lead_held, row_slot, front, left, right, lead_block, lead_diag, pivots)


def update_kernel(place_ref, lead_ref, row_slot_ref, col_slot_ref, arrived, left_raw, top_parts,
                  packed, lower, upper, diag, pivots, out_ref, right):
    a = pl.program_id(0)
    child, group = place_ref[0], place_ref[1]
    rows = lax.broadcasted_iota(jnp.int32, (NB, NB), 0)
    cols = lax.broadcasted_iota(jnp.int32, (NB, NB), 1)

    @pl.when(a == 0)
    def _():
        right[...] = jnp.zeros_like(right)
        for k in range(CHILDREN):
            for b in range(TC):
                slot = col_slot_ref[k * TC + b]

                @pl.when((slot >= 0) & (lead_ref[k] > 0))
                def _():
                    span = pl.ds(b * NB, NB)
                    right[:, span] = right[:, span] + top_parts[k, slot]

        chosen_rows = jnp.where(pivots[...] == cols, 1.0, 0.0)
        right[...] = full_dot(lower[...], full_dot(chosen_rows, right[...]))

        @pl.when(group == 0)
        def _():
            right[:, :NB] = jnp.zeros((NB, NB), jnp.float32)

    top = (a == 0) & (child == 0)

    @pl.when(top)
    def _():
        out_ref[...] = right[...]

        @pl.when(group == 0)
        def _():
            out_ref[:, :NB] = packed[...]

    @pl.when(jnp.logical_not(top))
    def _():
        left = full_dot(left_raw[0], upper[...])
        out_ref[...] = -full_dot(left, right[...])
        for k in range(CHILDREN):
            row_slot = row_slot_ref[k * TR + a]

            @pl.when(row_slot >= 0)
            def _():
                base = pl.multiple_of(row_slot * NB, NB)
                for b in range(TC):
                    col_slot = col_slot_ref[k * TC + b]

                    @pl.when(col_slot >= 0)
                    def _():
                        span = pl.ds(b * NB, NB)
                        out_ref[:, span] = out_ref[:, span] + arrived[col_slot, k, pl.ds(base, NB), :]

        on_diag = (lax.rem(group, CHILDREN) == child) & (lax.rem(a, 2) == group // CHILDREN)

        @pl.when(on_diag)
        def _():
            span = pl.ds(pl.multiple_of((a // 2) * NB, NB), NB)
            out_ref[:, span] = out_ref[:, span] + jnp.where(rows == cols, diag[0], 0.0)

        @pl.when(group == 0)
        def _():
            out_ref[:, :NB] = left


def update_front(place, lead_held, row_slot, col_slot, arrived, left_raw, top_parts,
                 packed, lower, upper, diag, pivots):
    return pl.pallas_call(
        update_kernel,
        grid=(TR,),
        out_shape=jax.ShapeDtypeStruct((TR * NB, TC * NB), jnp.float32),
        in_specs=[
            SMEM, SMEM, SMEM, SMEM, VMEM,
            pl.BlockSpec((1, NB, NB), lambda a: (a, 0, 0)),
            VMEM, VMEM, VMEM, VMEM,
            pl.BlockSpec((1, 1, NB), lambda a: (a, 0, 0)),
            VMEM,
        ],
        out_specs=pl.BlockSpec((NB, TC * NB), lambda a: (a, 0)),
        scratch_shapes=[pltpu.VMEM((NB, TC * NB), jnp.float32)],
        compiler_params=pltpu.CompilerParams(vmem_limit_bytes=52 * 2**20),
        name="update_front",
    )(place, lead_held, row_slot, col_slot, arrived, left_raw, top_parts,
      packed, lower, upper, diag, pivots)


def slot_tables(child_map):
    tiles = jnp.arange(PT)
    hits = child_map[:, None, :] == tiles[None, :, None]
    present = jnp.any(hits, axis=2)
    source = jnp.sum(jnp.where(hits, jnp.arange(CBT)[None, None, :], 0), axis=2)

    def by_class(classes, capacity):
        count = PT // classes
        held = present.reshape(CHILDREN, count, classes).transpose(0, 2, 1)
        tile = source.reshape(CHILDREN, count, classes).transpose(0, 2, 1)
        earlier = jnp.arange(count)[None, :] < jnp.arange(count)[:, None]
        rank = jnp.sum((held[:, :, None, :] & earlier).astype(jnp.int32), axis=3)
        slot = jnp.where(held, rank, -1)
        wanted = slot[:, :, None, :] == jnp.arange(capacity)[None, None, :, None]
        pick = jnp.sum(jnp.where(wanted, tile[:, :, None, :], 0), axis=3)
        return slot, pick

    return present, by_class(GROUPS, COL_SLOTS), by_class(CHILDREN, ROW_SLOTS)


def body(front_child, left_factor, right_factor, child_map, parent_diag, lead_block, pivots):
    child = lax.axis_index("child")
    group = lax.axis_index("grp")
    present, (col_slot, col_pick), (row_slot, row_pick) = slot_tables(child_map)

    def mine(table, index, dim):
        return lax.dynamic_index_in_dim(table, index, dim, keepdims=False).reshape(-1)

    lead_held = present[:, 0].astype(jnp.int32)
    row_slots = mine(row_slot, child, 1)
    col_slots = mine(col_slot, group, 1)
    pivot_column = pivots.reshape(NB, 1)
    arrived, left_raw, top_parts, packed, lower, upper = exchange(
        mine(col_pick, child, 0), mine(row_pick, child, 0), lead_held, row_slots,
        front_child[0], left_factor[0], right_factor[0], lead_block,
        parent_diag[:NB].reshape(1, NB), pivot_column,
    )
    diag = lax.dynamic_index_in_dim(
        parent_diag.reshape(TR, CHILDREN, NB), child, 1, keepdims=True
    )
    front = update_front(
        jnp.stack([child, group]).astype(jnp.int32), lead_held, row_slots, col_slots,
        arrived, left_raw, top_parts, packed, lower, upper, diag, pivot_column,
    )
    return front.reshape(1, TR * NB, 1, TC * NB)


def solution(mesh):
    in_specs = (
        P("child", "grp", None),
        P("child", "grp", None),
        P("child", None, "grp"),
        P(),
        P(),
        P(),
        P(),
    )
    out_specs = P("child", None, "grp", None)
    return jax.shard_map(body, mesh=mesh, in_specs=in_specs, out_specs=out_specs, check_vma=False)
```

```python
import jax
import jax.numpy as jnp
from jax import lax
from jax.experimental import pallas as pl
from jax.experimental.pallas import tpu as pltpu
from jax.sharding import PartitionSpec as P

NB = 128
CB = 4096
PIV = 1280
NP = 16384
CHILDREN = 8
GROUPS = 16
RING = 4
CBT = CB // NB
PT = NP // NB
TR = PT // CHILDREN
TC = PT // GROUPS
COL_SLOTS = 3
ROW_SLOTS = 6
ROWS = CB // GROUPS
COL_SLOT = 0
ROW_SLOT = CHILDREN
COL_PICK = 2 * CHILDREN
ROW_PICK = COL_PICK + COL_SLOTS * CHILDREN
TABLE_ROWS = ROW_PICK + ROW_SLOTS * CHILDREN
HALF = PIV // 2
QUARTER = PIV // 4
MESH = pl.DeviceIdType.MESH
ANY = pl.BlockSpec(memory_space=pl.ANY)
VMEM = pl.BlockSpec(memory_space=pltpu.VMEM)
SMEM = pl.BlockSpec(memory_space=pltpu.SMEM)


def full_dot(a, b):
    return jnp.dot(a, b, precision=lax.Precision.HIGHEST, preferred_element_type=jnp.float32)


def table_kernel(map_ref, table_ref):
    lanes = lax.broadcasted_iota(jnp.int32, (CHILDREN, PT), 1)
    tiles = map_ref[...]
    source = jnp.full((CHILDREN, PT), -1, jnp.int32)
    for t in range(CBT):
        source = jnp.where(tiles[:, t:t + 1] == lanes, t, source)
    held = (source >= 0).astype(jnp.int32)

    def fill(classes, capacity, slot_base, pick_base):
        rank = jnp.zeros((CHILDREN, PT), jnp.int32)
        for shift in range(classes, PT, classes):
            rank = rank + jnp.where(lanes >= shift, pltpu.roll(held, shift, 1), 0)
        slots = jnp.where(held > 0, rank, -1)
        table_ref[slot_base:slot_base + CHILDREN] = slots
        for slot in range(capacity):
            picked = jnp.where(slots == slot, source, 0)
            shift = classes
            while shift < PT:
                picked = picked + pltpu.roll(picked, shift, 1)
                shift *= 2
            base = pick_base + slot * CHILDREN
            table_ref[base:base + CHILDREN] = picked

    fill(GROUPS, COL_SLOTS, COL_SLOT, COL_PICK)
    fill(CHILDREN, ROW_SLOTS, ROW_SLOT, ROW_PICK)


def slot_table(child_map):
    return pl.pallas_call(
        table_kernel,
        out_shape=jax.ShapeDtypeStruct((TABLE_ROWS, PT), jnp.int32),
        name="slot_table",
    )(child_map)


def permute_rows(pivots, values):
    rows = lax.broadcasted_iota(jnp.int32, (NB, NB), 0)
    chosen = jnp.where(rows == pivots[...], 1.0, 0.0)
    return lax.dot_general(
        chosen, values, (((0,), (0,)), ((), ())),
        precision=lax.Precision.HIGHEST, preferred_element_type=jnp.float32,
    )


def factor_tile(packed_ref, lower_ref, upper_ref):
    rows = lax.broadcasted_iota(jnp.int32, (NB, NB), 0)
    cols = lax.broadcasted_iota(jnp.int32, (NB, NB), 1)
    lane = lax.broadcasted_iota(jnp.int32, (1, NB), 1)
    eye = jnp.where(rows == cols, 1.0, 0.0)
    lower_ref[...] = eye
    upper_ref[...] = eye

    def eliminate(j, carry):
        working = packed_ref[...]
        upper = upper_ref[...]
        row_part = packed_ref[pl.ds(j, 1), :]
        row_lower = lower_ref[pl.ds(j, 1), :]
        column = jnp.sum(jnp.where(cols == j, working, 0.0), axis=1, keepdims=True)
        column_upper = jnp.sum(jnp.where(cols == j, upper, 0.0), axis=1, keepdims=True)
        pivot_value = jnp.sum(jnp.where(lane == j, row_part, 0.0), axis=1, keepdims=True)
        multiplier = jnp.where(rows[:, :1] > j, column / pivot_value, 0.0)
        right = jnp.where(lane > j, row_part, 0.0)
        packed_ref[...] = jnp.where(
            (cols == j) & (rows > j), multiplier, working - multiplier * right
        )
        lower_ref[...] = lower_ref[...] - multiplier * row_lower
        scaled = column_upper / pivot_value
        upper_ref[...] = jnp.where(cols == j, scaled, upper - scaled * right)
        return carry

    lax.fori_loop(0, NB, eliminate, 0)


def exchange_kernel(table_ref, front_hbm, left_hbm, right_hbm, lead_block, diag, pivots,
                    arrived, left_panel, top_parts, packed, lower, upper,
                    factors, front, left, contribution, col_chosen, column_0, column_1, column_2,
                    first_column, raw_lead,
                    load_sem, ring_send, ring_recv, col_send, col_recv, own_col_sem,
                    top_send, top_recv, row_send, row_recv, own_row_sem, lead_send, lead_recv,
                    spread_send, spread_recv, share_send, share_recv):
    child = lax.axis_index("child")
    group = lax.axis_index("grp")
    at_y, at_x = group // RING, group % RING

    load_right = pltpu.make_async_copy(right_hbm, factors.at[group], load_sem.at[0])
    load_left = pltpu.make_async_copy(left_hbm, left, load_sem.at[1])
    load_front = pltpu.make_async_copy(front_hbm, front, load_sem.at[2])
    load_right.start()
    load_left.start()
    load_front.start()

    barrier = pltpu.get_barrier_semaphore()

    def greet_group(i, carry):
        pl.semaphore_signal(
            barrier, inc=1, device_id=(child, lax.rem(group + i, GROUPS)), device_id_type=MESH
        )
        return carry

    def greet_child(i, carry):
        pl.semaphore_signal(
            barrier, inc=1, device_id=(lax.rem(child + i, CHILDREN), group), device_id_type=MESH
        )
        return carry

    lax.fori_loop(1, GROUPS, greet_group, 0)
    lax.fori_loop(1, CHILDREN, greet_child, 0)
    pl.semaphore_wait(barrier, GROUPS + CHILDREN - 2)

    def place(half, first, second):
        return second * RING + first if half == 0 else first * RING + second

    def turn(position, by):
        return lax.rem(position + by + RING, RING)

    def piece(half, block, quarter):
        if quarter is None:
            return factors.at[block, pl.ds(half * HALF, HALF)]
        return factors.at[block, pl.ds(half * HALF + quarter * QUARTER, QUARTER)]

    copies = {}

    def make(key, half, block, quarter, target):
        number = len(copies)
        ref = piece(half, block, quarter)
        copies[key] = pltpu.make_async_remote_copy(
            src_ref=ref, dst_ref=ref, send_sem=ring_send.at[number], recv_sem=ring_recv.at[number],
            device_id=(child, target), device_id_type=MESH,
        )

    lines = (0, -1, 1, 2)
    for half in (0, 1):
        first, second = (at_x, at_y) if half == 0 else (at_y, at_x)
        for way in (1, -1):
            target = place(half, turn(first, way), second)
            make((half, "a", way), half, place(half, first, second), None, target)
            make((half, "af", way), half, place(half, turn(first, -way), second),
                 0 if way == 1 else 1, target)
        for line in lines:
            column = turn(first, line)
            for way in (1, -1):
                target = place(half, first, turn(second, way))
                make((half, line, way), half, place(half, column, second), None, target)
                make((half, line, "f", way), half, place(half, column, turn(second, -way)),
                     0 if way == 1 else 1, target)

    def start(*key):
        for half in (0, 1):
            for way in (1, -1):
                copies[(half,) + key + (way,)].start()

    def arrive(*key):
        for half in (0, 1):
            for way in (1, -1):
                copies[(half,) + key + (way,)].wait_recv()

    def multiply(offsets):
        def one(i, carry):
            block = jnp.int32(0)
            for number, (dy, dx) in enumerate(offsets):
                block = jnp.where(i == number, turn(at_y, dy) * RING + turn(at_x, dx), block)
            product = full_dot(left[...], factors[block])
            base = pl.multiple_of(block * ROWS, ROWS)
            result = front[:, pl.ds(base, ROWS)] - product
            contribution[2 * block] = result[:, :NB]
            contribution[2 * block + 1] = result[:, NB:]
            return carry

        lax.fori_loop(0, len(offsets), one, 0)

    load_right.wait()
    start("a")
    start(0)
    load_left.wait()
    load_front.wait()
    multiply([(0, 0)])
    arrive("a")
    start("af")
    start(-1)
    start(1)
    arrive(0)
    start(0, "f")
    multiply([(0, 1), (0, -1), (1, 0), (-1, 0)])
    arrive("af")
    start(2)
    arrive(0, "f")
    multiply([(0, 2), (2, 0)])
    arrive(-1)
    start(-1, "f")
    arrive(1)
    start(1, "f")
    multiply([(1, 1), (1, -1), (-1, 1), (-1, -1)])
    arrive(2)
    start(2, "f")
    arrive(-1, "f")
    arrive(1, "f")
    multiply([(1, 2), (-1, 2), (2, 1), (2, -1)])
    arrive(2, "f")
    multiply([(2, 2)])

    by_column = (column_0, column_1, column_2)

    def column_target(i):
        return lax.rem(group + i, GROUPS)

    def column_copy(slot, i):
        target = column_target(i)
        return pltpu.make_async_remote_copy(
            src_ref=col_chosen.at[slot, target],
            dst_ref=by_column[slot].at[pl.ds(2 * group, 2)],
            send_sem=col_send.at[slot * GROUPS + i], recv_sem=col_recv.at[slot * GROUPS + i],
            device_id=(child, target), device_id_type=MESH,
        )

    def own_column_copy(slot):
        return pltpu.make_async_copy(
            col_chosen.at[slot, group], by_column[slot].at[pl.ds(2 * group, 2)],
            own_col_sem.at[slot],
        )

    def select_column(slot, target):
        tile = contribution[table_ref[COL_PICK + slot * CHILDREN + child, target]]
        col_chosen[slot, target] = tile.reshape(2, NB, NB)

    def pass_columns(slot):
        def send_column(i, carry):
            select_column(slot, column_target(i))
            column_copy(slot, i).start()
            return carry

        lax.fori_loop(1, GROUPS, send_column, 0)
        select_column(slot, group)
        own_column_copy(slot).start()

    pass_columns(0)
    pass_columns(1)
    pass_columns(2)

    for key in copies:
        copies[key].wait_send()

    def top_copy(slot, i):
        return pltpu.make_async_remote_copy(
            src_ref=top_parts.at[child, slot], dst_ref=top_parts.at[child, slot],
            send_sem=top_send.at[slot * CHILDREN + i], recv_sem=top_recv.at[slot * CHILDREN + i],
            device_id=(lax.rem(child + i, CHILDREN), group), device_id_type=MESH,
        )

    def row_buffer(slot, target):
        number = slot * CHILDREN + target
        lanes = pl.multiple_of(lax.rem(number, 2) * NB, NB)
        return factors.at[number // 2, pl.ds(0, ROW_SLOTS * NB), pl.ds(lanes, NB)]

    def row_copy(slot, i):
        target = lax.rem(child + i, CHILDREN)
        return pltpu.make_async_remote_copy(
            src_ref=row_buffer(slot, target), dst_ref=arrived.at[slot, child],
            send_sem=row_send.at[slot * CHILDREN + i], recv_sem=row_recv.at[slot * CHILDREN + i],
            device_id=(target, group), device_id_type=MESH,
        )

    def own_row_copy(slot):
        return pltpu.make_async_copy(
            row_buffer(slot, child), arrived.at[slot, child], own_row_sem.at[slot]
        )

    def select_rows(slot, target):
        number = slot * CHILDREN + target
        lanes = pl.multiple_of(lax.rem(number, 2) * NB, NB)
        for r in range(ROW_SLOTS):
            tile = by_column[slot][table_ref[ROW_PICK + r * CHILDREN + child, target]]
            factors[number // 2, pl.ds(r * NB, NB), pl.ds(lanes, NB)] = tile

    def pass_rows(slot):
        def finish(i, carry):
            column_copy(slot, i).wait_recv()
            return carry

        lax.fori_loop(1, GROUPS, finish, 0)
        own_column_copy(slot).wait()
        top_parts[child, slot] = by_column[slot][table_ref[ROW_PICK + child, 0]]

        def send_top(i, carry):
            top_copy(slot, i).start()
            return carry

        lax.fori_loop(1, CHILDREN, send_top, 0)

        def send_rows(i, carry):
            select_rows(slot, lax.rem(child + i, CHILDREN))
            row_copy(slot, i).start()
            return carry

        lax.fori_loop(1, CHILDREN, send_rows, 0)
        select_rows(slot, child)
        own_row_copy(slot).start()

    def finish_top(slot):
        def arrive_top(i, carry):
            top_copy(slot, i).wait_recv()
            return carry

        lax.fori_loop(1, CHILDREN, arrive_top, 0)

    def finish_rows(slot):
        def finish(i, carry):
            row_copy(slot, i).wait_recv()
            return carry

        lax.fori_loop(1, CHILDREN, finish, 0)
        own_row_copy(slot).wait()

    def lead_copy(target):
        return pltpu.make_async_remote_copy(
            src_ref=raw_lead, dst_ref=raw_lead,
            send_sem=lead_send.at[target], recv_sem=lead_recv.at[0],
            device_id=(child, target), device_id_type=MESH,
        )

    def spread_copy(target):
        return pltpu.make_async_remote_copy(
            src_ref=left_panel.at[target], dst_ref=left_panel.at[target],
            send_sem=spread_send.at[target], recv_sem=spread_recv.at[0],
            device_id=(child, target), device_id_type=MESH,
        )

    def own_spread():
        return pltpu.make_async_remote_copy(
            src_ref=left_panel.at[group], dst_ref=left_panel.at[group],
            send_sem=spread_send.at[0], recv_sem=spread_recv.at[0],
            device_id=(child, 0), device_id_type=MESH,
        )

    def share_copy(i):
        return pltpu.make_async_remote_copy(
            src_ref=left_panel.at[group], dst_ref=left_panel.at[group],
            send_sem=share_send.at[i], recv_sem=share_recv.at[i],
            device_id=(child, lax.rem(group + i, GROUPS)), device_id_type=MESH,
        )

    pass_rows(0)
    finish_top(0)
    rows = lax.broadcasted_iota(jnp.int32, (NB, NB), 0)
    cols = lax.broadcasted_iota(jnp.int32, (NB, NB), 1)

    @pl.when(group == 0)
    def _():
        total = lead_block[...] + jnp.where(rows == cols, diag[0:1, :], 0.0)
        for k in range(CHILDREN):
            total = total + jnp.where(table_ref[COL_SLOT + k, 0] >= 0, top_parts[k, 0], 0.0)
        raw_lead[...] = permute_rows(pivots, total)

        def send_lead(i, carry):
            lead_copy(i).start()
            return carry

        lax.fori_loop(1, GROUPS, send_lead, 0)

    pass_rows(1)

    @pl.when(group != 0)
    def _():
        lead_copy(0).wait_recv()

    packed[...] = raw_lead[...]
    factor_tile(packed, lower, upper)
    pass_rows(2)

    finish_rows(0)

    @pl.when(group == 0)
    def _():
        loads = [
            pltpu.make_async_copy(
                arrived.at[0, :, pl.ds(r * NB, NB), :], first_column.at[:, r], load_sem.at[r]
            )
            for r in range(ROW_SLOTS)
        ]
        for load in loads:
            load.start()
        for load in loads:
            load.wait()

        def assemble(i, carry):
            a = lax.rem(i, TR)
            total = jnp.zeros((NB, NB), jnp.float32)
            for k in range(CHILDREN):
                slot = table_ref[ROW_SLOT + k, a * CHILDREN + child]
                held = (slot >= 0) & (table_ref[COL_SLOT + k, 0] >= 0)
                tile = first_column[k, jnp.maximum(slot, 0)]
                total = total + jnp.where(held, tile, 0.0)
            left_panel[a] = total

            @pl.when(a > 0)
            def _():
                spread_copy(a).start()

            return carry

        lax.fori_loop(1, TR + 1, assemble, 0)

    @pl.when(group != 0)
    def _():
        own_spread().wait_recv()

    def send_share(i, carry):
        @pl.when(lax.rem(group + i, GROUPS) != 0)
        def _():
            share_copy(i).start()
        return carry

    lax.fori_loop(1, GROUPS, send_share, 0)
    finish_top(1)
    finish_top(2)

    def finish_share(i, carry):
        @pl.when(lax.rem(group + i, GROUPS) != 0)
        def _():
            share_copy(i).wait_send()

        @pl.when(group != 0)
        def _():
            share_copy(i).wait_recv()

        @pl.when(group == 0)
        def _():
            lead_copy(i).wait_send()
            spread_copy(i).wait_send()

        return carry

    lax.fori_loop(1, GROUPS, finish_share, 0)
    finish_rows(1)
    finish_rows(2)

    for slot in range(COL_SLOTS):
        def sent_columns(i, carry):
            column_copy(slot, i).wait_send()
            return carry

        def sent_rows(i, carry):
            top_copy(slot, i).wait_send()
            row_copy(slot, i).wait_send()
            return carry

        lax.fori_loop(1, GROUPS, sent_columns, 0)
        lax.fori_loop(1, CHILDREN, sent_rows, 0)


def exchange(table, front, left, right, lead_block, diag, pivots):
    tile = jax.ShapeDtypeStruct((NB, NB), jnp.float32)
    dma = pltpu.SemaphoreType.DMA
    return pl.pallas_call(
        exchange_kernel,
        out_shape=(
            jax.ShapeDtypeStruct((COL_SLOTS, CHILDREN, ROW_SLOTS * NB, NB), jnp.float32),
            jax.ShapeDtypeStruct((TR, NB, NB), jnp.float32),
            jax.ShapeDtypeStruct((CHILDREN, COL_SLOTS, NB, NB), jnp.float32),
            tile, tile, tile,
        ),
        in_specs=[SMEM, ANY, ANY, ANY, VMEM, VMEM, VMEM],
        out_specs=(ANY, VMEM, VMEM, VMEM, VMEM, VMEM),
        scratch_shapes=[
            pltpu.VMEM((GROUPS, PIV, ROWS), jnp.float32),
            pltpu.VMEM((ROWS, CB), jnp.float32),
            pltpu.VMEM((ROWS, PIV), jnp.float32),
            pltpu.VMEM((CBT, ROWS, NB), jnp.float32),
            pltpu.VMEM((COL_SLOTS, GROUPS, 2, NB, NB), jnp.float32),
            pltpu.VMEM((CBT, NB, NB), jnp.float32),
            pltpu.VMEM((CBT, NB, NB), jnp.float32),
            pltpu.VMEM((CBT, NB, NB), jnp.float32),
            pltpu.VMEM((CHILDREN, ROW_SLOTS, NB, NB), jnp.float32),
            pltpu.VMEM((NB, NB), jnp.float32),
            dma((ROW_SLOTS,)), dma((40,)), dma((40,)),
            dma((COL_SLOTS * GROUPS,)), dma((COL_SLOTS * GROUPS,)), dma((COL_SLOTS,)),
            dma((COL_SLOTS * CHILDREN,)), dma((COL_SLOTS * CHILDREN,)),
            dma((COL_SLOTS * CHILDREN,)), dma((COL_SLOTS * CHILDREN,)), dma((COL_SLOTS,)),
            dma((GROUPS,)), dma((1,)), dma((GROUPS,)), dma((1,)), dma((GROUPS,)), dma((GROUPS,)),
        ],
        compiler_params=pltpu.CompilerParams(
            collective_id=0, has_side_effects=True, vmem_limit_bytes=56 * 2**20
        ),
        name="exchange",
    )(table, front, left, right, lead_block, diag, pivots)


def split(values):
    high = values.astype(jnp.bfloat16)
    return high, (values - high.astype(jnp.float32)).astype(jnp.bfloat16)


def update_kernel(table_ref, arrived, left_raw, top_parts,
                  packed, lower, upper, diag, pivots, out_ref, right, right_parts, total):
    a = pl.program_id(0)
    child = lax.axis_index("child")
    group = lax.axis_index("grp")
    rows = lax.broadcasted_iota(jnp.int32, (NB, NB), 0)
    cols = lax.broadcasted_iota(jnp.int32, (NB, NB), 1)

    @pl.when(a == 0)
    def _():
        right[...] = jnp.zeros_like(right)
        for k in range(CHILDREN):
            for b in range(TC):
                slot = table_ref[COL_SLOT + k, b * GROUPS + group]

                @pl.when((slot >= 0) & (table_ref[COL_SLOT + k, 0] >= 0))
                def _():
                    span = pl.ds(b * NB, NB)
                    right[:, span] = right[:, span] + top_parts[k, slot]

        right[...] = full_dot(lower[...], permute_rows(pivots, right[...]))

        @pl.when(group == 0)
        def _():
            right[:, :NB] = jnp.zeros((NB, NB), jnp.float32)

        high, low = split(right[...])
        right_parts[0:NB] = high
        right_parts[NB:2 * NB] = low
        right_parts[2 * NB:] = high

    top = (a == 0) & (child == 0)

    @pl.when(top)
    def _():
        total[...] = right[...]

        @pl.when(group == 0)
        def _():
            total[:, :NB] = packed[...]

    @pl.when(jnp.logical_not(top))
    def _():
        left = full_dot(left_raw[0], upper[...])
        high, low = split(left)
        left_parts = jnp.concatenate([high, high, low], axis=1)
        total[...] = -jnp.dot(
            left_parts, right_parts[...], preferred_element_type=jnp.float32
        )
        for k in range(CHILDREN):
            row_slot = table_ref[ROW_SLOT + k, a * CHILDREN + child]

            @pl.when(row_slot >= 0)
            def _():
                base = pl.multiple_of(row_slot * NB, NB)
                for b in range(TC):
                    col_slot = table_ref[COL_SLOT + k, b * GROUPS + group]

                    @pl.when(col_slot >= 0)
                    def _():
                        span = pl.ds(b * NB, NB)
                        total[:, span] = total[:, span] + arrived[col_slot, k, pl.ds(base, NB), :]

        on_diag = (lax.rem(group, CHILDREN) == child) & (lax.rem(a, 2) == group // CHILDREN)

        @pl.when(on_diag)
        def _():
            span = pl.ds(pl.multiple_of((a // 2) * NB, NB), NB)
            entries = diag[pl.ds(a * CHILDREN + child, 1), :]
            total[:, span] = total[:, span] + jnp.where(rows == cols, entries, 0.0)

        @pl.when(group == 0)
        def _():
            total[:, :NB] = left

    out_ref[0, :, 0, :] = total[...]


def update_front(table, arrived, left_raw, top_parts,
                 packed, lower, upper, diag, pivots):
    return pl.pallas_call(
        update_kernel,
        grid=(TR,),
        out_shape=jax.ShapeDtypeStruct((1, TR * NB, 1, TC * NB), jnp.float32),
        in_specs=[
            SMEM, VMEM,
            pl.BlockSpec((1, NB, NB), lambda a: (a, 0, 0)),
            VMEM, VMEM, VMEM, VMEM, VMEM, VMEM,
        ],
        out_specs=pl.BlockSpec((1, NB, 1, TC * NB), lambda a: (0, a, 0, 0)),
        scratch_shapes=[
            pltpu.VMEM((NB, TC * NB), jnp.float32),
            pltpu.VMEM((3 * NB, TC * NB), jnp.bfloat16),
            pltpu.VMEM((NB, TC * NB), jnp.float32),
        ],
        compiler_params=pltpu.CompilerParams(vmem_limit_bytes=60 * 2**20),
        name="update_front",
    )(table, arrived, left_raw, top_parts,
      packed, lower, upper, diag, pivots)


def body(front_child, left_factor, right_factor, child_map, parent_diag, lead_block, pivots):
    diag = parent_diag.reshape(PT, NB)
    pivot_row = pivots.reshape(1, NB)
    table = slot_table(child_map)
    arrived, left_raw, top_parts, packed, lower, upper = exchange(
        table, front_child[0], left_factor[0], right_factor[0], lead_block, diag, pivot_row
    )
    return update_front(
        table, arrived, left_raw, top_parts, packed, lower, upper, diag, pivot_row
    )


def solution(mesh):
    in_specs = (
        P("child", "grp", None),
        P("child", "grp", None),
        P("child", None, "grp"),
        P(),
        P(),
        P(),
        P(),
    )
    out_specs = P("child", None, "grp", None)
    return jax.shard_map(body, mesh=mesh, in_specs=in_specs, out_specs=out_specs, check_vma=False)
```

```python
import jax
import jax.numpy as jnp
from jax import lax
from jax.experimental import pallas as pl
from jax.experimental.pallas import tpu as pltpu
from jax.sharding import PartitionSpec as P

NB = 128
CB = 4096
PIV = 1280
NP = 16384
CHILDREN = 8
GROUPS = 16
RING = 4
CBT = CB // NB
PT = NP // NB
TR = PT // CHILDREN
TC = PT // GROUPS
COL_SLOTS = 3
ROW_SLOTS = 6
ROWS = CB // GROUPS
COL_SLOT = 0
ROW_SLOT = CHILDREN
COL_PICK = 2 * CHILDREN
ROW_PICK = COL_PICK + COL_SLOTS * CHILDREN
TABLE_ROWS = ROW_PICK + ROW_SLOTS * CHILDREN
MESH = pl.DeviceIdType.MESH
ANY = pl.BlockSpec(memory_space=pl.ANY)
VMEM = pl.BlockSpec(memory_space=pltpu.VMEM)
SMEM = pl.BlockSpec(memory_space=pltpu.SMEM)


def full_dot(a, b):
    return jnp.dot(a, b, precision=lax.Precision.HIGHEST, preferred_element_type=jnp.float32)


def table_kernel(map_ref, table_ref):
    lanes = lax.broadcasted_iota(jnp.int32, (CHILDREN, PT), 1)
    tiles = map_ref[...]
    source = jnp.full((CHILDREN, PT), -1, jnp.int32)
    for t in range(CBT):
        source = jnp.where(tiles[:, t:t + 1] == lanes, t, source)
    held = (source >= 0).astype(jnp.int32)

    def fill(classes, capacity, slot_base, pick_base):
        rank = jnp.zeros((CHILDREN, PT), jnp.int32)
        for shift in range(classes, PT, classes):
            rank = rank + jnp.where(lanes >= shift, pltpu.roll(held, shift, 1), 0)
        slots = jnp.where(held > 0, rank, -1)
        table_ref[slot_base:slot_base + CHILDREN] = slots
        for slot in range(capacity):
            picked = jnp.where(slots == slot, source, 0)
            shift = classes
            while shift < PT:
                picked = picked + pltpu.roll(picked, shift, 1)
                shift *= 2
            base = pick_base + slot * CHILDREN
            table_ref[base:base + CHILDREN] = picked

    fill(GROUPS, COL_SLOTS, COL_SLOT, COL_PICK)
    fill(CHILDREN, ROW_SLOTS, ROW_SLOT, ROW_PICK)


def slot_table(child_map):
    return pl.pallas_call(
        table_kernel,
        out_shape=jax.ShapeDtypeStruct((TABLE_ROWS, PT), jnp.int32),
        name="slot_table",
    )(child_map)


def permute_rows(pivots, values):
    rows = lax.broadcasted_iota(jnp.int32, (NB, NB), 0)
    chosen = jnp.where(rows == pivots[...], 1.0, 0.0)
    return lax.dot_general(
        chosen, values, (((0,), (0,)), ((), ())),
        precision=lax.Precision.HIGHEST, preferred_element_type=jnp.float32,
    )


def factor_tile(packed_ref, lower_ref, upper_ref):
    rows = lax.broadcasted_iota(jnp.int32, (NB, NB), 0)
    cols = lax.broadcasted_iota(jnp.int32, (NB, NB), 1)
    lane = lax.broadcasted_iota(jnp.int32, (1, NB), 1)
    eye = jnp.where(rows == cols, 1.0, 0.0)
    lower_ref[...] = eye
    upper_ref[...] = eye

    def eliminate(j, carry):
        working = packed_ref[...]
        upper = upper_ref[...]
        row_part = packed_ref[pl.ds(j, 1), :]
        row_lower = lower_ref[pl.ds(j, 1), :]
        column = jnp.sum(jnp.where(cols == j, working, 0.0), axis=1, keepdims=True)
        column_upper = jnp.sum(jnp.where(cols == j, upper, 0.0), axis=1, keepdims=True)
        pivot_value = jnp.sum(jnp.where(lane == j, row_part, 0.0), axis=1, keepdims=True)
        multiplier = jnp.where(rows[:, :1] > j, column / pivot_value, 0.0)
        right = jnp.where(lane > j, row_part, 0.0)
        packed_ref[...] = jnp.where(
            (cols == j) & (rows > j), multiplier, working - multiplier * right
        )
        lower_ref[...] = lower_ref[...] - multiplier * row_lower
        scaled = column_upper / pivot_value
        upper_ref[...] = jnp.where(cols == j, scaled, upper - scaled * right)
        return carry

    lax.fori_loop(0, NB, eliminate, 0)


def exchange_kernel(table_ref, front_hbm, left_hbm, right_hbm, lead_block, diag, pivots,
                    arrived, left_panel, top_parts, packed, lower, upper,
                    lefts, rights, products, returned, front, contribution, col_chosen, column_0, column_1, column_2,
                    row_chosen, first_column, raw_lead,
                    load_sem, ring_send, ring_recv, back_send, back_recv, col_send, col_recv, own_col_sem,
                    top_send, top_recv, row_send, row_recv, own_row_sem, lead_send, lead_recv,
                    spread_send, spread_recv, share_send, share_recv):
    child = lax.axis_index("child")
    group = lax.axis_index("grp")
    core = lax.rem(child, 2)
    at_y, at_x = group // RING, lax.rem(group, RING)
    along = jnp.where(core == 0, at_x, at_y)
    across = jnp.where(core == 0, at_y, at_x)

    load_right = pltpu.make_async_copy(right_hbm, rights.at[across], load_sem.at[0])
    load_left = pltpu.make_async_copy(left_hbm, lefts.at[along], load_sem.at[1])
    load_front = pltpu.make_async_copy(front_hbm, front, load_sem.at[2])
    load_right.start()
    load_left.start()
    load_front.start()

    barrier = pltpu.get_barrier_semaphore()

    def greet_group(i, carry):
        pl.semaphore_signal(
            barrier, inc=1, device_id=(child, lax.rem(group + i, GROUPS)), device_id_type=MESH
        )
        return carry

    def greet_child(i, carry):
        pl.semaphore_signal(
            barrier, inc=1, device_id=(lax.rem(child + i, CHILDREN), group), device_id_type=MESH
        )
        return carry

    lax.fori_loop(1, GROUPS, greet_group, 0)
    lax.fori_loop(1, CHILDREN, greet_child, 0)
    pl.semaphore_wait(barrier, GROUPS + CHILDREN - 2)

    def turn(position, by):
        return lax.rem(position + by + RING, RING)

    def place(u, v):
        return jnp.where(core == 0, v * RING + u, u * RING + v)

    gathers = {}

    def make(key, blocks, block, chunk, target):
        number = len(gathers)
        size = blocks.shape[1] // 2
        ref = blocks.at[block, pl.ds(chunk * size, size)]
        gathers[key] = pltpu.make_async_remote_copy(
            src_ref=ref, dst_ref=ref, send_sem=ring_send.at[number], recv_sem=ring_recv.at[number],
            device_id=(child, target), device_id_type=MESH,
        )

    for name, blocks, at in (("l", lefts, along), ("r", rights, across)):
        for way in (1, -1):
            target = place(turn(along, way), across) if name == "l" else place(along, turn(across, way))
            first = 0 if way == 1 else 1
            make((name, way, 0), blocks, at, first, target)
            make((name, way, 1), blocks, at, 1 - first, target)
            make((name, way, 2), blocks, turn(at, -way), first, target)

    def start(name, step):
        gathers[(name, 1, step)].start()
        gathers[(name, -1, step)].start()

    def arrive(name, step):
        gathers[(name, 1, step)].wait_recv()
        gathers[(name, -1, step)].wait_recv()

    def return_copy(to, piece):
        target = turn(along, to)
        number = to * RING + piece
        return pltpu.make_async_remote_copy(
            src_ref=products.at[target, piece], dst_ref=returned.at[along, piece],
            send_sem=back_send.at[number], recv_sem=back_recv.at[number],
            device_id=(child, place(target, across)), device_id_type=MESH,
        )

    def multiply(pairs):
        def one(i, carry):
            to, line = jnp.int32(0), jnp.int32(0)
            for number, (pair_to, pair_line) in enumerate(pairs):
                to = jnp.where(i == number, pair_to, to)
                line = jnp.where(i == number, pair_line, line)
            target, piece = turn(along, to), turn(across, line)
            product = full_dot(lefts[target], rights[piece])

            @pl.when(to == 0)
            def _():
                returned[along, piece] = product

            @pl.when(to != 0)
            def _():
                products[target, piece] = product
                return_copy(to, piece).start()

            return carry

        lax.fori_loop(0, len(pairs), one, 0)

    load_left.wait()
    start("l", 0)
    load_right.wait()
    start("r", 0)
    start("l", 1)
    start("r", 1)
    multiply([(0, 0)])
    arrive("l", 0)
    start("l", 2)
    arrive("r", 0)
    start("r", 2)
    arrive("l", 1)
    multiply([(1, 0), (3, 0)])
    arrive("r", 1)
    multiply([(1, 1), (3, 1), (1, 3), (3, 3), (0, 1), (0, 3)])
    arrive("l", 2)
    multiply([(2, 0), (2, 1), (2, 3)])
    arrive("r", 2)
    multiply([(2, 2), (1, 2), (3, 2), (0, 2)])
    load_front.wait()

    def subtract(source, piece):
        block = place(source, piece)
        base = pl.multiple_of(block * ROWS, ROWS)
        result = front[:, pl.ds(base, ROWS)] - returned[source, piece]
        contribution[2 * block] = result[:, :NB]
        contribution[2 * block + 1] = result[:, NB:]

    def subtract_own(piece, carry):
        subtract(along, piece)
        return carry

    lax.fori_loop(0, RING, subtract_own, 0)

    def subtract_returned(number, carry):
        to, line = 1 + number // RING, turn(across, lax.rem(number, RING))
        return_copy(to, line).wait_recv()
        subtract(turn(along, -to), line)
        return carry

    lax.fori_loop(0, (RING - 1) * RING, subtract_returned, 0)

    by_column = (column_0, column_1, column_2)

    def column_target(i):
        return lax.rem(group + i, GROUPS)

    def column_copy(slot, i):
        target = column_target(i)
        return pltpu.make_async_remote_copy(
            src_ref=col_chosen.at[slot, target],
            dst_ref=by_column[slot].at[pl.ds(2 * group, 2)],
            send_sem=col_send.at[slot * GROUPS + i], recv_sem=col_recv.at[slot * GROUPS + i],
            device_id=(child, target), device_id_type=MESH,
        )

    def own_column_copy(slot):
        return pltpu.make_async_copy(
            col_chosen.at[slot, group], by_column[slot].at[pl.ds(2 * group, 2)],
            own_col_sem.at[slot],
        )

    def select_column(slot, target):
        tile = contribution[table_ref[COL_PICK + slot * CHILDREN + child, target]]
        col_chosen[slot, target] = tile.reshape(2, NB, NB)

    def pass_columns(slot):
        def send_column(i, carry):
            select_column(slot, column_target(i))
            column_copy(slot, i).start()
            return carry

        lax.fori_loop(1, GROUPS, send_column, 0)
        select_column(slot, group)
        own_column_copy(slot).start()

    pass_columns(0)
    pass_columns(1)
    pass_columns(2)

    for key in gathers:
        gathers[key].wait_send()

    def sent_back(number, carry):
        return_copy(1 + number // RING, lax.rem(number, RING)).wait_send()
        return carry

    lax.fori_loop(0, (RING - 1) * RING, sent_back, 0)

    def top_copy(slot, i):
        return pltpu.make_async_remote_copy(
            src_ref=top_parts.at[child, slot], dst_ref=top_parts.at[child, slot],
            send_sem=top_send.at[slot * CHILDREN + i], recv_sem=top_recv.at[slot * CHILDREN + i],
            device_id=(lax.rem(child + i, CHILDREN), group), device_id_type=MESH,
        )

    def row_copy(slot, i):
        target = lax.rem(child + i, CHILDREN)
        return pltpu.make_async_remote_copy(
            src_ref=row_chosen.at[slot, target], dst_ref=arrived.at[slot, child],
            send_sem=row_send.at[slot * CHILDREN + i], recv_sem=row_recv.at[slot * CHILDREN + i],
            device_id=(target, group), device_id_type=MESH,
        )

    def own_row_copy(slot):
        return pltpu.make_async_copy(
            row_chosen.at[slot, child], arrived.at[slot, child], own_row_sem.at[slot]
        )

    def select_rows(slot, target):
        for r in range(ROW_SLOTS):
            tile = by_column[slot][table_ref[ROW_PICK + r * CHILDREN + child, target]]
            row_chosen[slot, target, pl.ds(r * NB, NB)] = tile

    def pass_rows(slot):
        def finish(i, carry):
            column_copy(slot, i).wait_recv()
            return carry

        lax.fori_loop(1, GROUPS, finish, 0)
        own_column_copy(slot).wait()
        top_parts[child, slot] = by_column[slot][table_ref[ROW_PICK + child, 0]]

        def send_top(i, carry):
            top_copy(slot, i).start()
            return carry

        lax.fori_loop(1, CHILDREN, send_top, 0)

        def send_rows(i, carry):
            select_rows(slot, lax.rem(child + i, CHILDREN))
            row_copy(slot, i).start()
            return carry

        lax.fori_loop(1, CHILDREN, send_rows, 0)
        select_rows(slot, child)
        own_row_copy(slot).start()

    def finish_top(slot):
        def arrive_top(i, carry):
            top_copy(slot, i).wait_recv()
            return carry

        lax.fori_loop(1, CHILDREN, arrive_top, 0)

    def finish_rows(slot):
        def finish(i, carry):
            row_copy(slot, i).wait_recv()
            return carry

        lax.fori_loop(1, CHILDREN, finish, 0)
        own_row_copy(slot).wait()

    def lead_copy(target):
        return pltpu.make_async_remote_copy(
            src_ref=raw_lead, dst_ref=raw_lead,
            send_sem=lead_send.at[target], recv_sem=lead_recv.at[0],
            device_id=(child, target), device_id_type=MESH,
        )

    def spread_copy(target):
        return pltpu.make_async_remote_copy(
            src_ref=left_panel.at[target], dst_ref=left_panel.at[target],
            send_sem=spread_send.at[target], recv_sem=spread_recv.at[0],
            device_id=(child, target), device_id_type=MESH,
        )

    def own_spread():
        return pltpu.make_async_remote_copy(
            src_ref=left_panel.at[group], dst_ref=left_panel.at[group],
            send_sem=spread_send.at[0], recv_sem=spread_recv.at[0],
            device_id=(child, 0), device_id_type=MESH,
        )

    def share_copy(i):
        return pltpu.make_async_remote_copy(
            src_ref=left_panel.at[group], dst_ref=left_panel.at[group],
            send_sem=share_send.at[i], recv_sem=share_recv.at[i],
            device_id=(child, lax.rem(group + i, GROUPS)), device_id_type=MESH,
        )

    pass_rows(0)
    finish_top(0)
    rows = lax.broadcasted_iota(jnp.int32, (NB, NB), 0)
    cols = lax.broadcasted_iota(jnp.int32, (NB, NB), 1)

    @pl.when(group == 0)
    def _():
        total = lead_block[...] + jnp.where(rows == cols, diag[0:1, :], 0.0)
        for k in range(CHILDREN):
            total = total + jnp.where(table_ref[COL_SLOT + k, 0] >= 0, top_parts[k, 0], 0.0)
        raw_lead[...] = permute_rows(pivots, total)

        def send_lead(i, carry):
            lead_copy(i).start()
            return carry

        lax.fori_loop(1, GROUPS, send_lead, 0)

    pass_rows(1)

    @pl.when(group != 0)
    def _():
        lead_copy(0).wait_recv()

    packed[...] = raw_lead[...]
    factor_tile(packed, lower, upper)
    pass_rows(2)

    finish_rows(0)

    @pl.when(group == 0)
    def _():
        loads = [
            pltpu.make_async_copy(
                arrived.at[0, :, pl.ds(r * NB, NB), :], first_column.at[:, r], load_sem.at[r]
            )
            for r in range(ROW_SLOTS)
        ]
        for load in loads:
            load.start()
        for load in loads:
            load.wait()

        def assemble(i, carry):
            a = lax.rem(i, TR)
            total = jnp.zeros((NB, NB), jnp.float32)
            for k in range(CHILDREN):
                slot = table_ref[ROW_SLOT + k, a * CHILDREN + child]
                held = (slot >= 0) & (table_ref[COL_SLOT + k, 0] >= 0)
                tile = first_column[k, jnp.maximum(slot, 0)]
                total = total + jnp.where(held, tile, 0.0)
            left_panel[a] = total

            @pl.when(a > 0)
            def _():
                spread_copy(a).start()

            return carry

        lax.fori_loop(1, TR + 1, assemble, 0)

    @pl.when(group != 0)
    def _():
        own_spread().wait_recv()

    def send_share(i, carry):
        @pl.when(lax.rem(group + i, GROUPS) != 0)
        def _():
            share_copy(i).start()
        return carry

    lax.fori_loop(1, GROUPS, send_share, 0)
    finish_top(1)
    finish_top(2)

    def finish_share(i, carry):
        @pl.when(lax.rem(group + i, GROUPS) != 0)
        def _():
            share_copy(i).wait_send()

        @pl.when(group != 0)
        def _():
            share_copy(i).wait_recv()

        @pl.when(group == 0)
        def _():
            lead_copy(i).wait_send()
            spread_copy(i).wait_send()

        return carry

    lax.fori_loop(1, GROUPS, finish_share, 0)
    finish_rows(1)
    finish_rows(2)

    for slot in range(COL_SLOTS):
        def sent_columns(i, carry):
            column_copy(slot, i).wait_send()
            return carry

        def sent_rows(i, carry):
            top_copy(slot, i).wait_send()
            row_copy(slot, i).wait_send()
            return carry

        lax.fori_loop(1, GROUPS, sent_columns, 0)
        lax.fori_loop(1, CHILDREN, sent_rows, 0)


def exchange(table, front, left, right, lead_block, diag, pivots):
    tile = jax.ShapeDtypeStruct((NB, NB), jnp.float32)
    dma = pltpu.SemaphoreType.DMA
    return pl.pallas_call(
        exchange_kernel,
        out_shape=(
            jax.ShapeDtypeStruct((COL_SLOTS, CHILDREN, ROW_SLOTS * NB, NB), jnp.float32),
            jax.ShapeDtypeStruct((TR, NB, NB), jnp.float32),
            jax.ShapeDtypeStruct((CHILDREN, COL_SLOTS, NB, NB), jnp.float32),
            tile, tile, tile,
        ),
        in_specs=[SMEM, ANY, ANY, ANY, VMEM, VMEM, VMEM],
        out_specs=(ANY, VMEM, VMEM, VMEM, VMEM, VMEM),
        scratch_shapes=[
            pltpu.VMEM((RING, ROWS, PIV), jnp.float32),
            pltpu.VMEM((RING, PIV, ROWS), jnp.float32),
            pltpu.VMEM((RING, RING, ROWS, ROWS), jnp.float32),
            pltpu.VMEM((RING, RING, ROWS, ROWS), jnp.float32),
            pltpu.VMEM((ROWS, CB), jnp.float32),
            pltpu.VMEM((CBT, ROWS, NB), jnp.float32),
            pltpu.VMEM((COL_SLOTS, GROUPS, 2, NB, NB), jnp.float32),
            pltpu.VMEM((CBT, NB, NB), jnp.float32),
            pltpu.VMEM((CBT, NB, NB), jnp.float32),
            pltpu.VMEM((CBT, NB, NB), jnp.float32),
            pltpu.VMEM((COL_SLOTS, CHILDREN, ROW_SLOTS * NB, NB), jnp.float32),
            pltpu.VMEM((CHILDREN, ROW_SLOTS, NB, NB), jnp.float32),
            pltpu.VMEM((NB, NB), jnp.float32),
            dma((ROW_SLOTS,)), dma((12,)), dma((12,)), dma((16,)), dma((16,)),
            dma((COL_SLOTS * GROUPS,)), dma((COL_SLOTS * GROUPS,)), dma((COL_SLOTS,)),
            dma((COL_SLOTS * CHILDREN,)), dma((COL_SLOTS * CHILDREN,)),
            dma((COL_SLOTS * CHILDREN,)), dma((COL_SLOTS * CHILDREN,)), dma((COL_SLOTS,)),
            dma((GROUPS,)), dma((1,)), dma((GROUPS,)), dma((1,)), dma((GROUPS,)), dma((GROUPS,)),
        ],
        compiler_params=pltpu.CompilerParams(
            collective_id=0, has_side_effects=True, vmem_limit_bytes=60 * 2**20
        ),
        name="exchange",
    )(table, front, left, right, lead_block, diag, pivots)


def split(values):
    high = values.astype(jnp.bfloat16)
    return high, (values - high.astype(jnp.float32)).astype(jnp.bfloat16)


def update_kernel(table_ref, arrived, left_raw, top_parts,
                  packed, lower, upper, diag, pivots, out_ref, right, right_parts, total):
    a = pl.program_id(0)
    child = lax.axis_index("child")
    group = lax.axis_index("grp")
    rows = lax.broadcasted_iota(jnp.int32, (NB, NB), 0)
    cols = lax.broadcasted_iota(jnp.int32, (NB, NB), 1)

    @pl.when(a == 0)
    def _():
        right[...] = jnp.zeros_like(right)
        for k in range(CHILDREN):
            for b in range(TC):
                slot = table_ref[COL_SLOT + k, b * GROUPS + group]

                @pl.when((slot >= 0) & (table_ref[COL_SLOT + k, 0] >= 0))
                def _():
                    span = pl.ds(b * NB, NB)
                    right[:, span] = right[:, span] + top_parts[k, slot]

        right[...] = full_dot(lower[...], permute_rows(pivots, right[...]))

        @pl.when(group == 0)
        def _():
            right[:, :NB] = jnp.zeros((NB, NB), jnp.float32)

        high, low = split(right[...])
        right_parts[0:NB] = high
        right_parts[NB:2 * NB] = low
        right_parts[2 * NB:] = high

    top = (a == 0) & (child == 0)

    @pl.when(top)
    def _():
        total[...] = right[...]

        @pl.when(group == 0)
        def _():
            total[:, :NB] = packed[...]

    @pl.when(jnp.logical_not(top))
    def _():
        left = full_dot(left_raw[0], upper[...])
        high, low = split(left)
        left_parts = jnp.concatenate([high, high, low], axis=1)
        total[...] = -jnp.dot(
            left_parts, right_parts[...], preferred_element_type=jnp.float32
        )
        for k in range(CHILDREN):
            row_slot = table_ref[ROW_SLOT + k, a * CHILDREN + child]

            @pl.when(row_slot >= 0)
            def _():
                base = pl.multiple_of(row_slot * NB, NB)
                for b in range(TC):
                    col_slot = table_ref[COL_SLOT + k, b * GROUPS + group]

                    @pl.when(col_slot >= 0)
                    def _():
                        span = pl.ds(b * NB, NB)
                        total[:, span] = total[:, span] + arrived[col_slot, k, pl.ds(base, NB), :]

        on_diag = (lax.rem(group, CHILDREN) == child) & (lax.rem(a, 2) == group // CHILDREN)

        @pl.when(on_diag)
        def _():
            span = pl.ds(pl.multiple_of((a // 2) * NB, NB), NB)
            entries = diag[pl.ds(a * CHILDREN + child, 1), :]
            total[:, span] = total[:, span] + jnp.where(rows == cols, entries, 0.0)

        @pl.when(group == 0)
        def _():
            total[:, :NB] = left

    out_ref[0, :, 0, :] = total[...]


def update_front(table, arrived, left_raw, top_parts,
                 packed, lower, upper, diag, pivots):
    return pl.pallas_call(
        update_kernel,
        grid=(TR,),
        out_shape=jax.ShapeDtypeStruct((1, TR * NB, 1, TC * NB), jnp.float32),
        in_specs=[
            SMEM, VMEM,
            pl.BlockSpec((1, NB, NB), lambda a: (a, 0, 0)),
            VMEM, VMEM, VMEM, VMEM, VMEM, VMEM,
        ],
        out_specs=pl.BlockSpec((1, NB, 1, TC * NB), lambda a: (0, a, 0, 0)),
        scratch_shapes=[
            pltpu.VMEM((NB, TC * NB), jnp.float32),
            pltpu.VMEM((3 * NB, TC * NB), jnp.bfloat16),
            pltpu.VMEM((NB, TC * NB), jnp.float32),
        ],
        compiler_params=pltpu.CompilerParams(vmem_limit_bytes=60 * 2**20),
        name="update_front",
    )(table, arrived, left_raw, top_parts,
      packed, lower, upper, diag, pivots)


def body(front_child, left_factor, right_factor, child_map, parent_diag, lead_block, pivots):
    diag = parent_diag.reshape(PT, NB)
    pivot_row = pivots.reshape(1, NB)
    table = slot_table(child_map)
    arrived, left_raw, top_parts, packed, lower, upper = exchange(
        table, front_child[0], left_factor[0], right_factor[0], lead_block, diag, pivot_row
    )
    return update_front(
        table, arrived, left_raw, top_parts, packed, lower, upper, diag, pivot_row
    )


def solution(mesh):
    in_specs = (
        P("child", "grp", None),
        P("child", "grp", None),
        P("child", None, "grp"),
        P(),
        P(),
        P(),
        P(),
    )
    out_specs = P("child", None, "grp", None)
    return jax.shard_map(body, mesh=mesh, in_specs=in_specs, out_specs=out_specs, check_vma=False)
```

```python
import jax
import jax.numpy as jnp
from jax import lax
from jax.experimental import pallas as pl
from jax.experimental.pallas import tpu as pltpu
from jax.sharding import PartitionSpec as P

NB = 128
CB = 4096
PIV = 1280
NP = 16384
CHILDREN = 8
GROUPS = 16
RING = 4
CBT = CB // NB
PT = NP // NB
TR = PT // CHILDREN
TC = PT // GROUPS
COL_SLOTS = 3
ROW_SLOTS = 6
PARTS = 2
PART = NB // PARTS
CHUNKS = COL_SLOTS * PARTS
STEP = 4
ROWS = CB // GROUPS
COL_SLOT = 0
ROW_SLOT = CHILDREN
COL_PICK = 2 * CHILDREN
ROW_PICK = COL_PICK + COL_SLOTS * CHILDREN
TABLE_ROWS = ROW_PICK + ROW_SLOTS * CHILDREN
MESH = pl.DeviceIdType.MESH
ANY = pl.BlockSpec(memory_space=pl.ANY)
VMEM = pl.BlockSpec(memory_space=pltpu.VMEM)
SMEM = pl.BlockSpec(memory_space=pltpu.SMEM)


def full_dot(a, b):
    return jnp.dot(a, b, precision=lax.Precision.HIGHEST, preferred_element_type=jnp.float32)


def table_kernel(map_ref, table_ref):
    lanes = lax.broadcasted_iota(jnp.int32, (CHILDREN, PT), 1)
    tiles = map_ref[...]
    source = jnp.full((CHILDREN, PT), -1, jnp.int32)
    for t in range(CBT):
        source = jnp.where(tiles[:, t:t + 1] == lanes, t, source)
    held = (source >= 0).astype(jnp.int32)

    def fill(classes, capacity, slot_base, pick_base):
        rank = jnp.zeros((CHILDREN, PT), jnp.int32)
        for shift in range(classes, PT, classes):
            rank = rank + jnp.where(lanes >= shift, pltpu.roll(held, shift, 1), 0)
        slots = jnp.where(held > 0, rank, -1)
        table_ref[slot_base:slot_base + CHILDREN] = slots
        for slot in range(capacity):
            picked = jnp.where(slots == slot, source, 0)
            shift = classes
            while shift < PT:
                picked = picked + pltpu.roll(picked, shift, 1)
                shift *= 2
            base = pick_base + slot * CHILDREN
            table_ref[base:base + CHILDREN] = picked

    fill(GROUPS, COL_SLOTS, COL_SLOT, COL_PICK)
    fill(CHILDREN, ROW_SLOTS, ROW_SLOT, ROW_PICK)


def slot_table(child_map):
    return pl.pallas_call(
        table_kernel,
        out_shape=jax.ShapeDtypeStruct((TABLE_ROWS, PT), jnp.int32),
        name="slot_table",
    )(child_map)


def permute_rows(pivots, values):
    rows = lax.broadcasted_iota(jnp.int32, (NB, NB), 0)
    chosen = jnp.where(rows == pivots[...], 1.0, 0.0)
    return lax.dot_general(
        chosen, values, (((0,), (0,)), ((), ())),
        precision=lax.Precision.HIGHEST, preferred_element_type=jnp.float32,
    )


def factor_tile(packed_ref, lower_ref, upper_ref):
    rows = lax.broadcasted_iota(jnp.int32, (NB, NB), 0)
    cols = lax.broadcasted_iota(jnp.int32, (NB, NB), 1)
    lane = lax.broadcasted_iota(jnp.int32, (1, NB), 1)
    eye = jnp.where(rows == cols, 1.0, 0.0)
    lower_ref[...] = eye
    upper_ref[...] = eye

    def eliminate(j, carry):
        working = packed_ref[...]
        upper = upper_ref[...]
        row_part = packed_ref[pl.ds(j, 1), :]
        row_lower = lower_ref[pl.ds(j, 1), :]
        column = jnp.sum(jnp.where(cols == j, working, 0.0), axis=1, keepdims=True)
        column_upper = jnp.sum(jnp.where(cols == j, upper, 0.0), axis=1, keepdims=True)
        pivot_value = jnp.sum(jnp.where(lane == j, row_part, 0.0), axis=1, keepdims=True)
        multiplier = jnp.where(rows[:, :1] > j, column / pivot_value, 0.0)
        right = jnp.where(lane > j, row_part, 0.0)
        packed_ref[...] = jnp.where(
            (cols == j) & (rows > j), multiplier, working - multiplier * right
        )
        lower_ref[...] = lower_ref[...] - multiplier * row_lower
        scaled = column_upper / pivot_value
        upper_ref[...] = jnp.where(cols == j, scaled, upper - scaled * right)
        return carry

    lax.fori_loop(0, NB, eliminate, 0)


def exchange_kernel(table_ref, front_hbm, left_hbm, right_hbm, lead_block, diag, pivots,
                    arrived, left_panel, right_panel, packed, lower, upper,
                    lefts, rights, products, returned, front, contribution, col_chosen,
                    column_0, column_1, column_2, column_3, column_4, column_5,
                    row_chosen, first_column, raw_lead, lead_parts,
                    top_own, top_peer, top_sum, top_got,
                    load_sem, ring_send, ring_recv, back_send, back_recv, col_send, col_recv, own_col_sem,
                    row_send, row_recv, own_row_sem,
                    lead_part_send, lead_part_recv, lead_cast_send, lead_cast_recv, lead_send, lead_recv,
                    spread_send, spread_recv, share_send, share_recv,
                    peer_send, peer_recv, reduce_send, reduce_recv, top_send, top_recv):
    by_column = (column_0, column_1, column_2, column_3, column_4, column_5)
    child = lax.axis_index("child")
    group = lax.axis_index("grp")
    core = lax.rem(child, 2)
    at_y, at_x = group // RING, lax.rem(group, RING)
    along = jnp.where(core == 0, at_x, at_y)
    across = jnp.where(core == 0, at_y, at_x)

    load_right = pltpu.make_async_copy(right_hbm, rights.at[across], load_sem.at[0])
    load_left = pltpu.make_async_copy(left_hbm, lefts.at[along], load_sem.at[1])
    load_front = pltpu.make_async_copy(front_hbm, front, load_sem.at[2])
    load_right.start()
    load_left.start()
    load_front.start()

    barrier = pltpu.get_barrier_semaphore()

    def greet_group(i, carry):
        pl.semaphore_signal(
            barrier, inc=1, device_id=(child, lax.rem(group + i, GROUPS)), device_id_type=MESH
        )
        return carry

    def greet_child(i, carry):
        pl.semaphore_signal(
            barrier, inc=1, device_id=(lax.rem(child + i, CHILDREN), group), device_id_type=MESH
        )
        return carry

    lax.fori_loop(1, GROUPS, greet_group, 0)
    lax.fori_loop(1, CHILDREN, greet_child, 0)
    pl.semaphore_wait(barrier, GROUPS + CHILDREN - 2)

    def turn(position, by):
        return lax.rem(position + by + RING, RING)

    def place(u, v):
        return jnp.where(core == 0, v * RING + u, u * RING + v)

    gathers = {}

    def make(key, blocks, block, chunk, target):
        number = len(gathers)
        size = blocks.shape[1] // 2
        ref = blocks.at[block, pl.ds(chunk * size, size)]
        gathers[key] = pltpu.make_async_remote_copy(
            src_ref=ref, dst_ref=ref, send_sem=ring_send.at[number], recv_sem=ring_recv.at[number],
            device_id=(child, target), device_id_type=MESH,
        )

    for name, blocks, at in (("l", lefts, along), ("r", rights, across)):
        for way in (1, -1):
            target = place(turn(along, way), across) if name == "l" else place(along, turn(across, way))
            first = 0 if way == 1 else 1
            make((name, way, 0), blocks, at, first, target)
            make((name, way, 1), blocks, at, 1 - first, target)
            make((name, way, 2), blocks, turn(at, -way), first, target)

    def start(name, step):
        gathers[(name, 1, step)].start()
        gathers[(name, -1, step)].start()

    def arrive(name, step):
        gathers[(name, 1, step)].wait_recv()
        gathers[(name, -1, step)].wait_recv()

    def return_copy(to, piece):
        target = turn(along, to)
        number = to * RING + piece
        return pltpu.make_async_remote_copy(
            src_ref=products.at[target, piece], dst_ref=returned.at[along, piece],
            send_sem=back_send.at[number], recv_sem=back_recv.at[number],
            device_id=(child, place(target, across)), device_id_type=MESH,
        )

    def multiply(pairs):
        def one(i, carry):
            to, line = jnp.int32(0), jnp.int32(0)
            for number, (pair_to, pair_line) in enumerate(pairs):
                to = jnp.where(i == number, pair_to, to)
                line = jnp.where(i == number, pair_line, line)
            target, piece = turn(along, to), turn(across, line)
            product = full_dot(lefts[target], rights[piece])

            @pl.when(to == 0)
            def _():
                returned[along, piece] = product

            @pl.when(to != 0)
            def _():
                products[target, piece] = product
                return_copy(to, piece).start()

            return carry

        lax.fori_loop(0, len(pairs), one, 0)

    load_left.wait()
    start("l", 0)
    load_right.wait()
    start("r", 0)
    start("l", 1)
    start("r", 1)
    multiply([(0, 0)])
    arrive("l", 0)
    start("l", 2)
    arrive("r", 0)
    start("r", 2)
    arrive("l", 1)
    multiply([(1, 0), (3, 0)])
    arrive("r", 1)
    multiply([(1, 1), (3, 1), (1, 3), (3, 3), (0, 1), (0, 3)])
    arrive("l", 2)
    multiply([(2, 0), (2, 1), (2, 3)])
    arrive("r", 2)
    multiply([(2, 2), (1, 2), (3, 2), (0, 2)])
    load_front.wait()

    def subtract(source, piece):
        block = place(source, piece)
        base = pl.multiple_of(block * ROWS, ROWS)
        result = front[:, pl.ds(base, ROWS)] - returned[source, piece]
        contribution[2 * block] = result[:, :NB].reshape(2, PARTS, PART, NB)
        contribution[2 * block + 1] = result[:, NB:].reshape(2, PARTS, PART, NB)

    def subtract_own(piece, carry):
        subtract(along, piece)
        return carry

    lax.fori_loop(0, RING, subtract_own, 0)

    def subtract_returned(number, carry):
        to, line = 1 + number // RING, turn(across, lax.rem(number, RING))
        return_copy(to, line).wait_recv()
        subtract(turn(along, -to), line)
        return carry

    lax.fori_loop(0, (RING - 1) * RING, subtract_returned, 0)

    def column_copy(chunk, i):
        target = lax.rem(group + i, GROUPS)
        return pltpu.make_async_remote_copy(
            src_ref=col_chosen.at[chunk, target],
            dst_ref=by_column[chunk].at[pl.ds(2 * group, 2)],
            send_sem=col_send.at[chunk * GROUPS + i], recv_sem=col_recv.at[chunk * GROUPS + i],
            device_id=(child, target), device_id_type=MESH,
        )

    def own_column_copy(chunk):
        return pltpu.make_async_copy(
            col_chosen.at[chunk, group], by_column[chunk].at[pl.ds(2 * group, 2)],
            own_col_sem.at[chunk],
        )

    def select_column(chunk, target):
        slot, part = chunk // PARTS, chunk % PARTS
        picked = table_ref[COL_PICK + slot * CHILDREN + child, target]
        for row in range(2):
            col_chosen[chunk, target, row] = contribution[picked, row, part]

    def pass_columns(chunk):
        def send_column(i, carry):
            select_column(chunk, lax.rem(group + i, GROUPS))
            column_copy(chunk, i).start()
            return carry

        lax.fori_loop(1, GROUPS, send_column, 0)
        select_column(chunk, group)
        own_column_copy(chunk).start()

    for chunk in range(CHUNKS):
        pass_columns(chunk)

    for key in gathers:
        gathers[key].wait_send()

    def sent_back(number, carry):
        return_copy(1 + number // RING, lax.rem(number, RING)).wait_send()
        return carry

    lax.fori_loop(0, (RING - 1) * RING, sent_back, 0)

    def row_copy(chunk, i):
        target = lax.rem(child + i, CHILDREN)
        return pltpu.make_async_remote_copy(
            src_ref=row_chosen.at[chunk, target], dst_ref=arrived.at[chunk, child],
            send_sem=row_send.at[chunk * CHILDREN + i], recv_sem=row_recv.at[chunk * CHILDREN + i],
            device_id=(target, group), device_id_type=MESH,
        )

    def own_row_copy(chunk):
        return pltpu.make_async_copy(
            row_chosen.at[chunk, child], arrived.at[chunk, child], own_row_sem.at[chunk]
        )

    def select_rows(chunk, target):
        for r in range(ROW_SLOTS):
            tile = by_column[chunk][table_ref[ROW_PICK + r * CHILDREN + child, target]]
            row_chosen[chunk, target, pl.ds(r * PART, PART)] = tile

    def pass_rows(chunk):
        def finish(i, carry):
            column_copy(chunk, i).wait_recv()
            return carry

        lax.fori_loop(1, GROUPS, finish, 0)
        own_column_copy(chunk).wait()

        def send_rows(i, carry):
            select_rows(chunk, lax.rem(child + i, CHILDREN))
            row_copy(chunk, i).start()
            return carry

        lax.fori_loop(1, CHILDREN, send_rows, 0)
        select_rows(chunk, child)
        own_row_copy(chunk).start()

    def finish_rows(chunk):
        def finish(i, carry):
            row_copy(chunk, i).wait_recv()
            return carry

        lax.fori_loop(1, CHILDREN, finish, 0)
        own_row_copy(chunk).wait()

    def top_tile(chunk):
        return by_column[chunk][table_ref[ROW_PICK + child, 0]]

    lead_here = table_ref[COL_SLOT + child, 0] >= 0

    def lead_part_copy(source):
        return pltpu.make_async_remote_copy(
            src_ref=lead_parts.at[source], dst_ref=lead_parts.at[source],
            send_sem=lead_part_send.at[0], recv_sem=lead_part_recv.at[source],
            device_id=(0, group), device_id_type=MESH,
        )

    def lead_cast_copy(target):
        return pltpu.make_async_remote_copy(
            src_ref=raw_lead, dst_ref=raw_lead,
            send_sem=lead_cast_send.at[target], recv_sem=lead_cast_recv.at[0],
            device_id=(target, group), device_id_type=MESH,
        )

    def lead_copy(target):
        return pltpu.make_async_remote_copy(
            src_ref=raw_lead, dst_ref=raw_lead,
            send_sem=lead_send.at[target], recv_sem=lead_recv.at[0],
            device_id=(child, target), device_id_type=MESH,
        )

    def send_lead_part():
        for part in range(PARTS):
            tile = jnp.where(lead_here, top_tile(part), 0.0)
            lead_parts[child, pl.ds(part * PART, PART)] = tile

        @pl.when(child != 0)
        def _():
            lead_part_copy(child).start()

    def sum_lead():
        def arrive_part(k, carry):
            lead_part_copy(k).wait_recv()
            return carry

        lax.fori_loop(1, CHILDREN, arrive_part, 0)
        rows = lax.broadcasted_iota(jnp.int32, (NB, NB), 0)
        cols = lax.broadcasted_iota(jnp.int32, (NB, NB), 1)
        total = lead_block[...] + jnp.where(rows == cols, diag[0:1, :], 0.0)
        for k in range(CHILDREN):
            total = total + lead_parts[k]
        raw_lead[...] = permute_rows(pivots, total)

        def cast(k, carry):
            lead_cast_copy(k).start()
            return carry

        lax.fori_loop(1, CHILDREN, cast, 0)

    def pass_lead():
        @pl.when(child != 0)
        def _():
            lead_cast_copy(0).wait_recv()

        def send_lead(i, carry):
            lead_copy(i).start()
            return carry

        lax.fori_loop(1, GROUPS, send_lead, 0)

    def spread_copy(target):
        return pltpu.make_async_remote_copy(
            src_ref=left_panel.at[target], dst_ref=left_panel.at[target],
            send_sem=spread_send.at[target], recv_sem=spread_recv.at[0],
            device_id=(child, target), device_id_type=MESH,
        )

    def own_spread():
        return pltpu.make_async_remote_copy(
            src_ref=left_panel.at[group], dst_ref=left_panel.at[group],
            send_sem=spread_send.at[0], recv_sem=spread_recv.at[0],
            device_id=(child, 0), device_id_type=MESH,
        )

    def share_copy(i):
        return pltpu.make_async_remote_copy(
            src_ref=left_panel.at[group], dst_ref=left_panel.at[group],
            send_sem=share_send.at[i], recv_sem=share_recv.at[i],
            device_id=(child, lax.rem(group + i, GROUPS)), device_id_type=MESH,
        )

    at_z = child // 2
    partner = child + 1 - 2 * core

    def peer_copy():
        return pltpu.make_async_remote_copy(
            src_ref=top_own.at[1 - core], dst_ref=top_peer,
            send_sem=peer_send.at[0], recv_sem=peer_recv.at[0],
            device_id=(partner, group), device_id_type=MESH,
        )

    def reduce_copy(i):
        target = turn(at_z, i)
        return pltpu.make_async_remote_copy(
            src_ref=top_sum.at[target], dst_ref=top_got.at[at_z],
            send_sem=reduce_send.at[i], recv_sem=reduce_recv.at[i],
            device_id=(2 * target + core, group), device_id_type=MESH,
        )

    def top_share_copy(i):
        target = turn(at_z, i)
        return pltpu.make_async_remote_copy(
            src_ref=right_panel.at[core, at_z], dst_ref=right_panel.at[core, at_z],
            send_sem=top_send.at[i], recv_sem=top_recv.at[i],
            device_id=(2 * target + core, group), device_id_type=MESH,
        )

    def peer_share_copy():
        return pltpu.make_async_remote_copy(
            src_ref=right_panel.at[core], dst_ref=right_panel.at[core],
            send_sem=peer_send.at[1], recv_sem=peer_recv.at[1],
            device_id=(partner, group), device_id_type=MESH,
        )

    pass_rows(0)
    pass_rows(1)

    @pl.when(group == 0)
    def _():
        send_lead_part()

    pass_rows(2)

    @pl.when((group == 0) & (child == 0))
    def _():
        sum_lead()

    pass_rows(3)

    @pl.when(group == 0)
    def _():
        pass_lead()

    @pl.when(group != 0)
    def _():
        lead_copy(0).wait_recv()

    packed[...] = raw_lead[...]
    factor_tile(packed, lower, upper)
    pass_rows(4)
    pass_rows(5)

    for b in range(TC):
        held = table_ref[COL_SLOT + child, b * GROUPS + group]
        for part in range(PARTS):
            total = jnp.zeros((PART, NB), jnp.float32)
            for slot in range(COL_SLOTS):
                tile = top_tile(slot * PARTS + part)
                total = jnp.where(lead_here & (held == slot), tile, total)
            top_own[b % 2, b // 2, part * PART:(part + 1) * PART] = total
    peer_copy().start()

    for part in range(PARTS):
        finish_rows(part)

    @pl.when(group == 0)
    def _():
        loads = [
            pltpu.make_async_copy(
                arrived.at[part, :, pl.ds(r * PART, PART), :], first_column.at[part, :, r],
                load_sem.at[part * ROW_SLOTS + r],
            )
            for part in range(PARTS) for r in range(ROW_SLOTS)
        ]
        for load in loads:
            load.start()
        for load in loads:
            load.wait()

        def assemble(i, carry):
            a = lax.rem(i, TR)
            for part in range(PARTS):
                total = jnp.zeros((PART, NB), jnp.float32)
                for k in range(CHILDREN):
                    slot = table_ref[ROW_SLOT + k, a * CHILDREN + child]
                    held = (slot >= 0) & (table_ref[COL_SLOT + k, 0] >= 0)
                    tile = first_column[part, k, jnp.maximum(slot, 0)]
                    total = total + jnp.where(held, tile, 0.0)
                left_panel[a, part * PART:(part + 1) * PART] = total

            @pl.when(a > 0)
            def _():
                spread_copy(a).start()

            return carry

        lax.fori_loop(1, TR + 1, assemble, 0)

    peer_copy().wait_recv()
    top_sum[...] = top_own[core] + top_peer[...]
    for i in range(1, RING):
        reduce_copy(i).start()

    @pl.when(group != 0)
    def _():
        own_spread().wait_recv()

    def send_share(i, carry):
        @pl.when(lax.rem(group + i, GROUPS) != 0)
        def _():
            share_copy(i).start()
        return carry

    lax.fori_loop(1, GROUPS, send_share, 0)

    for i in range(1, RING):
        reduce_copy(i).wait_recv()
    right_panel[core, at_z] = (
        top_sum[at_z] + top_got[turn(at_z, 1)] + top_got[turn(at_z, 2)] + top_got[turn(at_z, 3)]
    )
    for i in range(1, RING):
        top_share_copy(i).start()
    for i in range(1, RING):
        top_share_copy(i).wait_recv()
    peer_share_copy().start()

    def finish_share(i, carry):
        @pl.when(lax.rem(group + i, GROUPS) != 0)
        def _():
            share_copy(i).wait_send()

        @pl.when(group != 0)
        def _():
            share_copy(i).wait_recv()

        @pl.when(group == 0)
        def _():
            lead_copy(i).wait_send()
            spread_copy(i).wait_send()

        return carry

    lax.fori_loop(1, GROUPS, finish_share, 0)

    @pl.when((group == 0) & (child == 0))
    def _():
        def sent_cast(k, carry):
            lead_cast_copy(k).wait_send()
            return carry

        lax.fori_loop(1, CHILDREN, sent_cast, 0)

    @pl.when((group == 0) & (child != 0))
    def _():
        lead_part_copy(child).wait_send()

    peer_copy().wait_send()
    for i in range(1, RING):
        reduce_copy(i).wait_send()
        top_share_copy(i).wait_send()

    for chunk in range(CHUNKS):
        def sent_columns(i, carry):
            column_copy(chunk, i).wait_send()
            return carry

        lax.fori_loop(1, GROUPS, sent_columns, 0)

    for chunk in range(PARTS, CHUNKS):
        finish_rows(chunk)
    peer_share_copy().wait()

    for chunk in range(CHUNKS):
        def sent_rows(i, carry):
            row_copy(chunk, i).wait_send()
            return carry

        lax.fori_loop(1, CHILDREN, sent_rows, 0)


def exchange(table, front, left, right, lead_block, diag, pivots):
    tile = jax.ShapeDtypeStruct((NB, NB), jnp.float32)
    dma = pltpu.SemaphoreType.DMA
    return pl.pallas_call(
        exchange_kernel,
        out_shape=(
            jax.ShapeDtypeStruct((CHUNKS, CHILDREN, ROW_SLOTS * PART, NB), jnp.float32),
            jax.ShapeDtypeStruct((TR, NB, NB), jnp.float32),
            jax.ShapeDtypeStruct((2, RING, NB, NB), jnp.float32),
            tile, tile, tile,
        ),
        in_specs=[SMEM, ANY, ANY, ANY, VMEM, VMEM, VMEM],
        out_specs=(ANY, VMEM, VMEM, VMEM, VMEM, VMEM),
        scratch_shapes=[
            pltpu.VMEM((RING, ROWS, PIV), jnp.float32),
            pltpu.VMEM((RING, PIV, ROWS), jnp.float32),
            pltpu.VMEM((RING, RING, ROWS, ROWS), jnp.float32),
            pltpu.VMEM((RING, RING, ROWS, ROWS), jnp.float32),
            pltpu.VMEM((ROWS, CB), jnp.float32),
            pltpu.VMEM((CBT, 2, PARTS, PART, NB), jnp.float32),
            pltpu.VMEM((CHUNKS, GROUPS, 2, PART, NB), jnp.float32),
            pltpu.VMEM((CBT, PART, NB), jnp.float32),
            pltpu.VMEM((CBT, PART, NB), jnp.float32),
            pltpu.VMEM((CBT, PART, NB), jnp.float32),
            pltpu.VMEM((CBT, PART, NB), jnp.float32),
            pltpu.VMEM((CBT, PART, NB), jnp.float32),
            pltpu.VMEM((CBT, PART, NB), jnp.float32),
            pltpu.VMEM((CHUNKS, CHILDREN, ROW_SLOTS * PART, NB), jnp.float32),
            pltpu.VMEM((PARTS, CHILDREN, ROW_SLOTS, PART, NB), jnp.float32),
            pltpu.VMEM((NB, NB), jnp.float32),
            pltpu.VMEM((CHILDREN, NB, NB), jnp.float32),
            pltpu.VMEM((2, RING, NB, NB), jnp.float32),
            pltpu.VMEM((RING, NB, NB), jnp.float32),
            pltpu.VMEM((RING, NB, NB), jnp.float32),
            pltpu.VMEM((RING, NB, NB), jnp.float32),
            dma((PARTS * ROW_SLOTS,)), dma((12,)), dma((12,)), dma((16,)), dma((16,)),
            dma((CHUNKS * GROUPS,)), dma((CHUNKS * GROUPS,)), dma((CHUNKS,)),
            dma((CHUNKS * CHILDREN,)), dma((CHUNKS * CHILDREN,)), dma((CHUNKS,)),
            dma((1,)), dma((CHILDREN,)), dma((CHILDREN,)), dma((1,)), dma((GROUPS,)), dma((1,)),
            dma((GROUPS,)), dma((1,)), dma((GROUPS,)), dma((GROUPS,)),
            dma((2,)), dma((2,)), dma((RING,)), dma((RING,)), dma((RING,)), dma((RING,)),
        ],
        compiler_params=pltpu.CompilerParams(
            collective_id=0, has_side_effects=True, vmem_limit_bytes=60 * 2**20
        ),
        name="exchange",
    )(table, front, left, right, lead_block, diag, pivots)


def split(values):
    high = values.astype(jnp.bfloat16)
    return high, (values - high.astype(jnp.float32)).astype(jnp.bfloat16)


def update_kernel(table_ref, arrived, left_raw, right_panel,
                  packed, lower, upper, diag, pivots, out_ref, right, right_parts, total):
    step = pl.program_id(0)
    child = lax.axis_index("child")
    group = lax.axis_index("grp")
    rows = lax.broadcasted_iota(jnp.int32, (NB, NB), 0)
    cols = lax.broadcasted_iota(jnp.int32, (NB, NB), 1)

    @pl.when(step == 0)
    def _():
        for b in range(TC):
            right[:, b * NB:(b + 1) * NB] = right_panel[b % 2, b // 2]
        right[...] = full_dot(lower[...], permute_rows(pivots, right[...]))

        @pl.when(group == 0)
        def _():
            right[:, :NB] = jnp.zeros((NB, NB), jnp.float32)

        high, low = split(right[...])
        right_parts[0:NB] = high
        right_parts[NB:2 * NB] = low
        right_parts[2 * NB:] = high

    left = full_dot(left_raw[...].reshape(STEP * NB, NB), upper[...])
    high, low = split(left)
    left_parts = jnp.concatenate([high, high, low], axis=1)
    total[...] = -jnp.dot(left_parts, right_parts[...], preferred_element_type=jnp.float32)

    def place(row, carry):
        a = step * STEP + row
        for k in range(CHILDREN):
            row_slot = table_ref[ROW_SLOT + k, a * CHILDREN + child]

            @pl.when(row_slot >= 0)
            def _():
                base = pl.multiple_of(row_slot * PART, PART)
                for b in range(TC):
                    col_slot = table_ref[COL_SLOT + k, b * GROUPS + group]

                    @pl.when(col_slot >= 0)
                    def _():
                        across = pl.ds(b * NB, NB)
                        for part in range(PARTS):
                            down = pl.ds(pl.multiple_of(row * NB, NB) + part * PART, PART)
                            tile = arrived[col_slot * PARTS + part, k, pl.ds(base, PART), :]
                            total[down, across] = total[down, across] + tile

        on_diag = (lax.rem(group, CHILDREN) == child) & (lax.rem(a, 2) == group // CHILDREN)

        @pl.when(on_diag)
        def _():
            across = pl.ds(pl.multiple_of((a // 2) * NB, NB), NB)
            down = pl.ds(pl.multiple_of(row * NB, NB), NB)
            entries = diag[pl.ds(a * CHILDREN + child, 1), :]
            total[down, across] = total[down, across] + jnp.where(rows == cols, entries, 0.0)

        return carry

    lax.fori_loop(0, STEP, place, 0)

    @pl.when(group == 0)
    def _():
        total[:, :NB] = left

    @pl.when((step == 0) & (child == 0))
    def _():
        total[:NB, :] = right[...]

        @pl.when(group == 0)
        def _():
            total[:NB, :NB] = packed[...]

    out_ref[0, :, 0, :] = total[...]


def update_front(table, arrived, left_raw, right_panel, packed, lower, upper, diag, pivots):
    return pl.pallas_call(
        update_kernel,
        grid=(TR // STEP,),
        out_shape=jax.ShapeDtypeStruct((1, TR * NB, 1, TC * NB), jnp.float32),
        in_specs=[
            SMEM, VMEM,
            pl.BlockSpec((STEP, NB, NB), lambda a: (a, 0, 0)),
            VMEM, VMEM, VMEM, VMEM, VMEM, VMEM,
        ],
        out_specs=pl.BlockSpec((1, STEP * NB, 1, TC * NB), lambda a: (0, a, 0, 0)),
        scratch_shapes=[
            pltpu.VMEM((NB, TC * NB), jnp.float32),
            pltpu.VMEM((3 * NB, TC * NB), jnp.bfloat16),
            pltpu.VMEM((STEP * NB, TC * NB), jnp.float32),
        ],
        compiler_params=pltpu.CompilerParams(vmem_limit_bytes=60 * 2**20),
        name="update_front",
    )(table, arrived, left_raw, right_panel, packed, lower, upper, diag, pivots)


def body(front_child, left_factor, right_factor, child_map, parent_diag, lead_block, pivots):
    diag = parent_diag.reshape(PT, NB)
    pivot_row = pivots.reshape(1, NB)
    table = slot_table(child_map)
    arrived, left_raw, right_panel, packed, lower, upper = exchange(
        table, front_child[0], left_factor[0], right_factor[0], lead_block, diag, pivot_row
    )
    return update_front(
        table, arrived, left_raw, right_panel, packed, lower, upper, diag, pivot_row
    )


def solution(mesh):
    in_specs = (
        P("child", "grp", None),
        P("child", "grp", None),
        P("child", None, "grp"),
        P(),
        P(),
        P(),
        P(),
    )
    out_specs = P("child", None, "grp", None)
    return jax.shard_map(body, mesh=mesh, in_specs=in_specs, out_specs=out_specs, check_vma=False)
```

```python
import jax
import jax.numpy as jnp
from jax import lax
from jax.experimental import pallas as pl
from jax.experimental.pallas import tpu as pltpu
from jax.sharding import PartitionSpec as P

NB = 128
CB = 4096
PIV = 1280
NP = 16384
CHILDREN = 8
GROUPS = 16
RING = 4
CBT = CB // NB
PT = NP // NB
TR = PT // CHILDREN
TC = PT // GROUPS
COL_SLOTS = 3
ROW_SLOTS = 6
PARTS = 2
PART = NB // PARTS
CHUNKS = COL_SLOTS * PARTS
STEP = 4
ROWS = CB // GROUPS
COL_SLOT = 0
ROW_SLOT = CHILDREN
COL_PICK = 2 * CHILDREN
ROW_PICK = COL_PICK + COL_SLOTS * CHILDREN
TABLE_ROWS = ROW_PICK + ROW_SLOTS * CHILDREN
MESH = pl.DeviceIdType.MESH
ANY = pl.BlockSpec(memory_space=pl.ANY)
VMEM = pl.BlockSpec(memory_space=pltpu.VMEM)
SMEM = pl.BlockSpec(memory_space=pltpu.SMEM)


def full_dot(a, b):
    return jnp.dot(a, b, precision=lax.Precision.HIGHEST, preferred_element_type=jnp.float32)


def table_kernel(map_ref, table_ref):
    lanes = lax.broadcasted_iota(jnp.int32, (CHILDREN, PT), 1)
    tiles = map_ref[...]
    source = jnp.full((CHILDREN, PT), -1, jnp.int32)
    for t in range(CBT):
        source = jnp.where(tiles[:, t:t + 1] == lanes, t, source)
    held = (source >= 0).astype(jnp.int32)

    def fill(classes, capacity, slot_base, pick_base):
        rank = jnp.zeros((CHILDREN, PT), jnp.int32)
        for shift in range(classes, PT, classes):
            rank = rank + jnp.where(lanes >= shift, pltpu.roll(held, shift, 1), 0)
        slots = jnp.where(held > 0, rank, -1)
        table_ref[slot_base:slot_base + CHILDREN] = slots
        for slot in range(capacity):
            picked = jnp.where(slots == slot, source, 0)
            shift = classes
            while shift < PT:
                picked = picked + pltpu.roll(picked, shift, 1)
                shift *= 2
            base = pick_base + slot * CHILDREN
            table_ref[base:base + CHILDREN] = picked

    fill(GROUPS, COL_SLOTS, COL_SLOT, COL_PICK)
    fill(CHILDREN, ROW_SLOTS, ROW_SLOT, ROW_PICK)


def slot_table(child_map):
    return pl.pallas_call(
        table_kernel,
        out_shape=jax.ShapeDtypeStruct((TABLE_ROWS, PT), jnp.int32),
        name="slot_table",
    )(child_map)


def permute_rows(pivots, values):
    rows = lax.broadcasted_iota(jnp.int32, (NB, NB), 0)
    chosen = jnp.where(rows == pivots[...], 1.0, 0.0)
    return lax.dot_general(
        chosen, values, (((0,), (0,)), ((), ())),
        precision=lax.Precision.HIGHEST, preferred_element_type=jnp.float32,
    )


def factor_tile(packed_ref, lower_ref, upper_ref):
    rows = lax.broadcasted_iota(jnp.int32, (NB, NB), 0)
    cols = lax.broadcasted_iota(jnp.int32, (NB, NB), 1)
    lane = lax.broadcasted_iota(jnp.int32, (1, NB), 1)
    eye = jnp.where(rows == cols, 1.0, 0.0)
    lower_ref[...] = eye
    upper_ref[...] = eye

    def eliminate(j, carry):
        working = packed_ref[...]
        upper = upper_ref[...]
        row_part = packed_ref[pl.ds(j, 1), :]
        row_lower = lower_ref[pl.ds(j, 1), :]
        column = jnp.sum(jnp.where(cols == j, working, 0.0), axis=1, keepdims=True)
        column_upper = jnp.sum(jnp.where(cols == j, upper, 0.0), axis=1, keepdims=True)
        pivot_value = jnp.sum(jnp.where(lane == j, row_part, 0.0), axis=1, keepdims=True)
        multiplier = jnp.where(rows[:, :1] > j, column / pivot_value, 0.0)
        right = jnp.where(lane > j, row_part, 0.0)
        packed_ref[...] = jnp.where(
            (cols == j) & (rows > j), multiplier, working - multiplier * right
        )
        lower_ref[...] = lower_ref[...] - multiplier * row_lower
        scaled = column_upper / pivot_value
        upper_ref[...] = jnp.where(cols == j, scaled, upper - scaled * right)
        return carry

    lax.fori_loop(0, NB, eliminate, 0)


def exchange_kernel(table_ref, front_hbm, left_hbm, right_hbm, lead_block, diag, pivots,
                    arrived, left_panel, right_panel, packed, lower, upper,
                    lefts, rights, products, returned, front, contribution, col_chosen,
                    column_0, column_1, column_2, column_3, column_4, column_5,
                    row_chosen, first_column, raw_lead, lead_parts,
                    top_own, top_peer, top_sum, top_got,
                    load_sem, ring_send, ring_recv, back_send, back_recv, col_send, col_recv, own_col_sem,
                    row_send, row_recv, own_row_sem,
                    lead_part_send, lead_part_recv, lead_cast_send, lead_cast_recv, lead_send, lead_recv,
                    spread_send, spread_recv, share_send, share_recv,
                    peer_send, peer_recv, reduce_send, reduce_recv, top_send, top_recv):
    by_column = (column_0, column_1, column_2, column_3, column_4, column_5)
    child = lax.axis_index("child")
    group = lax.axis_index("grp")
    core = lax.rem(child, 2)
    at_y, at_x = group // RING, lax.rem(group, RING)
    along = jnp.where(core == 0, at_x, at_y)
    across = jnp.where(core == 0, at_y, at_x)

    load_right = pltpu.make_async_copy(right_hbm, rights.at[across], load_sem.at[0])
    load_left = pltpu.make_async_copy(left_hbm, lefts.at[along], load_sem.at[1])
    load_front = pltpu.make_async_copy(front_hbm, front, load_sem.at[2])
    load_right.start()
    load_left.start()
    load_front.start()

    barrier = pltpu.get_barrier_semaphore()

    def greet_group(i, carry):
        pl.semaphore_signal(
            barrier, inc=1, device_id=(child, lax.rem(group + i, GROUPS)), device_id_type=MESH
        )
        return carry

    def greet_child(i, carry):
        pl.semaphore_signal(
            barrier, inc=1, device_id=(lax.rem(child + i, CHILDREN), group), device_id_type=MESH
        )
        return carry

    lax.fori_loop(1, GROUPS, greet_group, 0)
    lax.fori_loop(1, CHILDREN, greet_child, 0)
    pl.semaphore_wait(barrier, GROUPS + CHILDREN - 2)

    def turn(position, by):
        return lax.rem(position + by + RING, RING)

    def place(u, v):
        return jnp.where(core == 0, v * RING + u, u * RING + v)

    gathers = {}

    def make(key, blocks, block, chunk, target):
        number = len(gathers)
        size = blocks.shape[1] // 2
        ref = blocks.at[block, pl.ds(chunk * size, size)]
        gathers[key] = pltpu.make_async_remote_copy(
            src_ref=ref, dst_ref=ref, send_sem=ring_send.at[number], recv_sem=ring_recv.at[number],
            device_id=(child, target), device_id_type=MESH,
        )

    for name, blocks, at in (("l", lefts, along), ("r", rights, across)):
        for way in (1, -1):
            target = place(turn(along, way), across) if name == "l" else place(along, turn(across, way))
            first = 0 if way == 1 else 1
            make((name, way, 0), blocks, at, first, target)
            make((name, way, 1), blocks, at, 1 - first, target)
            make((name, way, 2), blocks, turn(at, -way), first, target)

    def start(name, step):
        gathers[(name, 1, step)].start()
        gathers[(name, -1, step)].start()

    def arrive(name, step):
        gathers[(name, 1, step)].wait_recv()
        gathers[(name, -1, step)].wait_recv()

    def return_copy(to, piece):
        target = turn(along, to)
        number = to * RING + piece
        return pltpu.make_async_remote_copy(
            src_ref=products.at[target, piece], dst_ref=returned.at[along, piece],
            send_sem=back_send.at[number], recv_sem=back_recv.at[number],
            device_id=(child, place(target, across)), device_id_type=MESH,
        )

    def multiply(pairs):
        def one(i, carry):
            to, line = jnp.int32(0), jnp.int32(0)
            for number, (pair_to, pair_line) in enumerate(pairs):
                to = jnp.where(i == number, pair_to, to)
                line = jnp.where(i == number, pair_line, line)
            target, piece = turn(along, to), turn(across, line)
            product = full_dot(lefts[target], rights[piece])

            @pl.when(to == 0)
            def _():
                returned[along, piece] = product

            @pl.when(to != 0)
            def _():
                products[target, piece] = product
                return_copy(to, piece).start()

            return carry

        lax.fori_loop(0, len(pairs), one, 0)

    load_left.wait()
    start("l", 0)
    load_right.wait()
    start("r", 0)
    start("l", 1)
    start("r", 1)
    multiply([(0, 0)])
    arrive("l", 0)
    start("l", 2)
    arrive("r", 0)
    start("r", 2)
    arrive("l", 1)
    multiply([(1, 0), (3, 0)])
    arrive("r", 1)
    multiply([(1, 1), (3, 1), (1, 3), (3, 3), (0, 1), (0, 3)])
    arrive("l", 2)
    multiply([(2, 0), (2, 1), (2, 3)])
    arrive("r", 2)
    multiply([(2, 2), (1, 2), (3, 2), (0, 2)])
    load_front.wait()

    def subtract(source, piece):
        block = place(source, piece)
        base = pl.multiple_of(block * ROWS, ROWS)
        result = front[:, pl.ds(base, ROWS)] - returned[source, piece]
        contribution[2 * block] = result[:, :NB].reshape(2, PARTS, PART, NB)
        contribution[2 * block + 1] = result[:, NB:].reshape(2, PARTS, PART, NB)

    def subtract_own(piece, carry):
        subtract(along, piece)
        return carry

    lax.fori_loop(0, RING, subtract_own, 0)

    def subtract_returned(number, carry):
        to, line = 1 + number // RING, turn(across, lax.rem(number, RING))
        return_copy(to, line).wait_recv()
        subtract(turn(along, -to), line)
        return carry

    lax.fori_loop(0, (RING - 1) * RING, subtract_returned, 0)

    def column_copy(chunk, i):
        target = lax.rem(group + i, GROUPS)
        return pltpu.make_async_remote_copy(
            src_ref=col_chosen.at[chunk, target],
            dst_ref=by_column[chunk].at[pl.ds(2 * group, 2)],
            send_sem=col_send.at[chunk * GROUPS + i], recv_sem=col_recv.at[chunk * GROUPS + i],
            device_id=(child, target), device_id_type=MESH,
        )

    def own_column_copy(chunk):
        return pltpu.make_async_copy(
            col_chosen.at[chunk, group], by_column[chunk].at[pl.ds(2 * group, 2)],
            own_col_sem.at[chunk],
        )

    def select_column(chunk, target):
        slot, part = chunk // PARTS, chunk % PARTS
        picked = table_ref[COL_PICK + slot * CHILDREN + child, target]
        for row in range(2):
            col_chosen[chunk, target, row] = contribution[picked, row, part]

    def pass_columns(chunk):
        def send_column(i, carry):
            select_column(chunk, lax.rem(group + i, GROUPS))
            column_copy(chunk, i).start()
            return carry

        lax.fori_loop(1, GROUPS, send_column, 0)
        select_column(chunk, group)
        own_column_copy(chunk).start()

    for chunk in range(CHUNKS):
        pass_columns(chunk)

    for key in gathers:
        gathers[key].wait_send()

    def sent_back(number, carry):
        return_copy(1 + number // RING, lax.rem(number, RING)).wait_send()
        return carry

    lax.fori_loop(0, (RING - 1) * RING, sent_back, 0)

    def row_copy(chunk, i):
        target = lax.rem(child + i, CHILDREN)
        return pltpu.make_async_remote_copy(
            src_ref=row_chosen.at[chunk, target], dst_ref=arrived.at[chunk, child],
            send_sem=row_send.at[chunk * CHILDREN + i], recv_sem=row_recv.at[chunk * CHILDREN + i],
            device_id=(target, group), device_id_type=MESH,
        )

    def own_row_copy(chunk):
        return pltpu.make_async_copy(
            row_chosen.at[chunk, child], arrived.at[chunk, child], own_row_sem.at[chunk]
        )

    def select_rows(chunk, target):
        for r in range(ROW_SLOTS):
            tile = by_column[chunk][table_ref[ROW_PICK + r * CHILDREN + child, target]]
            row_chosen[chunk, target, pl.ds(r * PART, PART)] = tile

    def finish_columns(chunk):
        def finish(i, carry):
            column_copy(chunk, i).wait_recv()
            return carry

        lax.fori_loop(1, GROUPS, finish, 0)
        own_column_copy(chunk).wait()

    def send_rows(chunk, first=1, last=CHILDREN):
        def send(i, carry):
            select_rows(chunk, lax.rem(child + i, CHILDREN))
            row_copy(chunk, i).start()
            return carry

        lax.fori_loop(first, last, send, 0)
        if last == CHILDREN:
            select_rows(chunk, child)
            own_row_copy(chunk).start()

    def finish_rows(chunk):
        def finish(i, carry):
            row_copy(chunk, i).wait_recv()
            return carry

        lax.fori_loop(1, CHILDREN, finish, 0)
        own_row_copy(chunk).wait()

    def top_tile(chunk):
        return by_column[chunk][table_ref[ROW_PICK + child, 0]]

    lead_here = table_ref[COL_SLOT + child, 0] >= 0

    def lead_part_copy(source):
        return pltpu.make_async_remote_copy(
            src_ref=lead_parts.at[source], dst_ref=lead_parts.at[source],
            send_sem=lead_part_send.at[0], recv_sem=lead_part_recv.at[source],
            device_id=(0, group), device_id_type=MESH,
        )

    def lead_cast_copy(target):
        return pltpu.make_async_remote_copy(
            src_ref=raw_lead, dst_ref=raw_lead,
            send_sem=lead_cast_send.at[target], recv_sem=lead_cast_recv.at[0],
            device_id=(target, group), device_id_type=MESH,
        )

    def lead_copy(target):
        return pltpu.make_async_remote_copy(
            src_ref=raw_lead, dst_ref=raw_lead,
            send_sem=lead_send.at[target], recv_sem=lead_recv.at[0],
            device_id=(child, target), device_id_type=MESH,
        )

    def send_lead_part():
        for part in range(PARTS):
            tile = jnp.where(lead_here, top_tile(part), 0.0)
            lead_parts[child, pl.ds(part * PART, PART)] = tile

        @pl.when(child != 0)
        def _():
            lead_part_copy(child).start()

    def sum_lead():
        def arrive_part(k, carry):
            lead_part_copy(k).wait_recv()
            return carry

        lax.fori_loop(1, CHILDREN, arrive_part, 0)
        rows = lax.broadcasted_iota(jnp.int32, (NB, NB), 0)
        cols = lax.broadcasted_iota(jnp.int32, (NB, NB), 1)
        total = lead_block[...] + jnp.where(rows == cols, diag[0:1, :], 0.0)
        for k in range(CHILDREN):
            total = total + lead_parts[k]
        raw_lead[...] = permute_rows(pivots, total)

        def cast(k, carry):
            lead_cast_copy(k).start()
            return carry

        lax.fori_loop(1, CHILDREN, cast, 0)

    def pass_lead():
        @pl.when(child != 0)
        def _():
            lead_cast_copy(0).wait_recv()

        def send_lead(i, carry):
            lead_copy(i).start()
            return carry

        lax.fori_loop(1, GROUPS, send_lead, 0)

    def spread_copy(target):
        return pltpu.make_async_remote_copy(
            src_ref=left_panel.at[target], dst_ref=left_panel.at[target],
            send_sem=spread_send.at[target], recv_sem=spread_recv.at[0],
            device_id=(child, target), device_id_type=MESH,
        )

    def own_spread():
        return pltpu.make_async_remote_copy(
            src_ref=left_panel.at[group], dst_ref=left_panel.at[group],
            send_sem=spread_send.at[0], recv_sem=spread_recv.at[0],
            device_id=(child, 0), device_id_type=MESH,
        )

    def share_copy(i):
        return pltpu.make_async_remote_copy(
            src_ref=left_panel.at[group], dst_ref=left_panel.at[group],
            send_sem=share_send.at[i], recv_sem=share_recv.at[i],
            device_id=(child, lax.rem(group + i, GROUPS)), device_id_type=MESH,
        )

    at_z = child // 2
    partner = child + 1 - 2 * core

    def peer_copy():
        return pltpu.make_async_remote_copy(
            src_ref=top_own.at[1 - core], dst_ref=top_peer,
            send_sem=peer_send.at[0], recv_sem=peer_recv.at[0],
            device_id=(partner, group), device_id_type=MESH,
        )

    def reduce_copy(i):
        target = turn(at_z, i)
        return pltpu.make_async_remote_copy(
            src_ref=top_sum.at[target], dst_ref=top_got.at[at_z],
            send_sem=reduce_send.at[i], recv_sem=reduce_recv.at[i],
            device_id=(2 * target + core, group), device_id_type=MESH,
        )

    def top_share_copy(i):
        target = turn(at_z, i)
        return pltpu.make_async_remote_copy(
            src_ref=right_panel.at[core, at_z], dst_ref=right_panel.at[core, at_z],
            send_sem=top_send.at[i], recv_sem=top_recv.at[i],
            device_id=(2 * target + core, group), device_id_type=MESH,
        )

    def peer_share_copy():
        return pltpu.make_async_remote_copy(
            src_ref=right_panel.at[core], dst_ref=right_panel.at[core],
            send_sem=peer_send.at[1], recv_sem=peer_recv.at[1],
            device_id=(partner, group), device_id_type=MESH,
        )

    finish_columns(0)
    send_rows(0)
    finish_columns(1)

    @pl.when(group == 0)
    def _():
        send_lead_part()

    send_rows(1)
    finish_columns(2)

    @pl.when((group == 0) & (child == 0))
    def _():
        sum_lead()

    send_rows(2)
    finish_columns(3)
    send_rows(3)

    @pl.when(group == 0)
    def _():
        pass_lead()

    for part in range(PARTS):
        finish_rows(part)

    @pl.when(group == 0)
    def _():
        loads = [
            pltpu.make_async_copy(
                arrived.at[part, :, pl.ds(r * PART, PART), :], first_column.at[part, :, r],
                load_sem.at[part * ROW_SLOTS + r],
            )
            for part in range(PARTS) for r in range(ROW_SLOTS)
        ]
        for load in loads:
            load.start()
        for load in loads:
            load.wait()

        def assemble(i, carry):
            a = lax.rem(i, TR)
            for part in range(PARTS):
                total = jnp.zeros((PART, NB), jnp.float32)
                for k in range(CHILDREN):
                    slot = table_ref[ROW_SLOT + k, a * CHILDREN + child]
                    held = (slot >= 0) & (table_ref[COL_SLOT + k, 0] >= 0)
                    tile = first_column[part, k, jnp.maximum(slot, 0)]
                    total = total + jnp.where(held, tile, 0.0)
                left_panel[a, part * PART:(part + 1) * PART] = total

            @pl.when(a > 0)
            def _():
                spread_copy(a).start()

            return carry

        lax.fori_loop(1, TR + 1, assemble, 0)

    finish_columns(4)
    send_rows(4)
    finish_columns(5)

    for b in range(TC):
        held = table_ref[COL_SLOT + child, b * GROUPS + group]
        for part in range(PARTS):
            total = jnp.zeros((PART, NB), jnp.float32)
            for slot in range(COL_SLOTS):
                tile = top_tile(slot * PARTS + part)
                total = jnp.where(lead_here & (held == slot), tile, total)
            top_own[b % 2, b // 2, part * PART:(part + 1) * PART] = total
    peer_copy().start()
    peer_copy().wait_recv()
    top_sum[...] = top_own[core] + top_peer[...]
    for i in range(1, RING):
        reduce_copy(i).start()
    send_rows(5, 1, RING)

    @pl.when(group != 0)
    def _():
        own_spread().wait_recv()

    def send_share(i, carry):
        @pl.when(lax.rem(group + i, GROUPS) != 0)
        def _():
            share_copy(i).start()
        return carry

    lax.fori_loop(1, GROUPS, send_share, 0)

    @pl.when(group != 0)
    def _():
        lead_copy(0).wait_recv()

    packed[...] = raw_lead[...]
    factor_tile(packed, lower, upper)

    for i in range(1, RING):
        reduce_copy(i).wait_recv()
    right_panel[core, at_z] = (
        top_sum[at_z] + top_got[turn(at_z, 1)] + top_got[turn(at_z, 2)] + top_got[turn(at_z, 3)]
    )
    for i in range(1, RING):
        top_share_copy(i).start()
    send_rows(5, RING, CHILDREN)
    for i in range(1, RING):
        top_share_copy(i).wait_recv()
    peer_share_copy().start()

    def finish_share(i, carry):
        @pl.when(lax.rem(group + i, GROUPS) != 0)
        def _():
            share_copy(i).wait_send()

        @pl.when(group != 0)
        def _():
            share_copy(i).wait_recv()

        @pl.when(group == 0)
        def _():
            lead_copy(i).wait_send()
            spread_copy(i).wait_send()

        return carry

    lax.fori_loop(1, GROUPS, finish_share, 0)

    @pl.when((group == 0) & (child == 0))
    def _():
        def sent_cast(k, carry):
            lead_cast_copy(k).wait_send()
            return carry

        lax.fori_loop(1, CHILDREN, sent_cast, 0)

    @pl.when((group == 0) & (child != 0))
    def _():
        lead_part_copy(child).wait_send()

    peer_copy().wait_send()
    for i in range(1, RING):
        reduce_copy(i).wait_send()
        top_share_copy(i).wait_send()

    for chunk in range(CHUNKS):
        def sent_columns(i, carry):
            column_copy(chunk, i).wait_send()
            return carry

        lax.fori_loop(1, GROUPS, sent_columns, 0)

    for chunk in range(PARTS, CHUNKS):
        finish_rows(chunk)
    peer_share_copy().wait()

    for chunk in range(CHUNKS):
        def sent_rows(i, carry):
            row_copy(chunk, i).wait_send()
            return carry

        lax.fori_loop(1, CHILDREN, sent_rows, 0)


def exchange(table, front, left, right, lead_block, diag, pivots):
    tile = jax.ShapeDtypeStruct((NB, NB), jnp.float32)
    dma = pltpu.SemaphoreType.DMA
    return pl.pallas_call(
        exchange_kernel,
        out_shape=(
            jax.ShapeDtypeStruct((CHUNKS, CHILDREN, ROW_SLOTS * PART, NB), jnp.float32),
            jax.ShapeDtypeStruct((TR, NB, NB), jnp.float32),
            jax.ShapeDtypeStruct((2, RING, NB, NB), jnp.float32),
            tile, tile, tile,
        ),
        in_specs=[SMEM, ANY, ANY, ANY, VMEM, VMEM, VMEM],
        out_specs=(ANY, VMEM, VMEM, VMEM, VMEM, VMEM),
        scratch_shapes=[
            pltpu.VMEM((RING, ROWS, PIV), jnp.float32),
            pltpu.VMEM((RING, PIV, ROWS), jnp.float32),
            pltpu.VMEM((RING, RING, ROWS, ROWS), jnp.float32),
            pltpu.VMEM((RING, RING, ROWS, ROWS), jnp.float32),
            pltpu.VMEM((ROWS, CB), jnp.float32),
            pltpu.VMEM((CBT, 2, PARTS, PART, NB), jnp.float32),
            pltpu.VMEM((CHUNKS, GROUPS, 2, PART, NB), jnp.float32),
            pltpu.VMEM((CBT, PART, NB), jnp.float32),
            pltpu.VMEM((CBT, PART, NB), jnp.float32),
            pltpu.VMEM((CBT, PART, NB), jnp.float32),
            pltpu.VMEM((CBT, PART, NB), jnp.float32),
            pltpu.VMEM((CBT, PART, NB), jnp.float32),
            pltpu.VMEM((CBT, PART, NB), jnp.float32),
            pltpu.VMEM((CHUNKS, CHILDREN, ROW_SLOTS * PART, NB), jnp.float32),
            pltpu.VMEM((PARTS, CHILDREN, ROW_SLOTS, PART, NB), jnp.float32),
            pltpu.VMEM((NB, NB), jnp.float32),
            pltpu.VMEM((CHILDREN, NB, NB), jnp.float32),
            pltpu.VMEM((2, RING, NB, NB), jnp.float32),
            pltpu.VMEM((RING, NB, NB), jnp.float32),
            pltpu.VMEM((RING, NB, NB), jnp.float32),
            pltpu.VMEM((RING, NB, NB), jnp.float32),
            dma((PARTS * ROW_SLOTS,)), dma((12,)), dma((12,)), dma((16,)), dma((16,)),
            dma((CHUNKS * GROUPS,)), dma((CHUNKS * GROUPS,)), dma((CHUNKS,)),
            dma((CHUNKS * CHILDREN,)), dma((CHUNKS * CHILDREN,)), dma((CHUNKS,)),
            dma((1,)), dma((CHILDREN,)), dma((CHILDREN,)), dma((1,)), dma((GROUPS,)), dma((1,)),
            dma((GROUPS,)), dma((1,)), dma((GROUPS,)), dma((GROUPS,)),
            dma((2,)), dma((2,)), dma((RING,)), dma((RING,)), dma((RING,)), dma((RING,)),
        ],
        compiler_params=pltpu.CompilerParams(
            collective_id=0, has_side_effects=True, vmem_limit_bytes=60 * 2**20
        ),
        name="exchange",
    )(table, front, left, right, lead_block, diag, pivots)


def split(values):
    high = values.astype(jnp.bfloat16)
    return high, (values - high.astype(jnp.float32)).astype(jnp.bfloat16)


def update_kernel(table_ref, arrived, left_raw, right_panel,
                  packed, lower, upper, diag, pivots, out_ref, right, right_parts, total):
    step = pl.program_id(0)
    child = lax.axis_index("child")
    group = lax.axis_index("grp")
    rows = lax.broadcasted_iota(jnp.int32, (NB, NB), 0)
    cols = lax.broadcasted_iota(jnp.int32, (NB, NB), 1)

    @pl.when(step == 0)
    def _():
        for b in range(TC):
            right[:, b * NB:(b + 1) * NB] = right_panel[b % 2, b // 2]
        right[...] = full_dot(lower[...], permute_rows(pivots, right[...]))

        @pl.when(group == 0)
        def _():
            right[:, :NB] = jnp.zeros((NB, NB), jnp.float32)

        high, low = split(right[...])
        right_parts[0:NB] = high
        right_parts[NB:2 * NB] = low
        right_parts[2 * NB:] = high

    left = full_dot(left_raw[...].reshape(STEP * NB, NB), upper[...])
    high, low = split(left)
    left_parts = jnp.concatenate([high, high, low], axis=1)
    total[...] = -jnp.dot(left_parts, right_parts[...], preferred_element_type=jnp.float32)

    def place(row, carry):
        a = step * STEP + row
        for k in range(CHILDREN):
            row_slot = table_ref[ROW_SLOT + k, a * CHILDREN + child]

            @pl.when(row_slot >= 0)
            def _():
                base = pl.multiple_of(row_slot * PART, PART)
                for b in range(TC):
                    col_slot = table_ref[COL_SLOT + k, b * GROUPS + group]

                    @pl.when(col_slot >= 0)
                    def _():
                        across = pl.ds(b * NB, NB)
                        for part in range(PARTS):
                            down = pl.ds(pl.multiple_of(row * NB, NB) + part * PART, PART)
                            tile = arrived[col_slot * PARTS + part, k, pl.ds(base, PART), :]
                            total[down, across] = total[down, across] + tile

        on_diag = (lax.rem(group, CHILDREN) == child) & (lax.rem(a, 2) == group // CHILDREN)

        @pl.when(on_diag)
        def _():
            across = pl.ds(pl.multiple_of((a // 2) * NB, NB), NB)
            down = pl.ds(pl.multiple_of(row * NB, NB), NB)
            entries = diag[pl.ds(a * CHILDREN + child, 1), :]
            total[down, across] = total[down, across] + jnp.where(rows == cols, entries, 0.0)

        return carry

    lax.fori_loop(0, STEP, place, 0)

    @pl.when(group == 0)
    def _():
        total[:, :NB] = left

    @pl.when((step == 0) & (child == 0))
    def _():
        total[:NB, :] = right[...]

        @pl.when(group == 0)
        def _():
            total[:NB, :NB] = packed[...]

    out_ref[0, :, 0, :] = total[...]


def update_front(table, arrived, left_raw, right_panel, packed, lower, upper, diag, pivots):
    return pl.pallas_call(
        update_kernel,
        grid=(TR // STEP,),
        out_shape=jax.ShapeDtypeStruct((1, TR * NB, 1, TC * NB), jnp.float32),
        in_specs=[
            SMEM, VMEM,
            pl.BlockSpec((STEP, NB, NB), lambda a: (a, 0, 0)),
            VMEM, VMEM, VMEM, VMEM, VMEM, VMEM,
        ],
        out_specs=pl.BlockSpec((1, STEP * NB, 1, TC * NB), lambda a: (0, a, 0, 0)),
        scratch_shapes=[
            pltpu.VMEM((NB, TC * NB), jnp.float32),
            pltpu.VMEM((3 * NB, TC * NB), jnp.bfloat16),
            pltpu.VMEM((STEP * NB, TC * NB), jnp.float32),
        ],
        compiler_params=pltpu.CompilerParams(vmem_limit_bytes=60 * 2**20),
        name="update_front",
    )(table, arrived, left_raw, right_panel, packed, lower, upper, diag, pivots)


def body(front_child, left_factor, right_factor, child_map, parent_diag, lead_block, pivots):
    diag = parent_diag.reshape(PT, NB)
    pivot_row = pivots.reshape(1, NB)
    table = slot_table(child_map)
    arrived, left_raw, right_panel, packed, lower, upper = exchange(
        table, front_child[0], left_factor[0], right_factor[0], lead_block, diag, pivot_row
    )
    return update_front(
        table, arrived, left_raw, right_panel, packed, lower, upper, diag, pivot_row
    )


def solution(mesh):
    in_specs = (
        P("child", "grp", None),
        P("child", "grp", None),
        P("child", None, "grp"),
        P(),
        P(),
        P(),
        P(),
    )
    out_specs = P("child", None, "grp", None)
    return jax.shard_map(body, mesh=mesh, in_specs=in_specs, out_specs=out_specs, check_vma=False)
```

```python
import jax
import jax.numpy as jnp
from jax import lax
from jax.experimental import pallas as pl
from jax.experimental.pallas import tpu as pltpu
from jax.sharding import PartitionSpec as P

NB = 128
CB = 4096
PIV = 1280
NP = 16384
CHILDREN = 8
GROUPS = 16
RING = 4
CBT = CB // NB
PT = NP // NB
TR = PT // CHILDREN
TC = PT // GROUPS
COL_SLOTS = 3
ROW_SLOTS = 6
PARTS = 4
PART = NB // PARTS
CHUNKS = COL_SLOTS * PARTS
STEP = 4
ROWS = CB // GROUPS
COL_SLOT = 0
ROW_SLOT = CHILDREN
COL_PICK = 2 * CHILDREN
ROW_PICK = COL_PICK + COL_SLOTS * CHILDREN
TABLE_ROWS = ROW_PICK + ROW_SLOTS * CHILDREN
MESH = pl.DeviceIdType.MESH
ANY = pl.BlockSpec(memory_space=pl.ANY)
VMEM = pl.BlockSpec(memory_space=pltpu.VMEM)
SMEM = pl.BlockSpec(memory_space=pltpu.SMEM)


def full_dot(a, b):
    return jnp.dot(a, b, precision=lax.Precision.HIGHEST, preferred_element_type=jnp.float32)


def table_kernel(map_ref, table_ref):
    lanes = lax.broadcasted_iota(jnp.int32, (CHILDREN, PT), 1)
    tiles = map_ref[...]
    source = jnp.full((CHILDREN, PT), -1, jnp.int32)
    for t in range(CBT):
        source = jnp.where(tiles[:, t:t + 1] == lanes, t, source)
    held = (source >= 0).astype(jnp.int32)

    def fill(classes, capacity, slot_base, pick_base):
        rank = jnp.zeros((CHILDREN, PT), jnp.int32)
        for shift in range(classes, PT, classes):
            rank = rank + jnp.where(lanes >= shift, pltpu.roll(held, shift, 1), 0)
        slots = jnp.where(held > 0, rank, -1)
        table_ref[slot_base:slot_base + CHILDREN] = slots
        for slot in range(capacity):
            picked = jnp.where(slots == slot, source, 0)
            shift = classes
            while shift < PT:
                picked = picked + pltpu.roll(picked, shift, 1)
                shift *= 2
            base = pick_base + slot * CHILDREN
            table_ref[base:base + CHILDREN] = picked

    fill(GROUPS, COL_SLOTS, COL_SLOT, COL_PICK)
    fill(CHILDREN, ROW_SLOTS, ROW_SLOT, ROW_PICK)


def slot_table(child_map):
    return pl.pallas_call(
        table_kernel,
        out_shape=jax.ShapeDtypeStruct((TABLE_ROWS, PT), jnp.int32),
        name="slot_table",
    )(child_map)


def permute_rows(pivots, values):
    rows = lax.broadcasted_iota(jnp.int32, (NB, NB), 0)
    chosen = jnp.where(rows == pivots[...], 1.0, 0.0)
    return lax.dot_general(
        chosen, values, (((0,), (0,)), ((), ())),
        precision=lax.Precision.HIGHEST, preferred_element_type=jnp.float32,
    )


def factor_tile(packed_ref, lower_ref, upper_ref):
    rows = lax.broadcasted_iota(jnp.int32, (NB, NB), 0)
    cols = lax.broadcasted_iota(jnp.int32, (NB, NB), 1)
    lane = lax.broadcasted_iota(jnp.int32, (1, NB), 1)
    eye = jnp.where(rows == cols, 1.0, 0.0)
    lower_ref[...] = eye
    upper_ref[...] = eye

    def eliminate(j, carry):
        working = packed_ref[...]
        upper = upper_ref[...]
        row_part = packed_ref[pl.ds(j, 1), :]
        row_lower = lower_ref[pl.ds(j, 1), :]
        column = jnp.sum(jnp.where(cols == j, working, 0.0), axis=1, keepdims=True)
        column_upper = jnp.sum(jnp.where(cols == j, upper, 0.0), axis=1, keepdims=True)
        pivot_value = jnp.sum(jnp.where(lane == j, row_part, 0.0), axis=1, keepdims=True)
        multiplier = jnp.where(rows[:, :1] > j, column / pivot_value, 0.0)
        right = jnp.where(lane > j, row_part, 0.0)
        packed_ref[...] = jnp.where(
            (cols == j) & (rows > j), multiplier, working - multiplier * right
        )
        lower_ref[...] = lower_ref[...] - multiplier * row_lower
        scaled = column_upper / pivot_value
        upper_ref[...] = jnp.where(cols == j, scaled, upper - scaled * right)
        return carry

    lax.fori_loop(0, NB, eliminate, 0)


def exchange_kernel(table_ref, front_hbm, left_hbm, right_hbm, lead_block, diag, pivots,
                    arrived, left_panel, right_panel, packed, lower, upper,
                    lefts, rights, products, returned, front, contribution, col_chosen,
                    column_0, column_1, column_2, column_3, column_4, column_5,
                    column_6, column_7, column_8, column_9, column_10, column_11,
                    row_chosen, first_column, raw_lead, lead_parts,
                    top_own, top_peer, top_sum, top_got,
                    load_sem, ring_send, ring_recv, back_send, back_recv, col_send, col_recv, own_col_sem,
                    row_send, row_recv, own_row_sem,
                    lead_part_send, lead_part_recv, lead_cast_send, lead_cast_recv, lead_send, lead_recv,
                    spread_send, spread_recv, share_send, share_recv,
                    peer_send, peer_recv, reduce_send, reduce_recv, top_send, top_recv):
    by_column = (
        column_0, column_1, column_2, column_3, column_4, column_5,
        column_6, column_7, column_8, column_9, column_10, column_11,
    )
    child = lax.axis_index("child")
    group = lax.axis_index("grp")
    core = lax.rem(child, 2)
    at_y, at_x = group // RING, lax.rem(group, RING)
    along = jnp.where(core == 0, at_x, at_y)
    across = jnp.where(core == 0, at_y, at_x)

    load_right = pltpu.make_async_copy(right_hbm, rights.at[across], load_sem.at[0])
    load_left = pltpu.make_async_copy(left_hbm, lefts.at[along], load_sem.at[1])
    load_front = pltpu.make_async_copy(front_hbm, front, load_sem.at[2])
    load_right.start()
    load_left.start()
    load_front.start()

    barrier = pltpu.get_barrier_semaphore()

    def greet_group(i, carry):
        pl.semaphore_signal(
            barrier, inc=1, device_id=(child, lax.rem(group + i, GROUPS)), device_id_type=MESH
        )
        return carry

    def greet_child(i, carry):
        pl.semaphore_signal(
            barrier, inc=1, device_id=(lax.rem(child + i, CHILDREN), group), device_id_type=MESH
        )
        return carry

    lax.fori_loop(1, GROUPS, greet_group, 0)
    lax.fori_loop(1, CHILDREN, greet_child, 0)
    pl.semaphore_wait(barrier, GROUPS + CHILDREN - 2)

    def turn(position, by):
        return lax.rem(position + by + RING, RING)

    def place(u, v):
        return jnp.where(core == 0, v * RING + u, u * RING + v)

    gathers = {}

    def make(key, blocks, block, chunk, target):
        number = len(gathers)
        size = blocks.shape[1] // 2
        ref = blocks.at[block, pl.ds(chunk * size, size)]
        gathers[key] = pltpu.make_async_remote_copy(
            src_ref=ref, dst_ref=ref, send_sem=ring_send.at[number], recv_sem=ring_recv.at[number],
            device_id=(child, target), device_id_type=MESH,
        )

    for name, blocks, at in (("l", lefts, along), ("r", rights, across)):
        for way in (1, -1):
            target = place(turn(along, way), across) if name == "l" else place(along, turn(across, way))
            first = 0 if way == 1 else 1
            make((name, way, 0), blocks, at, first, target)
            make((name, way, 1), blocks, at, 1 - first, target)
            make((name, way, 2), blocks, turn(at, -way), first, target)

    def start(name, step):
        gathers[(name, 1, step)].start()
        gathers[(name, -1, step)].start()

    def arrive(name, step):
        gathers[(name, 1, step)].wait_recv()
        gathers[(name, -1, step)].wait_recv()

    def return_copy(to, piece):
        target = turn(along, to)
        number = to * RING + piece
        return pltpu.make_async_remote_copy(
            src_ref=products.at[target, piece], dst_ref=returned.at[along, piece],
            send_sem=back_send.at[number], recv_sem=back_recv.at[number],
            device_id=(child, place(target, across)), device_id_type=MESH,
        )

    def multiply(pairs):
        def one(i, carry):
            to, line = jnp.int32(0), jnp.int32(0)
            for number, (pair_to, pair_line) in enumerate(pairs):
                to = jnp.where(i == number, pair_to, to)
                line = jnp.where(i == number, pair_line, line)
            target, piece = turn(along, to), turn(across, line)
            product = full_dot(lefts[target], rights[piece])

            @pl.when(to == 0)
            def _():
                returned[along, piece] = product

            @pl.when(to != 0)
            def _():
                products[target, piece] = product
                return_copy(to, piece).start()

            return carry

        lax.fori_loop(0, len(pairs), one, 0)

    load_left.wait()
    start("l", 0)
    load_right.wait()
    start("r", 0)
    start("l", 1)
    start("r", 1)
    multiply([(0, 0)])
    arrive("l", 0)
    start("l", 2)
    arrive("r", 0)
    start("r", 2)
    arrive("l", 1)
    multiply([(1, 0), (3, 0)])
    arrive("r", 1)
    multiply([(1, 1), (3, 1), (1, 3), (3, 3), (0, 1), (0, 3)])
    arrive("l", 2)
    multiply([(2, 0), (2, 1), (2, 3)])
    arrive("r", 2)
    multiply([(2, 2), (1, 2), (3, 2), (0, 2)])
    load_front.wait()

    def subtract(source, piece):
        block = place(source, piece)
        base = pl.multiple_of(block * ROWS, ROWS)
        result = front[:, pl.ds(base, ROWS)] - returned[source, piece]
        contribution[2 * block] = result[:, :NB].reshape(2, PARTS, PART, NB)
        contribution[2 * block + 1] = result[:, NB:].reshape(2, PARTS, PART, NB)

    def subtract_own(piece, carry):
        subtract(along, piece)
        return carry

    lax.fori_loop(0, RING, subtract_own, 0)

    def subtract_returned(number, carry):
        to, line = 1 + number // RING, turn(across, lax.rem(number, RING))
        return_copy(to, line).wait_recv()
        subtract(turn(along, -to), line)
        return carry

    lax.fori_loop(0, (RING - 1) * RING, subtract_returned, 0)

    def column_copy(chunk, i):
        target = lax.rem(group + i, GROUPS)
        return pltpu.make_async_remote_copy(
            src_ref=col_chosen.at[chunk, target],
            dst_ref=by_column[chunk].at[pl.ds(2 * group, 2)],
            send_sem=col_send.at[chunk * GROUPS + i], recv_sem=col_recv.at[chunk * GROUPS + i],
            device_id=(child, target), device_id_type=MESH,
        )

    def own_column_copy(chunk):
        return pltpu.make_async_copy(
            col_chosen.at[chunk, group], by_column[chunk].at[pl.ds(2 * group, 2)],
            own_col_sem.at[chunk],
        )

    def select_column(chunk, target):
        slot, part = chunk // PARTS, chunk % PARTS
        picked = table_ref[COL_PICK + slot * CHILDREN + child, target]
        for row in range(2):
            col_chosen[chunk, target, row] = contribution[picked, row, part]

    def pass_columns(chunk):
        def send_column(i, carry):
            select_column(chunk, lax.rem(group + i, GROUPS))
            column_copy(chunk, i).start()
            return carry

        lax.fori_loop(1, GROUPS, send_column, 0)
        select_column(chunk, group)
        own_column_copy(chunk).start()

    for chunk in range(CHUNKS):
        pass_columns(chunk)

    for key in gathers:
        gathers[key].wait_send()

    def sent_back(number, carry):
        return_copy(1 + number // RING, lax.rem(number, RING)).wait_send()
        return carry

    lax.fori_loop(0, (RING - 1) * RING, sent_back, 0)

    def row_copy(chunk, i):
        target = lax.rem(child + i, CHILDREN)
        return pltpu.make_async_remote_copy(
            src_ref=row_chosen.at[chunk, target], dst_ref=arrived.at[chunk, child],
            send_sem=row_send.at[chunk * CHILDREN + i], recv_sem=row_recv.at[chunk * CHILDREN + i],
            device_id=(target, group), device_id_type=MESH,
        )

    def own_row_copy(chunk):
        return pltpu.make_async_copy(
            row_chosen.at[chunk, child], arrived.at[chunk, child], own_row_sem.at[chunk]
        )

    def select_rows(chunk, target):
        for r in range(ROW_SLOTS):
            tile = by_column[chunk][table_ref[ROW_PICK + r * CHILDREN + child, target]]
            row_chosen[chunk, target, pl.ds(r * PART, PART)] = tile

    def finish_columns(chunk):
        def finish(i, carry):
            column_copy(chunk, i).wait_recv()
            return carry

        lax.fori_loop(1, GROUPS, finish, 0)
        own_column_copy(chunk).wait()

    def send_rows(chunk, first=1, last=CHILDREN):
        def send(i, carry):
            select_rows(chunk, lax.rem(child + i, CHILDREN))
            row_copy(chunk, i).start()
            return carry

        lax.fori_loop(first, last, send, 0)
        if last == CHILDREN:
            select_rows(chunk, child)
            own_row_copy(chunk).start()

    def finish_rows(chunk):
        def finish(i, carry):
            row_copy(chunk, i).wait_recv()
            return carry

        lax.fori_loop(1, CHILDREN, finish, 0)
        own_row_copy(chunk).wait()

    def top_tile(chunk):
        return by_column[chunk][table_ref[ROW_PICK + child, 0]]

    lead_here = table_ref[COL_SLOT + child, 0] >= 0

    def lead_part_copy(source):
        return pltpu.make_async_remote_copy(
            src_ref=lead_parts.at[source], dst_ref=lead_parts.at[source],
            send_sem=lead_part_send.at[0], recv_sem=lead_part_recv.at[source],
            device_id=(0, group), device_id_type=MESH,
        )

    def lead_cast_copy(target):
        return pltpu.make_async_remote_copy(
            src_ref=raw_lead, dst_ref=raw_lead,
            send_sem=lead_cast_send.at[target], recv_sem=lead_cast_recv.at[0],
            device_id=(target, group), device_id_type=MESH,
        )

    def lead_copy(target):
        return pltpu.make_async_remote_copy(
            src_ref=raw_lead, dst_ref=raw_lead,
            send_sem=lead_send.at[target], recv_sem=lead_recv.at[0],
            device_id=(child, target), device_id_type=MESH,
        )

    def send_lead_part():
        for part in range(PARTS):
            tile = jnp.where(lead_here, top_tile(part), 0.0)
            lead_parts[child, pl.ds(part * PART, PART)] = tile

        @pl.when(child != 0)
        def _():
            lead_part_copy(child).start()

    def sum_lead():
        def arrive_part(k, carry):
            lead_part_copy(k).wait_recv()
            return carry

        lax.fori_loop(1, CHILDREN, arrive_part, 0)
        rows = lax.broadcasted_iota(jnp.int32, (NB, NB), 0)
        cols = lax.broadcasted_iota(jnp.int32, (NB, NB), 1)
        total = lead_block[...] + jnp.where(rows == cols, diag[0:1, :], 0.0)
        for k in range(CHILDREN):
            total = total + lead_parts[k]
        raw_lead[...] = permute_rows(pivots, total)

        def cast(k, carry):
            lead_cast_copy(k).start()
            return carry

        lax.fori_loop(1, CHILDREN, cast, 0)

    def pass_lead():
        @pl.when(child != 0)
        def _():
            lead_cast_copy(0).wait_recv()

        def send_lead(i, carry):
            lead_copy(i).start()
            return carry

        lax.fori_loop(1, GROUPS, send_lead, 0)

    def spread_copy(target):
        return pltpu.make_async_remote_copy(
            src_ref=left_panel.at[target], dst_ref=left_panel.at[target],
            send_sem=spread_send.at[target], recv_sem=spread_recv.at[0],
            device_id=(child, target), device_id_type=MESH,
        )

    def own_spread():
        return pltpu.make_async_remote_copy(
            src_ref=left_panel.at[group], dst_ref=left_panel.at[group],
            send_sem=spread_send.at[0], recv_sem=spread_recv.at[0],
            device_id=(child, 0), device_id_type=MESH,
        )

    def share_copy(i):
        return pltpu.make_async_remote_copy(
            src_ref=left_panel.at[group], dst_ref=left_panel.at[group],
            send_sem=share_send.at[i], recv_sem=share_recv.at[i],
            device_id=(child, lax.rem(group + i, GROUPS)), device_id_type=MESH,
        )

    at_z = child // 2
    partner = child + 1 - 2 * core

    def peer_copy():
        return pltpu.make_async_remote_copy(
            src_ref=top_own.at[1 - core], dst_ref=top_peer,
            send_sem=peer_send.at[0], recv_sem=peer_recv.at[0],
            device_id=(partner, group), device_id_type=MESH,
        )

    def reduce_copy(i):
        target = turn(at_z, i)
        return pltpu.make_async_remote_copy(
            src_ref=top_sum.at[target], dst_ref=top_got.at[at_z],
            send_sem=reduce_send.at[i], recv_sem=reduce_recv.at[i],
            device_id=(2 * target + core, group), device_id_type=MESH,
        )

    def top_share_copy(i):
        target = turn(at_z, i)
        return pltpu.make_async_remote_copy(
            src_ref=right_panel.at[core, at_z], dst_ref=right_panel.at[core, at_z],
            send_sem=top_send.at[i], recv_sem=top_recv.at[i],
            device_id=(2 * target + core, group), device_id_type=MESH,
        )

    def peer_share_copy():
        return pltpu.make_async_remote_copy(
            src_ref=right_panel.at[core], dst_ref=right_panel.at[core],
            send_sem=peer_send.at[1], recv_sem=peer_recv.at[1],
            device_id=(partner, group), device_id_type=MESH,
        )

    def pass_chunks(first, last):
        for chunk in range(first, last):
            finish_columns(chunk)
            send_rows(chunk)

    pass_chunks(0, PARTS - 1)
    finish_columns(PARTS - 1)

    @pl.when(group == 0)
    def _():
        send_lead_part()

    send_rows(PARTS - 1)
    pass_chunks(PARTS, 3 * PARTS // 2 - 1)
    finish_columns(3 * PARTS // 2 - 1)

    @pl.when((group == 0) & (child == 0))
    def _():
        sum_lead()

    send_rows(3 * PARTS // 2 - 1)
    pass_chunks(3 * PARTS // 2, 2 * PARTS)

    @pl.when(group == 0)
    def _():
        pass_lead()

    for part in range(PARTS):
        finish_rows(part)

    @pl.when(group == 0)
    def _():
        loads = [
            pltpu.make_async_copy(
                arrived.at[part, :, pl.ds(r * PART, PART), :], first_column.at[part, :, r],
                load_sem.at[part * ROW_SLOTS + r],
            )
            for part in range(PARTS) for r in range(ROW_SLOTS)
        ]
        for load in loads:
            load.start()
        for load in loads:
            load.wait()

        def assemble(i, carry):
            a = lax.rem(i, TR)
            for part in range(PARTS):
                total = jnp.zeros((PART, NB), jnp.float32)
                for k in range(CHILDREN):
                    slot = table_ref[ROW_SLOT + k, a * CHILDREN + child]
                    held = (slot >= 0) & (table_ref[COL_SLOT + k, 0] >= 0)
                    tile = first_column[part, k, jnp.maximum(slot, 0)]
                    total = total + jnp.where(held, tile, 0.0)
                left_panel[a, part * PART:(part + 1) * PART] = total

            @pl.when(a > 0)
            def _():
                spread_copy(a).start()

            return carry

        lax.fori_loop(1, TR + 1, assemble, 0)

    pass_chunks(2 * PARTS, CHUNKS - 1)
    finish_columns(CHUNKS - 1)

    for b in range(TC):
        held = table_ref[COL_SLOT + child, b * GROUPS + group]
        for part in range(PARTS):
            total = jnp.zeros((PART, NB), jnp.float32)
            for slot in range(COL_SLOTS):
                tile = top_tile(slot * PARTS + part)
                total = jnp.where(lead_here & (held == slot), tile, total)
            top_own[b % 2, b // 2, part * PART:(part + 1) * PART] = total
    peer_copy().start()
    peer_copy().wait_recv()
    top_sum[...] = top_own[core] + top_peer[...]
    for i in range(1, RING):
        reduce_copy(i).start()
    send_rows(CHUNKS - 1, 1, RING)

    @pl.when(group != 0)
    def _():
        own_spread().wait_recv()

    def send_share(i, carry):
        @pl.when(lax.rem(group + i, GROUPS) != 0)
        def _():
            share_copy(i).start()
        return carry

    lax.fori_loop(1, GROUPS, send_share, 0)

    @pl.when(group != 0)
    def _():
        lead_copy(0).wait_recv()

    packed[...] = raw_lead[...]
    factor_tile(packed, lower, upper)

    for i in range(1, RING):
        reduce_copy(i).wait_recv()
    right_panel[core, at_z] = (
        top_sum[at_z] + top_got[turn(at_z, 1)] + top_got[turn(at_z, 2)] + top_got[turn(at_z, 3)]
    )
    for i in range(1, RING):
        top_share_copy(i).start()
    send_rows(CHUNKS - 1, RING, CHILDREN)
    for i in range(1, RING):
        top_share_copy(i).wait_recv()
    peer_share_copy().start()

    def finish_share(i, carry):
        @pl.when(lax.rem(group + i, GROUPS) != 0)
        def _():
            share_copy(i).wait_send()

        @pl.when(group != 0)
        def _():
            share_copy(i).wait_recv()

        @pl.when(group == 0)
        def _():
            lead_copy(i).wait_send()
            spread_copy(i).wait_send()

        return carry

    lax.fori_loop(1, GROUPS, finish_share, 0)

    @pl.when((group == 0) & (child == 0))
    def _():
        def sent_cast(k, carry):
            lead_cast_copy(k).wait_send()
            return carry

        lax.fori_loop(1, CHILDREN, sent_cast, 0)

    @pl.when((group == 0) & (child != 0))
    def _():
        lead_part_copy(child).wait_send()

    peer_copy().wait_send()
    for i in range(1, RING):
        reduce_copy(i).wait_send()
        top_share_copy(i).wait_send()

    for chunk in range(CHUNKS):
        def sent_columns(i, carry):
            column_copy(chunk, i).wait_send()
            return carry

        lax.fori_loop(1, GROUPS, sent_columns, 0)

    for chunk in range(PARTS, CHUNKS):
        finish_rows(chunk)
    peer_share_copy().wait()

    for chunk in range(CHUNKS):
        def sent_rows(i, carry):
            row_copy(chunk, i).wait_send()
            return carry

        lax.fori_loop(1, CHILDREN, sent_rows, 0)


def exchange(table, front, left, right, lead_block, diag, pivots):
    tile = jax.ShapeDtypeStruct((NB, NB), jnp.float32)
    dma = pltpu.SemaphoreType.DMA
    return pl.pallas_call(
        exchange_kernel,
        out_shape=(
            jax.ShapeDtypeStruct((CHUNKS, CHILDREN, ROW_SLOTS * PART, NB), jnp.float32),
            jax.ShapeDtypeStruct((TR, NB, NB), jnp.float32),
            jax.ShapeDtypeStruct((2, RING, NB, NB), jnp.float32),
            tile, tile, tile,
        ),
        in_specs=[SMEM, ANY, ANY, ANY, VMEM, VMEM, VMEM],
        out_specs=(ANY, VMEM, VMEM, VMEM, VMEM, VMEM),
        scratch_shapes=[
            pltpu.VMEM((RING, ROWS, PIV), jnp.float32),
            pltpu.VMEM((RING, PIV, ROWS), jnp.float32),
            pltpu.VMEM((RING, RING, ROWS, ROWS), jnp.float32),
            pltpu.VMEM((RING, RING, ROWS, ROWS), jnp.float32),
            pltpu.VMEM((ROWS, CB), jnp.float32),
            pltpu.VMEM((CBT, 2, PARTS, PART, NB), jnp.float32),
            pltpu.VMEM((CHUNKS, GROUPS, 2, PART, NB), jnp.float32),
            pltpu.VMEM((CBT, PART, NB), jnp.float32),
            pltpu.VMEM((CBT, PART, NB), jnp.float32),
            pltpu.VMEM((CBT, PART, NB), jnp.float32),
            pltpu.VMEM((CBT, PART, NB), jnp.float32),
            pltpu.VMEM((CBT, PART, NB), jnp.float32),
            pltpu.VMEM((CBT, PART, NB), jnp.float32),
            pltpu.VMEM((CBT, PART, NB), jnp.float32),
            pltpu.VMEM((CBT, PART, NB), jnp.float32),
            pltpu.VMEM((CBT, PART, NB), jnp.float32),
            pltpu.VMEM((CBT, PART, NB), jnp.float32),
            pltpu.VMEM((CBT, PART, NB), jnp.float32),
            pltpu.VMEM((CBT, PART, NB), jnp.float32),
            pltpu.VMEM((CHUNKS, CHILDREN, ROW_SLOTS * PART, NB), jnp.float32),
            pltpu.VMEM((PARTS, CHILDREN, ROW_SLOTS, PART, NB), jnp.float32),
            pltpu.VMEM((NB, NB), jnp.float32),
            pltpu.VMEM((CHILDREN, NB, NB), jnp.float32),
            pltpu.VMEM((2, RING, NB, NB), jnp.float32),
            pltpu.VMEM((RING, NB, NB), jnp.float32),
            pltpu.VMEM((RING, NB, NB), jnp.float32),
            pltpu.VMEM((RING, NB, NB), jnp.float32),
            dma((PARTS * ROW_SLOTS,)), dma((12,)), dma((12,)), dma((16,)), dma((16,)),
            dma((CHUNKS * GROUPS,)), dma((CHUNKS * GROUPS,)), dma((CHUNKS,)),
            dma((CHUNKS * CHILDREN,)), dma((CHUNKS * CHILDREN,)), dma((CHUNKS,)),
            dma((1,)), dma((CHILDREN,)), dma((CHILDREN,)), dma((1,)), dma((GROUPS,)), dma((1,)),
            dma((GROUPS,)), dma((1,)), dma((GROUPS,)), dma((GROUPS,)),
            dma((2,)), dma((2,)), dma((RING,)), dma((RING,)), dma((RING,)), dma((RING,)),
        ],
        compiler_params=pltpu.CompilerParams(
            collective_id=0, has_side_effects=True, vmem_limit_bytes=60 * 2**20
        ),
        name="exchange",
    )(table, front, left, right, lead_block, diag, pivots)


def split(values):
    high = values.astype(jnp.bfloat16)
    return high, (values - high.astype(jnp.float32)).astype(jnp.bfloat16)


def update_kernel(table_ref, arrived_hbm, left_raw, right_panel,
                  packed, lower, upper, diag, pivots, out_ref,
                  right, right_parts, total, arrived, arrive_sem):
    step = pl.program_id(0)

    def load(chunk):
        return pltpu.make_async_copy(
            arrived_hbm.at[chunk], arrived.at[chunk], arrive_sem.at[chunk]
        )

    @pl.when(step == 0)
    def _():
        for chunk in range(CHUNKS):
            load(chunk).start()

    child = lax.axis_index("child")
    group = lax.axis_index("grp")
    rows = lax.broadcasted_iota(jnp.int32, (NB, NB), 0)
    cols = lax.broadcasted_iota(jnp.int32, (NB, NB), 1)

    @pl.when(step == 0)
    def _():
        for b in range(TC):
            right[:, b * NB:(b + 1) * NB] = right_panel[b % 2, b // 2]
        right[...] = full_dot(lower[...], permute_rows(pivots, right[...]))

        @pl.when(group == 0)
        def _():
            right[:, :NB] = jnp.zeros((NB, NB), jnp.float32)

        high, low = split(right[...])
        right_parts[0:NB] = high
        right_parts[NB:2 * NB] = low
        right_parts[2 * NB:] = high

    left = full_dot(left_raw[...].reshape(STEP * NB, NB), upper[...])
    high, low = split(left)
    left_parts = jnp.concatenate([high, high, low], axis=1)
    total[...] = -jnp.dot(left_parts, right_parts[...], preferred_element_type=jnp.float32)

    @pl.when(step == 0)
    def _():
        for chunk in range(CHUNKS):
            load(chunk).wait()

    def place(row, carry):
        a = step * STEP + row
        for k in range(CHILDREN):
            row_slot = table_ref[ROW_SLOT + k, a * CHILDREN + child]

            @pl.when(row_slot >= 0)
            def _():
                base = pl.multiple_of(row_slot * PART, PART)
                for b in range(TC):
                    col_slot = table_ref[COL_SLOT + k, b * GROUPS + group]

                    @pl.when(col_slot >= 0)
                    def _():
                        across = pl.ds(b * NB, NB)
                        for part in range(PARTS):
                            down = pl.ds(pl.multiple_of(row * NB, NB) + part * PART, PART)
                            tile = arrived[col_slot * PARTS + part, k, pl.ds(base, PART), :]
                            total[down, across] = total[down, across] + tile

        on_diag = (lax.rem(group, CHILDREN) == child) & (lax.rem(a, 2) == group // CHILDREN)

        @pl.when(on_diag)
        def _():
            across = pl.ds(pl.multiple_of((a // 2) * NB, NB), NB)
            down = pl.ds(pl.multiple_of(row * NB, NB), NB)
            entries = diag[pl.ds(a * CHILDREN + child, 1), :]
            total[down, across] = total[down, across] + jnp.where(rows == cols, entries, 0.0)

        return carry

    lax.fori_loop(0, STEP, place, 0)

    @pl.when(group == 0)
    def _():
        total[:, :NB] = left

    @pl.when((step == 0) & (child == 0))
    def _():
        total[:NB, :] = right[...]

        @pl.when(group == 0)
        def _():
            total[:NB, :NB] = packed[...]

    out_ref[0, :, 0, :] = total[...]


def update_front(table, arrived, left_raw, right_panel, packed, lower, upper, diag, pivots):
    return pl.pallas_call(
        update_kernel,
        grid=(TR // STEP,),
        out_shape=jax.ShapeDtypeStruct((1, TR * NB, 1, TC * NB), jnp.float32),
        in_specs=[
            SMEM, ANY,
            pl.BlockSpec((STEP, NB, NB), lambda a: (a, 0, 0)),
            VMEM, VMEM, VMEM, VMEM, VMEM, VMEM,
        ],
        out_specs=pl.BlockSpec((1, STEP * NB, 1, TC * NB), lambda a: (0, a, 0, 0)),
        scratch_shapes=[
            pltpu.VMEM((NB, TC * NB), jnp.float32),
            pltpu.VMEM((3 * NB, TC * NB), jnp.bfloat16),
            pltpu.VMEM((STEP * NB, TC * NB), jnp.float32),
            pltpu.VMEM((CHUNKS, CHILDREN, ROW_SLOTS * PART, NB), jnp.float32),
            pltpu.SemaphoreType.DMA((CHUNKS,)),
        ],
        compiler_params=pltpu.CompilerParams(vmem_limit_bytes=60 * 2**20),
        name="update_front",
    )(table, arrived, left_raw, right_panel, packed, lower, upper, diag, pivots)


def body(front_child, left_factor, right_factor, child_map, parent_diag, lead_block, pivots):
    diag = parent_diag.reshape(PT, NB)
    pivot_row = pivots.reshape(1, NB)
    table = slot_table(child_map)
    arrived, left_raw, right_panel, packed, lower, upper = exchange(
        table, front_child[0], left_factor[0], right_factor[0], lead_block, diag, pivot_row
    )
    return update_front(
        table, arrived, left_raw, right_panel, packed, lower, upper, diag, pivot_row
    )


def solution(mesh):
    in_specs = (
        P("child", "grp", None),
        P("child", "grp", None),
        P("child", None, "grp"),
        P(),
        P(),
        P(),
        P(),
    )
    out_specs = P("child", None, "grp", None)
    return jax.shard_map(body, mesh=mesh, in_specs=in_specs, out_specs=out_specs, check_vma=False)
```

```python
import jax
import jax.numpy as jnp
from jax import lax
from jax.experimental import pallas as pl
from jax.experimental.pallas import tpu as pltpu
from jax.sharding import PartitionSpec as P

NB = 128
CB = 4096
PIV = 1280
NP = 16384
CHILDREN = 8
GROUPS = 16
RING = 4
CBT = CB // NB
PT = NP // NB
TR = PT // CHILDREN
TC = PT // GROUPS
COL_SLOTS = 3
ROW_SLOTS = 6
PARTS = 4
PART = NB // PARTS
CHUNKS = COL_SLOTS * PARTS
STEP = 4
ROWS = CB // GROUPS
COL_SLOT = 0
ROW_SLOT = CHILDREN
COL_PICK = 2 * CHILDREN
ROW_PICK = COL_PICK + COL_SLOTS * CHILDREN
TABLE_ROWS = ROW_PICK + ROW_SLOTS * CHILDREN
MESH = pl.DeviceIdType.MESH
ANY = pl.BlockSpec(memory_space=pl.ANY)
VMEM = pl.BlockSpec(memory_space=pltpu.VMEM)
SMEM = pl.BlockSpec(memory_space=pltpu.SMEM)


def full_dot(a, b):
    return jnp.dot(a, b, precision=lax.Precision.HIGHEST, preferred_element_type=jnp.float32)


def permute_columns(pivots, values):
    rows = lax.broadcasted_iota(jnp.int32, (NB, NB), 0)
    chosen = jnp.where(rows == pivots[...], 1.0, 0.0)
    return lax.dot_general(
        values, chosen, (((1,), (1,)), ((), ())),
        precision=lax.Precision.HIGHEST, preferred_element_type=jnp.float32,
    )


def table_kernel(map_ref, table_ref):
    lanes = lax.broadcasted_iota(jnp.int32, (CHILDREN, PT), 1)
    tiles = map_ref[...]
    source = jnp.full((CHILDREN, PT), -1, jnp.int32)
    for t in range(CBT):
        source = jnp.where(tiles[:, t:t + 1] == lanes, t, source)
    held = (source >= 0).astype(jnp.int32)

    def fill(classes, capacity, slot_base, pick_base):
        rank = jnp.zeros((CHILDREN, PT), jnp.int32)
        for shift in range(classes, PT, classes):
            rank = rank + jnp.where(lanes >= shift, pltpu.roll(held, shift, 1), 0)
        slots = jnp.where(held > 0, rank, -1)
        table_ref[slot_base:slot_base + CHILDREN] = slots
        for slot in range(capacity):
            picked = jnp.where(slots == slot, source, 0)
            shift = classes
            while shift < PT:
                picked = picked + pltpu.roll(picked, shift, 1)
                shift *= 2
            base = pick_base + slot * CHILDREN
            table_ref[base:base + CHILDREN] = picked

    fill(GROUPS, COL_SLOTS, COL_SLOT, COL_PICK)
    fill(CHILDREN, ROW_SLOTS, ROW_SLOT, ROW_PICK)


def slot_table(child_map):
    return pl.pallas_call(
        table_kernel,
        out_shape=jax.ShapeDtypeStruct((TABLE_ROWS, PT), jnp.int32),
        name="slot_table",
    )(child_map)


def permute_rows(pivots, values):
    rows = lax.broadcasted_iota(jnp.int32, (NB, NB), 0)
    chosen = jnp.where(rows == pivots[...], 1.0, 0.0)
    return lax.dot_general(
        chosen, values, (((0,), (0,)), ((), ())),
        precision=lax.Precision.HIGHEST, preferred_element_type=jnp.float32,
    )


def factor_tile(packed_ref, lower_ref, upper_ref):
    rows = lax.broadcasted_iota(jnp.int32, (NB, NB), 0)
    cols = lax.broadcasted_iota(jnp.int32, (NB, NB), 1)
    lane = lax.broadcasted_iota(jnp.int32, (1, NB), 1)
    eye = jnp.where(rows == cols, 1.0, 0.0)
    lower_ref[...] = eye
    upper_ref[...] = eye

    def eliminate(j, carry):
        working = packed_ref[...]
        upper = upper_ref[...]
        row_part = packed_ref[pl.ds(j, 1), :]
        row_lower = lower_ref[pl.ds(j, 1), :]
        column = jnp.sum(jnp.where(cols == j, working, 0.0), axis=1, keepdims=True)
        column_upper = jnp.sum(jnp.where(cols == j, upper, 0.0), axis=1, keepdims=True)
        pivot_value = jnp.sum(jnp.where(lane == j, row_part, 0.0), axis=1, keepdims=True)
        multiplier = jnp.where(rows[:, :1] > j, column / pivot_value, 0.0)
        right = jnp.where(lane > j, row_part, 0.0)
        packed_ref[...] = jnp.where(
            (cols == j) & (rows > j), multiplier, working - multiplier * right
        )
        lower_ref[...] = lower_ref[...] - multiplier * row_lower
        scaled = column_upper / pivot_value
        upper_ref[...] = jnp.where(cols == j, scaled, upper - scaled * right)
        return carry

    lax.fori_loop(0, NB, eliminate, 0)


def exchange_kernel(table_ref, front_hbm, left_hbm, right_hbm, lead_block, diag, pivots,
                    arrived, left_panel, right_panel, packed, lower, upper,
                    lefts, rights, products, returned, front, contribution, col_chosen,
                    column_0, column_1, column_2, column_3, column_4, column_5,
                    column_6, column_7, column_8, column_9, column_10, column_11,
                    row_chosen, first_column, raw_lead, lead_parts,
                    top_own, top_peer, top_sum, top_got,
                    load_sem, ring_send, ring_recv, back_send, back_recv, col_send, col_recv, own_col_sem,
                    row_send, row_recv, own_row_sem,
                    lead_part_send, lead_part_recv, lead_cast_send, lead_cast_recv, lead_send, lead_recv,
                    spread_send, spread_recv, share_send, share_recv,
                    peer_send, peer_recv, reduce_send, reduce_recv, top_send, top_recv):
    by_column = (
        column_0, column_1, column_2, column_3, column_4, column_5,
        column_6, column_7, column_8, column_9, column_10, column_11,
    )
    child = lax.axis_index("child")
    group = lax.axis_index("grp")
    core = lax.rem(child, 2)
    at_y, at_x = group // RING, lax.rem(group, RING)
    along = jnp.where(core == 0, at_x, at_y)
    across = jnp.where(core == 0, at_y, at_x)

    load_right = pltpu.make_async_copy(right_hbm, rights.at[across], load_sem.at[0])
    load_left = pltpu.make_async_copy(left_hbm, lefts.at[along], load_sem.at[1])
    load_front = pltpu.make_async_copy(front_hbm, front, load_sem.at[2])
    load_right.start()
    load_left.start()
    load_front.start()

    barrier = pltpu.get_barrier_semaphore()

    def greet_group(i, carry):
        pl.semaphore_signal(
            barrier, inc=1, device_id=(child, lax.rem(group + i, GROUPS)), device_id_type=MESH
        )
        return carry

    def greet_child(i, carry):
        pl.semaphore_signal(
            barrier, inc=1, device_id=(lax.rem(child + i, CHILDREN), group), device_id_type=MESH
        )
        return carry

    lax.fori_loop(1, GROUPS, greet_group, 0)
    lax.fori_loop(1, CHILDREN, greet_child, 0)
    pl.semaphore_wait(barrier, GROUPS + CHILDREN - 2)

    def turn(position, by):
        return lax.rem(position + by + RING, RING)

    def place(u, v):
        return jnp.where(core == 0, v * RING + u, u * RING + v)

    gathers = {}

    def make(key, blocks, block, chunk, target):
        number = len(gathers)
        size = blocks.shape[1] // 2
        ref = blocks.at[block, pl.ds(chunk * size, size)]
        gathers[key] = pltpu.make_async_remote_copy(
            src_ref=ref, dst_ref=ref, send_sem=ring_send.at[number], recv_sem=ring_recv.at[number],
            device_id=(child, target), device_id_type=MESH,
        )

    for name, blocks, at in (("l", lefts, along), ("r", rights, across)):
        for way in (1, -1):
            target = place(turn(along, way), across) if name == "l" else place(along, turn(across, way))
            first = 0 if way == 1 else 1
            make((name, way, 0), blocks, at, first, target)
            make((name, way, 1), blocks, at, 1 - first, target)
            make((name, way, 2), blocks, turn(at, -way), first, target)

    def start(name, step):
        gathers[(name, 1, step)].start()
        gathers[(name, -1, step)].start()

    def arrive(name, step):
        gathers[(name, 1, step)].wait_recv()
        gathers[(name, -1, step)].wait_recv()

    def return_copy(to, piece):
        target = turn(along, to)
        number = to * RING + piece
        return pltpu.make_async_remote_copy(
            src_ref=products.at[target, piece], dst_ref=returned.at[along, piece],
            send_sem=back_send.at[number], recv_sem=back_recv.at[number],
            device_id=(child, place(target, across)), device_id_type=MESH,
        )

    def multiply(pairs):
        def one(i, carry):
            to, line = jnp.int32(0), jnp.int32(0)
            for number, (pair_to, pair_line) in enumerate(pairs):
                to = jnp.where(i == number, pair_to, to)
                line = jnp.where(i == number, pair_line, line)
            target, piece = turn(along, to), turn(across, line)
            product = full_dot(lefts[target], rights[piece])

            @pl.when(to == 0)
            def _():
                returned[along, piece] = product

            @pl.when(to != 0)
            def _():
                products[target, piece] = product
                return_copy(to, piece).start()

            return carry

        lax.fori_loop(0, len(pairs), one, 0)

    load_left.wait()
    start("l", 0)
    load_right.wait()
    start("r", 0)
    start("l", 1)
    start("r", 1)
    multiply([(0, 0)])
    arrive("l", 0)
    start("l", 2)
    arrive("r", 0)
    start("r", 2)
    arrive("l", 1)
    multiply([(1, 0), (3, 0)])
    arrive("r", 1)
    multiply([(1, 1), (3, 1), (1, 3), (3, 3), (0, 1), (0, 3)])
    arrive("l", 2)
    multiply([(2, 0), (2, 1), (2, 3)])
    arrive("r", 2)
    multiply([(2, 2), (1, 2), (3, 2), (0, 2)])
    load_front.wait()

    def subtract(source, piece):
        block = place(source, piece)
        base = pl.multiple_of(block * ROWS, ROWS)
        result = front[:, pl.ds(base, ROWS)] - returned[source, piece]
        contribution[2 * block] = result[:, :NB].reshape(2, PARTS, PART, NB)
        contribution[2 * block + 1] = result[:, NB:].reshape(2, PARTS, PART, NB)

    def subtract_own(piece, carry):
        subtract(along, piece)
        return carry

    lax.fori_loop(0, RING, subtract_own, 0)

    def subtract_returned(number, carry):
        to, line = 1 + number // RING, turn(across, lax.rem(number, RING))
        return_copy(to, line).wait_recv()
        subtract(turn(along, -to), line)
        return carry

    lax.fori_loop(0, (RING - 1) * RING, subtract_returned, 0)

    def column_copy(chunk, i):
        target = lax.rem(group + i, GROUPS)
        return pltpu.make_async_remote_copy(
            src_ref=col_chosen.at[chunk, target],
            dst_ref=by_column[chunk].at[pl.ds(2 * group, 2)],
            send_sem=col_send.at[chunk * GROUPS + i], recv_sem=col_recv.at[chunk * GROUPS + i],
            device_id=(child, target), device_id_type=MESH,
        )

    def own_column_copy(chunk):
        return pltpu.make_async_copy(
            col_chosen.at[chunk, group], by_column[chunk].at[pl.ds(2 * group, 2)],
            own_col_sem.at[chunk],
        )

    def select_column(chunk, target):
        slot, part = chunk // PARTS, chunk % PARTS
        picked = table_ref[COL_PICK + slot * CHILDREN + child, target]
        for row in range(2):
            col_chosen[chunk, target, row] = contribution[picked, row, part]

    def pass_columns(chunk):
        def send_column(i, carry):
            select_column(chunk, lax.rem(group + i, GROUPS))
            column_copy(chunk, i).start()
            return carry

        lax.fori_loop(1, GROUPS, send_column, 0)
        select_column(chunk, group)
        own_column_copy(chunk).start()

    for chunk in range(CHUNKS):
        pass_columns(chunk)

    for key in gathers:
        gathers[key].wait_send()

    def sent_back(number, carry):
        return_copy(1 + number // RING, lax.rem(number, RING)).wait_send()
        return carry

    lax.fori_loop(0, (RING - 1) * RING, sent_back, 0)

    def row_copy(chunk, i):
        target = lax.rem(child + i, CHILDREN)
        return pltpu.make_async_remote_copy(
            src_ref=row_chosen.at[chunk, target], dst_ref=arrived.at[chunk, child],
            send_sem=row_send.at[chunk * CHILDREN + i], recv_sem=row_recv.at[chunk * CHILDREN + i],
            device_id=(target, group), device_id_type=MESH,
        )

    def own_row_copy(chunk):
        return pltpu.make_async_copy(
            row_chosen.at[chunk, child], arrived.at[chunk, child], own_row_sem.at[chunk]
        )

    def select_rows(chunk, target):
        for r in range(ROW_SLOTS):
            tile = by_column[chunk][table_ref[ROW_PICK + r * CHILDREN + child, target]]
            row_chosen[chunk, target, pl.ds(r * PART, PART)] = tile

    def finish_columns(chunk):
        def finish(i, carry):
            column_copy(chunk, i).wait_recv()
            return carry

        lax.fori_loop(1, GROUPS, finish, 0)
        own_column_copy(chunk).wait()

    def send_rows(chunk, first=1, last=CHILDREN):
        def send(i, carry):
            select_rows(chunk, lax.rem(child + i, CHILDREN))
            row_copy(chunk, i).start()
            return carry

        lax.fori_loop(first, last, send, 0)
        if last == CHILDREN:
            select_rows(chunk, child)
            own_row_copy(chunk).start()

    def finish_rows(chunk):
        def finish(i, carry):
            row_copy(chunk, i).wait_recv()
            return carry

        lax.fori_loop(1, CHILDREN, finish, 0)
        own_row_copy(chunk).wait()

    def top_tile(chunk):
        return by_column[chunk][table_ref[ROW_PICK + child, 0]]

    lead_here = table_ref[COL_SLOT + child, 0] >= 0

    def lead_part_copy(source):
        return pltpu.make_async_remote_copy(
            src_ref=lead_parts.at[source], dst_ref=lead_parts.at[source],
            send_sem=lead_part_send.at[0], recv_sem=lead_part_recv.at[source],
            device_id=(0, group), device_id_type=MESH,
        )

    def lead_cast_copy(target):
        return pltpu.make_async_remote_copy(
            src_ref=raw_lead, dst_ref=raw_lead,
            send_sem=lead_cast_send.at[target], recv_sem=lead_cast_recv.at[0],
            device_id=(target, group), device_id_type=MESH,
        )

    def lead_copy(target):
        return pltpu.make_async_remote_copy(
            src_ref=raw_lead, dst_ref=raw_lead,
            send_sem=lead_send.at[target], recv_sem=lead_recv.at[0],
            device_id=(child, target), device_id_type=MESH,
        )

    def send_lead_part():
        for part in range(PARTS):
            tile = jnp.where(lead_here, top_tile(part), 0.0)
            lead_parts[child, pl.ds(part * PART, PART)] = tile

        @pl.when(child != 0)
        def _():
            lead_part_copy(child).start()

    def sum_lead():
        def arrive_part(k, carry):
            lead_part_copy(k).wait_recv()
            return carry

        lax.fori_loop(1, CHILDREN, arrive_part, 0)
        rows = lax.broadcasted_iota(jnp.int32, (NB, NB), 0)
        cols = lax.broadcasted_iota(jnp.int32, (NB, NB), 1)
        total = lead_block[...] + jnp.where(rows == cols, diag[0:1, :], 0.0)
        for k in range(CHILDREN):
            total = total + lead_parts[k]
        raw_lead[...] = permute_rows(pivots, total)

        def cast(k, carry):
            lead_cast_copy(k).start()
            return carry

        lax.fori_loop(1, CHILDREN, cast, 0)

    def pass_lead():
        @pl.when(child != 0)
        def _():
            lead_cast_copy(0).wait_recv()

        def send_lead(i, carry):
            lead_copy(i).start()
            return carry

        lax.fori_loop(1, GROUPS, send_lead, 0)

    def spread_copy(target):
        return pltpu.make_async_remote_copy(
            src_ref=left_panel.at[target], dst_ref=left_panel.at[target],
            send_sem=spread_send.at[target], recv_sem=spread_recv.at[0],
            device_id=(child, target), device_id_type=MESH,
        )

    def own_spread():
        return pltpu.make_async_remote_copy(
            src_ref=left_panel.at[group], dst_ref=left_panel.at[group],
            send_sem=spread_send.at[0], recv_sem=spread_recv.at[0],
            device_id=(child, 0), device_id_type=MESH,
        )

    def share_copy(i):
        return pltpu.make_async_remote_copy(
            src_ref=left_panel.at[group], dst_ref=left_panel.at[group],
            send_sem=share_send.at[i], recv_sem=share_recv.at[i],
            device_id=(child, lax.rem(group + i, GROUPS)), device_id_type=MESH,
        )

    at_z = child // 2
    partner = child + 1 - 2 * core

    def peer_copy():
        return pltpu.make_async_remote_copy(
            src_ref=top_own.at[1 - core], dst_ref=top_peer,
            send_sem=peer_send.at[0], recv_sem=peer_recv.at[0],
            device_id=(partner, group), device_id_type=MESH,
        )

    def reduce_copy(i):
        target = turn(at_z, i)
        return pltpu.make_async_remote_copy(
            src_ref=top_sum.at[target], dst_ref=top_got.at[at_z],
            send_sem=reduce_send.at[i], recv_sem=reduce_recv.at[i],
            device_id=(2 * target + core, group), device_id_type=MESH,
        )

    def top_share_copy(i):
        target = turn(at_z, i)
        return pltpu.make_async_remote_copy(
            src_ref=right_panel.at[core, at_z], dst_ref=right_panel.at[core, at_z],
            send_sem=top_send.at[i], recv_sem=top_recv.at[i],
            device_id=(2 * target + core, group), device_id_type=MESH,
        )

    def peer_share_copy():
        return pltpu.make_async_remote_copy(
            src_ref=right_panel.at[core], dst_ref=right_panel.at[core],
            send_sem=peer_send.at[1], recv_sem=peer_recv.at[1],
            device_id=(partner, group), device_id_type=MESH,
        )

    def pass_chunks(first, last):
        for chunk in range(first, last):
            finish_columns(chunk)
            send_rows(chunk)

    pass_chunks(0, PARTS - 1)
    finish_columns(PARTS - 1)

    @pl.when(group == 0)
    def _():
        send_lead_part()

    send_rows(PARTS - 1)
    pass_chunks(PARTS, 3 * PARTS // 2 - 1)
    finish_columns(3 * PARTS // 2 - 1)

    @pl.when((group == 0) & (child == 0))
    def _():
        sum_lead()

    send_rows(3 * PARTS // 2 - 1)
    pass_chunks(3 * PARTS // 2, 2 * PARTS)

    @pl.when(group == 0)
    def _():
        pass_lead()

    for part in range(PARTS):
        finish_rows(part)

    @pl.when(group == 0)
    def _():
        loads = [
            pltpu.make_async_copy(
                arrived.at[part, :, pl.ds(r * PART, PART), :], first_column.at[part, :, r],
                load_sem.at[part * ROW_SLOTS + r],
            )
            for part in range(PARTS) for r in range(ROW_SLOTS)
        ]
        for load in loads:
            load.start()
        for load in loads:
            load.wait()

        def assemble(i, carry):
            a = lax.rem(i, TR)
            for part in range(PARTS):
                total = jnp.zeros((PART, NB), jnp.float32)
                for k in range(CHILDREN):
                    slot = table_ref[ROW_SLOT + k, a * CHILDREN + child]
                    held = (slot >= 0) & (table_ref[COL_SLOT + k, 0] >= 0)
                    tile = first_column[part, k, jnp.maximum(slot, 0)]
                    total = total + jnp.where(held, tile, 0.0)
                left_panel[a, part * PART:(part + 1) * PART] = total

            @pl.when(a > 0)
            def _():
                spread_copy(a).start()

            return carry

        lax.fori_loop(1, TR + 1, assemble, 0)

    pass_chunks(2 * PARTS, CHUNKS - 1)
    finish_columns(CHUNKS - 1)

    for b in range(TC):
        held = table_ref[COL_SLOT + child, b * GROUPS + group]
        for part in range(PARTS):
            total = jnp.zeros((PART, NB), jnp.float32)
            for slot in range(COL_SLOTS):
                tile = top_tile(slot * PARTS + part)
                total = jnp.where(lead_here & (held == slot), tile, total)
            top_own[b % 2, b // 2, part * PART:(part + 1) * PART] = total
    peer_copy().start()
    peer_copy().wait_recv()
    top_sum[...] = top_own[core] + top_peer[...]
    for i in range(1, RING):
        reduce_copy(i).start()
    send_rows(CHUNKS - 1, 1, RING)

    @pl.when(group != 0)
    def _():
        own_spread().wait_recv()

    def send_share(i, carry):
        @pl.when(lax.rem(group + i, GROUPS) != 0)
        def _():
            share_copy(i).start()
        return carry

    lax.fori_loop(1, GROUPS, send_share, 0)

    @pl.when(group != 0)
    def _():
        lead_copy(0).wait_recv()

    packed[...] = raw_lead[...]
    factor_tile(packed, lower, upper)

    def finish_share(i, carry):
        @pl.when(lax.rem(group + i, GROUPS) != 0)
        def _():
            share_copy(i).wait_send()

        @pl.when(group != 0)
        def _():
            share_copy(i).wait_recv()

        @pl.when(group == 0)
        def _():
            lead_copy(i).wait_send()
            spread_copy(i).wait_send()

        return carry

    lax.fori_loop(1, GROUPS, finish_share, 0)

    for quarter in range(TR // STEP):
        span = slice(quarter * STEP, (quarter + 1) * STEP)
        raw = left_panel[span].reshape(STEP * NB, NB)
        left_panel[span] = full_dot(raw, upper[...]).reshape(STEP, NB, NB)
    lower[...] = permute_columns(pivots, lower[...])

    for i in range(1, RING):
        reduce_copy(i).wait_recv()
    right_panel[core, at_z] = (
        top_sum[at_z] + top_got[turn(at_z, 1)] + top_got[turn(at_z, 2)] + top_got[turn(at_z, 3)]
    )
    for i in range(1, RING):
        top_share_copy(i).start()
    send_rows(CHUNKS - 1, RING, CHILDREN)
    for i in range(1, RING):
        top_share_copy(i).wait_recv()
    peer_share_copy().start()

    @pl.when((group == 0) & (child == 0))
    def _():
        def sent_cast(k, carry):
            lead_cast_copy(k).wait_send()
            return carry

        lax.fori_loop(1, CHILDREN, sent_cast, 0)

    @pl.when((group == 0) & (child != 0))
    def _():
        lead_part_copy(child).wait_send()

    peer_copy().wait_send()
    for i in range(1, RING):
        reduce_copy(i).wait_send()
        top_share_copy(i).wait_send()

    for chunk in range(CHUNKS):
        def sent_columns(i, carry):
            column_copy(chunk, i).wait_send()
            return carry

        lax.fori_loop(1, GROUPS, sent_columns, 0)

    for chunk in range(PARTS, CHUNKS):
        finish_rows(chunk)
    peer_share_copy().wait()

    for chunk in range(CHUNKS):
        def sent_rows(i, carry):
            row_copy(chunk, i).wait_send()
            return carry

        lax.fori_loop(1, CHILDREN, sent_rows, 0)


def exchange(table, front, left, right, lead_block, diag, pivots):
    tile = jax.ShapeDtypeStruct((NB, NB), jnp.float32)
    dma = pltpu.SemaphoreType.DMA
    return pl.pallas_call(
        exchange_kernel,
        out_shape=(
            jax.ShapeDtypeStruct((CHUNKS, CHILDREN, ROW_SLOTS * PART, NB), jnp.float32),
            jax.ShapeDtypeStruct((TR, NB, NB), jnp.float32),
            jax.ShapeDtypeStruct((2, RING, NB, NB), jnp.float32),
            tile, tile, tile,
        ),
        in_specs=[SMEM, ANY, ANY, ANY, VMEM, VMEM, VMEM],
        out_specs=(ANY, VMEM, VMEM, VMEM, VMEM, VMEM),
        scratch_shapes=[
            pltpu.VMEM((RING, ROWS, PIV), jnp.float32),
            pltpu.VMEM((RING, PIV, ROWS), jnp.float32),
            pltpu.VMEM((RING, RING, ROWS, ROWS), jnp.float32),
            pltpu.VMEM((RING, RING, ROWS, ROWS), jnp.float32),
            pltpu.VMEM((ROWS, CB), jnp.float32),
            pltpu.VMEM((CBT, 2, PARTS, PART, NB), jnp.float32),
            pltpu.VMEM((CHUNKS, GROUPS, 2, PART, NB), jnp.float32),
            pltpu.VMEM((CBT, PART, NB), jnp.float32),
            pltpu.VMEM((CBT, PART, NB), jnp.float32),
            pltpu.VMEM((CBT, PART, NB), jnp.float32),
            pltpu.VMEM((CBT, PART, NB), jnp.float32),
            pltpu.VMEM((CBT, PART, NB), jnp.float32),
            pltpu.VMEM((CBT, PART, NB), jnp.float32),
            pltpu.VMEM((CBT, PART, NB), jnp.float32),
            pltpu.VMEM((CBT, PART, NB), jnp.float32),
            pltpu.VMEM((CBT, PART, NB), jnp.float32),
            pltpu.VMEM((CBT, PART, NB), jnp.float32),
            pltpu.VMEM((CBT, PART, NB), jnp.float32),
            pltpu.VMEM((CBT, PART, NB), jnp.float32),
            pltpu.VMEM((CHUNKS, CHILDREN, ROW_SLOTS * PART, NB), jnp.float32),
            pltpu.VMEM((PARTS, CHILDREN, ROW_SLOTS, PART, NB), jnp.float32),
            pltpu.VMEM((NB, NB), jnp.float32),
            pltpu.VMEM((CHILDREN, NB, NB), jnp.float32),
            pltpu.VMEM((2, RING, NB, NB), jnp.float32),
            pltpu.VMEM((RING, NB, NB), jnp.float32),
            pltpu.VMEM((RING, NB, NB), jnp.float32),
            pltpu.VMEM((RING, NB, NB), jnp.float32),
            dma((PARTS * ROW_SLOTS,)), dma((12,)), dma((12,)), dma((16,)), dma((16,)),
            dma((CHUNKS * GROUPS,)), dma((CHUNKS * GROUPS,)), dma((CHUNKS,)),
            dma((CHUNKS * CHILDREN,)), dma((CHUNKS * CHILDREN,)), dma((CHUNKS,)),
            dma((1,)), dma((CHILDREN,)), dma((CHILDREN,)), dma((1,)), dma((GROUPS,)), dma((1,)),
            dma((GROUPS,)), dma((1,)), dma((GROUPS,)), dma((GROUPS,)),
            dma((2,)), dma((2,)), dma((RING,)), dma((RING,)), dma((RING,)), dma((RING,)),
        ],
        compiler_params=pltpu.CompilerParams(
            collective_id=0, has_side_effects=True, vmem_limit_bytes=60 * 2**20
        ),
        name="exchange",
    )(table, front, left, right, lead_block, diag, pivots)


def split(values):
    high = values.astype(jnp.bfloat16)
    return high, (values - high.astype(jnp.float32)).astype(jnp.bfloat16)


def update_kernel(table_ref, arrived_hbm, left_raw, right_panel,
                  packed, lower, diag, out_ref,
                  right, right_parts, total, arrived, arrive_sem):
    step = pl.program_id(0)

    def load(chunk):
        return pltpu.make_async_copy(
            arrived_hbm.at[chunk], arrived.at[chunk], arrive_sem.at[chunk]
        )

    @pl.when(step == 0)
    def _():
        for chunk in range(CHUNKS):
            load(chunk).start()

    child = lax.axis_index("child")
    group = lax.axis_index("grp")
    rows = lax.broadcasted_iota(jnp.int32, (NB, NB), 0)
    cols = lax.broadcasted_iota(jnp.int32, (NB, NB), 1)

    @pl.when(step == 0)
    def _():
        for b in range(TC):
            right[:, b * NB:(b + 1) * NB] = right_panel[b % 2, b // 2]
        right[...] = full_dot(lower[...], right[...])

        @pl.when(group == 0)
        def _():
            right[:, :NB] = jnp.zeros((NB, NB), jnp.float32)

        high, low = split(right[...])
        right_parts[0:NB] = high
        right_parts[NB:2 * NB] = low
        right_parts[2 * NB:] = high

    left = left_raw[...].reshape(STEP * NB, NB)
    high, low = split(left)
    left_parts = jnp.concatenate([high, high, low], axis=1)
    total[...] = -jnp.dot(left_parts, right_parts[...], preferred_element_type=jnp.float32)

    @pl.when(step == 0)
    def _():
        for chunk in range(CHUNKS):
            load(chunk).wait()

    def place(row, carry):
        a = step * STEP + row
        for k in range(CHILDREN):
            row_slot = table_ref[ROW_SLOT + k, a * CHILDREN + child]

            @pl.when(row_slot >= 0)
            def _():
                base = pl.multiple_of(row_slot * PART, PART)
                for b in range(TC):
                    col_slot = table_ref[COL_SLOT + k, b * GROUPS + group]

                    @pl.when(col_slot >= 0)
                    def _():
                        across = pl.ds(b * NB, NB)
                        for part in range(PARTS):
                            down = pl.ds(pl.multiple_of(row * NB, NB) + part * PART, PART)
                            tile = arrived[col_slot * PARTS + part, k, pl.ds(base, PART), :]
                            total[down, across] = total[down, across] + tile

        on_diag = (lax.rem(group, CHILDREN) == child) & (lax.rem(a, 2) == group // CHILDREN)

        @pl.when(on_diag)
        def _():
            across = pl.ds(pl.multiple_of((a // 2) * NB, NB), NB)
            down = pl.ds(pl.multiple_of(row * NB, NB), NB)
            entries = diag[pl.ds(a * CHILDREN + child, 1), :]
            total[down, across] = total[down, across] + jnp.where(rows == cols, entries, 0.0)

        return carry

    lax.fori_loop(0, STEP, place, 0)

    @pl.when(group == 0)
    def _():
        total[:, :NB] = left

    @pl.when((step == 0) & (child == 0))
    def _():
        total[:NB, :] = right[...]

        @pl.when(group == 0)
        def _():
            total[:NB, :NB] = packed[...]

    out_ref[0, :, 0, :] = total[...]


def update_front(table, arrived, left_raw, right_panel, packed, lower, diag):
    return pl.pallas_call(
        update_kernel,
        grid=(TR // STEP,),
        out_shape=jax.ShapeDtypeStruct((1, TR * NB, 1, TC * NB), jnp.float32),
        in_specs=[
            SMEM, ANY,
            pl.BlockSpec((STEP, NB, NB), lambda a: (a, 0, 0)),
            VMEM, VMEM, VMEM, VMEM,
        ],
        out_specs=pl.BlockSpec((1, STEP * NB, 1, TC * NB), lambda a: (0, a, 0, 0)),
        scratch_shapes=[
            pltpu.VMEM((NB, TC * NB), jnp.float32),
            pltpu.VMEM((3 * NB, TC * NB), jnp.bfloat16),
            pltpu.VMEM((STEP * NB, TC * NB), jnp.float32),
            pltpu.VMEM((CHUNKS, CHILDREN, ROW_SLOTS * PART, NB), jnp.float32),
            pltpu.SemaphoreType.DMA((CHUNKS,)),
        ],
        compiler_params=pltpu.CompilerParams(vmem_limit_bytes=60 * 2**20),
        name="update_front",
    )(table, arrived, left_raw, right_panel, packed, lower, diag)


def body(front_child, left_factor, right_factor, child_map, parent_diag, lead_block, pivots):
    diag = parent_diag.reshape(PT, NB)
    pivot_row = pivots.reshape(1, NB)
    table = slot_table(child_map)
    arrived, left_raw, right_panel, packed, lower, _ = exchange(
        table, front_child[0], left_factor[0], right_factor[0], lead_block, diag, pivot_row
    )
    return update_front(table, arrived, left_raw, right_panel, packed, lower, diag)


def solution(mesh):
    in_specs = (
        P("child", "grp", None),
        P("child", "grp", None),
        P("child", None, "grp"),
        P(),
        P(),
        P(),
        P(),
    )
    out_specs = P("child", None, "grp", None)
    return jax.shard_map(body, mesh=mesh, in_specs=in_specs, out_specs=out_specs, check_vma=False)
```

```python
import jax
import jax.numpy as jnp
from jax import lax
from jax.experimental import pallas as pl
from jax.experimental.pallas import tpu as pltpu
from jax.sharding import PartitionSpec as P

NB = 128
CB = 4096
PIV = 1280
NP = 16384
CHILDREN = 8
GROUPS = 16
RING = 4
CBT = CB // NB
PT = NP // NB
TR = PT // CHILDREN
TC = PT // GROUPS
COL_SLOTS = 3
ROW_SLOTS = 6
PARTS = 4
PART = NB // PARTS
CHUNKS = COL_SLOTS * PARTS
STEP = 4
ROWS = CB // GROUPS
COL_SLOT = 0
ROW_SLOT = CHILDREN
COL_PICK = 2 * CHILDREN
ROW_PICK = COL_PICK + COL_SLOTS * CHILDREN
TABLE_ROWS = ROW_PICK + ROW_SLOTS * CHILDREN
MESH = pl.DeviceIdType.MESH
ANY = pl.BlockSpec(memory_space=pl.ANY)
VMEM = pl.BlockSpec(memory_space=pltpu.VMEM)
SMEM = pl.BlockSpec(memory_space=pltpu.SMEM)


def full_dot(a, b):
    return jnp.dot(a, b, precision=lax.Precision.HIGHEST, preferred_element_type=jnp.float32)


def permute_columns(pivots, values):
    rows = lax.broadcasted_iota(jnp.int32, (NB, NB), 0)
    chosen = jnp.where(rows == pivots[...], 1.0, 0.0)
    return lax.dot_general(
        values, chosen, (((1,), (1,)), ((), ())),
        precision=lax.Precision.HIGHEST, preferred_element_type=jnp.float32,
    )


def table_kernel(map_ref, table_ref):
    lanes = lax.broadcasted_iota(jnp.int32, (CHILDREN, PT), 1)
    tiles = map_ref[...]
    source = jnp.full((CHILDREN, PT), -1, jnp.int32)
    for t in range(CBT):
        source = jnp.where(tiles[:, t:t + 1] == lanes, t, source)
    held = (source >= 0).astype(jnp.int32)

    def fill(classes, capacity, slot_base, pick_base):
        rank = jnp.zeros((CHILDREN, PT), jnp.int32)
        for shift in range(classes, PT, classes):
            rank = rank + jnp.where(lanes >= shift, pltpu.roll(held, shift, 1), 0)
        slots = jnp.where(held > 0, rank, -1)
        table_ref[slot_base:slot_base + CHILDREN] = slots
        for slot in range(capacity):
            picked = jnp.where(slots == slot, source, 0)
            shift = classes
            while shift < PT:
                picked = picked + pltpu.roll(picked, shift, 1)
                shift *= 2
            base = pick_base + slot * CHILDREN
            table_ref[base:base + CHILDREN] = picked

    fill(GROUPS, COL_SLOTS, COL_SLOT, COL_PICK)
    fill(CHILDREN, ROW_SLOTS, ROW_SLOT, ROW_PICK)


def slot_table(child_map):
    return pl.pallas_call(
        table_kernel,
        out_shape=jax.ShapeDtypeStruct((TABLE_ROWS, PT), jnp.int32),
        name="slot_table",
    )(child_map)


def permute_rows(pivots, values):
    rows = lax.broadcasted_iota(jnp.int32, (NB, NB), 0)
    chosen = jnp.where(rows == pivots[...], 1.0, 0.0)
    return lax.dot_general(
        chosen, values, (((0,), (0,)), ((), ())),
        precision=lax.Precision.HIGHEST, preferred_element_type=jnp.float32,
    )


def factor_tile(packed_ref, lower_ref, upper_ref):
    rows = lax.broadcasted_iota(jnp.int32, (NB, NB), 0)
    cols = lax.broadcasted_iota(jnp.int32, (NB, NB), 1)
    lane = lax.broadcasted_iota(jnp.int32, (1, NB), 1)
    eye = jnp.where(rows == cols, 1.0, 0.0)
    lower_ref[...] = eye
    upper_ref[...] = eye

    def eliminate(j, carry):
        working = packed_ref[...]
        upper = upper_ref[...]
        row_part = packed_ref[pl.ds(j, 1), :]
        row_lower = lower_ref[pl.ds(j, 1), :]
        column = jnp.sum(jnp.where(cols == j, working, 0.0), axis=1, keepdims=True)
        column_upper = jnp.sum(jnp.where(cols == j, upper, 0.0), axis=1, keepdims=True)
        pivot_value = jnp.sum(jnp.where(lane == j, row_part, 0.0), axis=1, keepdims=True)
        multiplier = jnp.where(rows[:, :1] > j, column / pivot_value, 0.0)
        right = jnp.where(lane > j, row_part, 0.0)
        packed_ref[...] = jnp.where(
            (cols == j) & (rows > j), multiplier, working - multiplier * right
        )
        lower_ref[...] = lower_ref[...] - multiplier * row_lower
        scaled = column_upper / pivot_value
        upper_ref[...] = jnp.where(cols == j, scaled, upper - scaled * right)
        return carry

    lax.fori_loop(0, NB, eliminate, 0)


def exchange_kernel(table_ref, front_hbm, left_hbm, right_hbm, lead_block, diag, pivots,
                    arrived, left_panel, right_panel, packed, lower, upper,
                    lefts, rights, products, returned, front, contribution, col_chosen,
                    column_0, column_1, column_2, column_3, column_4, column_5,
                    column_6, column_7, column_8, column_9, column_10, column_11,
                    row_chosen, first_column, raw_lead, lead_parts,
                    top_own, top_peer, top_sum, top_got,
                    load_sem, ring_send, ring_recv, back_send, back_recv, col_send, col_recv, own_col_sem,
                    row_send, row_recv, own_row_sem,
                    lead_part_send, lead_part_recv, lead_cast_send, lead_cast_recv, lead_send, lead_recv,
                    spread_send, spread_recv, share_send, share_recv,
                    peer_send, peer_recv, reduce_send, reduce_recv, top_send, top_recv):
    by_column = (
        column_0, column_1, column_2, column_3, column_4, column_5,
        column_6, column_7, column_8, column_9, column_10, column_11,
    )
    child = lax.axis_index("child")
    group = lax.axis_index("grp")
    core = lax.rem(child, 2)
    at_y, at_x = group // RING, lax.rem(group, RING)
    along = jnp.where(core == 0, at_x, at_y)
    across = jnp.where(core == 0, at_y, at_x)

    load_right = pltpu.make_async_copy(right_hbm, rights.at[across], load_sem.at[0])
    load_left = pltpu.make_async_copy(left_hbm, lefts.at[along], load_sem.at[1])
    load_front = pltpu.make_async_copy(front_hbm, front, load_sem.at[2])
    load_right.start()
    load_left.start()
    load_front.start()

    barrier = pltpu.get_barrier_semaphore()

    def greet_group(i, carry):
        pl.semaphore_signal(
            barrier, inc=1, device_id=(child, lax.rem(group + i, GROUPS)), device_id_type=MESH
        )
        return carry

    def greet_child(i, carry):
        pl.semaphore_signal(
            barrier, inc=1, device_id=(lax.rem(child + i, CHILDREN), group), device_id_type=MESH
        )
        return carry

    lax.fori_loop(1, GROUPS, greet_group, 0)
    lax.fori_loop(1, CHILDREN, greet_child, 0)
    pl.semaphore_wait(barrier, GROUPS + CHILDREN - 2)

    def turn(position, by):
        return lax.rem(position + by + RING, RING)

    def place(u, v):
        return jnp.where(core == 0, v * RING + u, u * RING + v)

    gathers = {}

    def make(key, blocks, block, chunk, target, own=None):
        number = len(gathers)
        size = blocks.shape[1] // 2
        ref = blocks.at[block, pl.ds(chunk * size, size)]
        source = ref if own is None else own.at[pl.ds(chunk * size, size)]
        gathers[key] = pltpu.make_async_remote_copy(
            src_ref=source, dst_ref=ref, send_sem=ring_send.at[number], recv_sem=ring_recv.at[number],
            device_id=(child, target), device_id_type=MESH,
        )

    for name, blocks, at, own in (
        ("l", lefts, along, left_hbm), ("r", rights, across, right_hbm)
    ):
        for way in (1, -1):
            target = place(turn(along, way), across) if name == "l" else place(along, turn(across, way))
            first = 0 if way == 1 else 1
            make((name, way, 0), blocks, at, first, target, own)
            make((name, way, 1), blocks, at, 1 - first, target, own)
            make((name, way, 2), blocks, turn(at, -way), first, target)

    def start(name, step):
        gathers[(name, 1, step)].start()
        gathers[(name, -1, step)].start()

    def arrive(name, step):
        gathers[(name, 1, step)].wait_recv()
        gathers[(name, -1, step)].wait_recv()

    def return_copy(to, piece):
        target = turn(along, to)
        number = to * RING + piece
        return pltpu.make_async_remote_copy(
            src_ref=products.at[target, piece], dst_ref=returned.at[along, piece],
            send_sem=back_send.at[number], recv_sem=back_recv.at[number],
            device_id=(child, place(target, across)), device_id_type=MESH,
        )

    def multiply(pairs):
        def one(i, carry):
            to, line = jnp.int32(0), jnp.int32(0)
            for number, (pair_to, pair_line) in enumerate(pairs):
                to = jnp.where(i == number, pair_to, to)
                line = jnp.where(i == number, pair_line, line)
            target, piece = turn(along, to), turn(across, line)
            product = full_dot(lefts[target], rights[piece])

            @pl.when(to == 0)
            def _():
                returned[along, piece] = product

            @pl.when(to != 0)
            def _():
                products[target, piece] = product
                return_copy(to, piece).start()

            return carry

        lax.fori_loop(0, len(pairs), one, 0)

    start("l", 0)
    start("r", 0)
    start("l", 1)
    start("r", 1)
    load_left.wait()
    load_right.wait()
    multiply([(0, 0)])
    arrive("l", 0)
    start("l", 2)
    arrive("r", 0)
    start("r", 2)
    arrive("l", 1)
    multiply([(1, 0), (3, 0)])
    arrive("r", 1)
    multiply([(1, 1), (3, 1), (1, 3), (3, 3), (0, 1), (0, 3)])
    arrive("l", 2)
    multiply([(2, 0), (2, 1), (2, 3)])
    arrive("r", 2)
    multiply([(2, 2), (1, 2), (3, 2), (0, 2)])
    load_front.wait()

    def subtract(source, piece):
        block = place(source, piece)
        base = pl.multiple_of(block * ROWS, ROWS)
        result = front[:, pl.ds(base, ROWS)] - returned[source, piece]
        contribution[2 * block] = result[:, :NB].reshape(2, PARTS, PART, NB)
        contribution[2 * block + 1] = result[:, NB:].reshape(2, PARTS, PART, NB)

    def subtract_own(piece, carry):
        subtract(along, piece)
        return carry

    lax.fori_loop(0, RING, subtract_own, 0)

    def subtract_returned(number, carry):
        to, line = 1 + number // RING, turn(across, lax.rem(number, RING))
        return_copy(to, line).wait_recv()
        subtract(turn(along, -to), line)
        return carry

    lax.fori_loop(0, (RING - 1) * RING, subtract_returned, 0)

    def column_target(i):
        by = lax.rem(5 * i, GROUPS)
        return turn(at_y, by // RING) * RING + turn(at_x, lax.rem(by, RING))

    def column_copy(chunk, i):
        target = column_target(i)
        return pltpu.make_async_remote_copy(
            src_ref=col_chosen.at[chunk, target],
            dst_ref=by_column[chunk].at[pl.ds(2 * group, 2)],
            send_sem=col_send.at[chunk * GROUPS + i], recv_sem=col_recv.at[chunk * GROUPS + i],
            device_id=(child, target), device_id_type=MESH,
        )

    def own_column_copy(chunk):
        return pltpu.make_async_copy(
            col_chosen.at[chunk, group], by_column[chunk].at[pl.ds(2 * group, 2)],
            own_col_sem.at[chunk],
        )

    def select_column(chunk, target):
        slot, part = chunk // PARTS, chunk % PARTS
        picked = table_ref[COL_PICK + slot * CHILDREN + child, target]
        for row in range(2):
            col_chosen[chunk, target, row] = contribution[picked, row, part]

    def pass_columns(chunk):
        def send_column(i, carry):
            select_column(chunk, column_target(i))
            column_copy(chunk, i).start()
            return carry

        lax.fori_loop(1, GROUPS, send_column, 0)
        select_column(chunk, group)
        own_column_copy(chunk).start()

    for chunk in range(CHUNKS):
        pass_columns(chunk)

    for key in gathers:
        gathers[key].wait_send()

    def sent_back(number, carry):
        return_copy(1 + number // RING, lax.rem(number, RING)).wait_send()
        return carry

    lax.fori_loop(0, (RING - 1) * RING, sent_back, 0)

    def row_copy(chunk, i):
        target = lax.rem(child + i, CHILDREN)
        return pltpu.make_async_remote_copy(
            src_ref=row_chosen.at[chunk, target], dst_ref=arrived.at[chunk, child],
            send_sem=row_send.at[chunk * CHILDREN + i], recv_sem=row_recv.at[chunk * CHILDREN + i],
            device_id=(target, group), device_id_type=MESH,
        )

    def own_row_copy(chunk):
        return pltpu.make_async_copy(
            row_chosen.at[chunk, child], arrived.at[chunk, child], own_row_sem.at[chunk]
        )

    def select_rows(chunk, target):
        for r in range(ROW_SLOTS):
            tile = by_column[chunk][table_ref[ROW_PICK + r * CHILDREN + child, target]]
            row_chosen[chunk, target, pl.ds(r * PART, PART)] = tile

    def finish_columns(chunk):
        def finish(i, carry):
            column_copy(chunk, i).wait_recv()
            return carry

        lax.fori_loop(1, GROUPS, finish, 0)
        own_column_copy(chunk).wait()

    def send_rows(chunk, first=1, last=CHILDREN):
        def send(i, carry):
            select_rows(chunk, lax.rem(child + i, CHILDREN))
            row_copy(chunk, i).start()
            return carry

        lax.fori_loop(first, last, send, 0)
        if last == CHILDREN:
            select_rows(chunk, child)
            own_row_copy(chunk).start()

    def finish_rows(chunk):
        def finish(i, carry):
            row_copy(chunk, i).wait_recv()
            return carry

        lax.fori_loop(1, CHILDREN, finish, 0)
        own_row_copy(chunk).wait()

    def top_tile(chunk):
        return by_column[chunk][table_ref[ROW_PICK + child, 0]]

    lead_here = table_ref[COL_SLOT + child, 0] >= 0

    def lead_part_copy(source):
        return pltpu.make_async_remote_copy(
            src_ref=lead_parts.at[source], dst_ref=lead_parts.at[source],
            send_sem=lead_part_send.at[0], recv_sem=lead_part_recv.at[source],
            device_id=(0, group), device_id_type=MESH,
        )

    def lead_cast_copy(target):
        return pltpu.make_async_remote_copy(
            src_ref=raw_lead, dst_ref=raw_lead,
            send_sem=lead_cast_send.at[target], recv_sem=lead_cast_recv.at[0],
            device_id=(target, group), device_id_type=MESH,
        )

    def lead_copy(target):
        return pltpu.make_async_remote_copy(
            src_ref=raw_lead, dst_ref=raw_lead,
            send_sem=lead_send.at[target], recv_sem=lead_recv.at[0],
            device_id=(child, target), device_id_type=MESH,
        )

    def send_lead_part():
        for part in range(PARTS):
            tile = jnp.where(lead_here, top_tile(part), 0.0)
            lead_parts[child, pl.ds(part * PART, PART)] = tile

        @pl.when(child != 0)
        def _():
            lead_part_copy(child).start()

    def sum_lead():
        def arrive_part(k, carry):
            lead_part_copy(k).wait_recv()
            return carry

        lax.fori_loop(1, CHILDREN, arrive_part, 0)
        rows = lax.broadcasted_iota(jnp.int32, (NB, NB), 0)
        cols = lax.broadcasted_iota(jnp.int32, (NB, NB), 1)
        total = lead_block[...] + jnp.where(rows == cols, diag[0:1, :], 0.0)
        for k in range(CHILDREN):
            total = total + lead_parts[k]
        raw_lead[...] = permute_rows(pivots, total)

        def cast(k, carry):
            lead_cast_copy(k).start()
            return carry

        lax.fori_loop(1, CHILDREN, cast, 0)

    def pass_lead():
        @pl.when(child != 0)
        def _():
            lead_cast_copy(0).wait_recv()

        def send_lead(i, carry):
            lead_copy(i).start()
            return carry

        lax.fori_loop(1, GROUPS, send_lead, 0)

    def spread_copy(target):
        return pltpu.make_async_remote_copy(
            src_ref=left_panel.at[target], dst_ref=left_panel.at[target],
            send_sem=spread_send.at[target], recv_sem=spread_recv.at[0],
            device_id=(child, target), device_id_type=MESH,
        )

    def own_spread():
        return pltpu.make_async_remote_copy(
            src_ref=left_panel.at[group], dst_ref=left_panel.at[group],
            send_sem=spread_send.at[0], recv_sem=spread_recv.at[0],
            device_id=(child, 0), device_id_type=MESH,
        )

    def share_copy(i):
        return pltpu.make_async_remote_copy(
            src_ref=left_panel.at[group], dst_ref=left_panel.at[group],
            send_sem=share_send.at[i], recv_sem=share_recv.at[i],
            device_id=(child, lax.rem(group + i, GROUPS)), device_id_type=MESH,
        )

    at_z = child // 2
    partner = child + 1 - 2 * core

    def peer_copy():
        return pltpu.make_async_remote_copy(
            src_ref=top_own.at[1 - core], dst_ref=top_peer,
            send_sem=peer_send.at[0], recv_sem=peer_recv.at[0],
            device_id=(partner, group), device_id_type=MESH,
        )

    def reduce_copy(i):
        target = turn(at_z, i)
        return pltpu.make_async_remote_copy(
            src_ref=top_sum.at[target], dst_ref=top_got.at[at_z],
            send_sem=reduce_send.at[i], recv_sem=reduce_recv.at[i],
            device_id=(2 * target + core, group), device_id_type=MESH,
        )

    def top_share_copy(i):
        target = turn(at_z, i)
        return pltpu.make_async_remote_copy(
            src_ref=right_panel.at[core, at_z], dst_ref=right_panel.at[core, at_z],
            send_sem=top_send.at[i], recv_sem=top_recv.at[i],
            device_id=(2 * target + core, group), device_id_type=MESH,
        )

    def peer_share_copy():
        return pltpu.make_async_remote_copy(
            src_ref=right_panel.at[core], dst_ref=right_panel.at[core],
            send_sem=peer_send.at[1], recv_sem=peer_recv.at[1],
            device_id=(partner, group), device_id_type=MESH,
        )

    def pass_chunks(first, last):
        for chunk in range(first, last):
            finish_columns(chunk)
            send_rows(chunk)

    pass_chunks(0, PARTS - 1)
    finish_columns(PARTS - 1)

    @pl.when(group == 0)
    def _():
        send_lead_part()

    send_rows(PARTS - 1)
    pass_chunks(PARTS, 3 * PARTS // 2 - 1)
    finish_columns(3 * PARTS // 2 - 1)

    @pl.when((group == 0) & (child == 0))
    def _():
        sum_lead()

    send_rows(3 * PARTS // 2 - 1)
    pass_chunks(3 * PARTS // 2, 2 * PARTS)

    @pl.when(group == 0)
    def _():
        pass_lead()

    for part in range(PARTS):
        finish_rows(part)

    @pl.when(group == 0)
    def _():
        loads = [
            pltpu.make_async_copy(
                arrived.at[part, :, pl.ds(r * PART, PART), :], first_column.at[part, :, r],
                load_sem.at[part * ROW_SLOTS + r],
            )
            for part in range(PARTS) for r in range(ROW_SLOTS)
        ]
        for load in loads:
            load.start()
        for load in loads:
            load.wait()

        def assemble(i, carry):
            a = lax.rem(i, TR)
            for part in range(PARTS):
                total = jnp.zeros((PART, NB), jnp.float32)
                for k in range(CHILDREN):
                    slot = table_ref[ROW_SLOT + k, a * CHILDREN + child]
                    held = (slot >= 0) & (table_ref[COL_SLOT + k, 0] >= 0)
                    tile = first_column[part, k, jnp.maximum(slot, 0)]
                    total = total + jnp.where(held, tile, 0.0)
                left_panel[a, part * PART:(part + 1) * PART] = total

            @pl.when(a > 0)
            def _():
                spread_copy(a).start()

            return carry

        lax.fori_loop(1, TR + 1, assemble, 0)

    pass_chunks(2 * PARTS, CHUNKS - 1)
    finish_columns(CHUNKS - 1)

    for b in range(TC):
        held = table_ref[COL_SLOT + child, b * GROUPS + group]
        for part in range(PARTS):
            total = jnp.zeros((PART, NB), jnp.float32)
            for slot in range(COL_SLOTS):
                tile = top_tile(slot * PARTS + part)
                total = jnp.where(lead_here & (held == slot), tile, total)
            top_own[b % 2, b // 2, part * PART:(part + 1) * PART] = total
    peer_copy().start()
    peer_copy().wait_recv()
    top_sum[...] = top_own[core] + top_peer[...]
    for i in range(1, RING):
        reduce_copy(i).start()
    send_rows(CHUNKS - 1, 1, RING)

    @pl.when(group != 0)
    def _():
        own_spread().wait_recv()

    def send_share(i, carry):
        @pl.when(lax.rem(group + i, GROUPS) != 0)
        def _():
            share_copy(i).start()
        return carry

    lax.fori_loop(1, GROUPS, send_share, 0)

    @pl.when(group != 0)
    def _():
        lead_copy(0).wait_recv()

    packed[...] = raw_lead[...]
    factor_tile(packed, lower, upper)

    def finish_share(i, carry):
        @pl.when(lax.rem(group + i, GROUPS) != 0)
        def _():
            share_copy(i).wait_send()

        @pl.when(group != 0)
        def _():
            share_copy(i).wait_recv()

        @pl.when(group == 0)
        def _():
            lead_copy(i).wait_send()
            spread_copy(i).wait_send()

        return carry

    lax.fori_loop(1, GROUPS, finish_share, 0)

    for quarter in range(TR // STEP):
        span = slice(quarter * STEP, (quarter + 1) * STEP)
        raw = left_panel[span].reshape(STEP * NB, NB)
        left_panel[span] = full_dot(raw, upper[...]).reshape(STEP, NB, NB)
    lower[...] = permute_columns(pivots, lower[...])

    for i in range(1, RING):
        reduce_copy(i).wait_recv()
    right_panel[core, at_z] = (
        top_sum[at_z] + top_got[turn(at_z, 1)] + top_got[turn(at_z, 2)] + top_got[turn(at_z, 3)]
    )
    for i in range(1, RING):
        top_share_copy(i).start()
    send_rows(CHUNKS - 1, RING, CHILDREN)
    for i in range(1, RING):
        top_share_copy(i).wait_recv()
    peer_share_copy().start()

    @pl.when((group == 0) & (child == 0))
    def _():
        def sent_cast(k, carry):
            lead_cast_copy(k).wait_send()
            return carry

        lax.fori_loop(1, CHILDREN, sent_cast, 0)

    @pl.when((group == 0) & (child != 0))
    def _():
        lead_part_copy(child).wait_send()

    peer_copy().wait_send()
    for i in range(1, RING):
        reduce_copy(i).wait_send()
        top_share_copy(i).wait_send()

    for chunk in range(CHUNKS):
        def sent_columns(i, carry):
            column_copy(chunk, i).wait_send()
            return carry

        lax.fori_loop(1, GROUPS, sent_columns, 0)

    for chunk in range(PARTS, CHUNKS):
        finish_rows(chunk)
    peer_share_copy().wait()

    for chunk in range(CHUNKS):
        def sent_rows(i, carry):
            row_copy(chunk, i).wait_send()
            return carry

        lax.fori_loop(1, CHILDREN, sent_rows, 0)


def exchange(table, front, left, right, lead_block, diag, pivots):
    tile = jax.ShapeDtypeStruct((NB, NB), jnp.float32)
    dma = pltpu.SemaphoreType.DMA
    return pl.pallas_call(
        exchange_kernel,
        out_shape=(
            jax.ShapeDtypeStruct((CHUNKS, CHILDREN, ROW_SLOTS * PART, NB), jnp.float32),
            jax.ShapeDtypeStruct((TR, NB, NB), jnp.float32),
            jax.ShapeDtypeStruct((2, RING, NB, NB), jnp.float32),
            tile, tile, tile,
        ),
        in_specs=[SMEM, ANY, ANY, ANY, VMEM, VMEM, VMEM],
        out_specs=(ANY, VMEM, VMEM, VMEM, VMEM, VMEM),
        scratch_shapes=[
            pltpu.VMEM((RING, ROWS, PIV), jnp.float32),
            pltpu.VMEM((RING, PIV, ROWS), jnp.float32),
            pltpu.VMEM((RING, RING, ROWS, ROWS), jnp.float32),
            pltpu.VMEM((RING, RING, ROWS, ROWS), jnp.float32),
            pltpu.VMEM((ROWS, CB), jnp.float32),
            pltpu.VMEM((CBT, 2, PARTS, PART, NB), jnp.float32),
            pltpu.VMEM((CHUNKS, GROUPS, 2, PART, NB), jnp.float32),
            pltpu.VMEM((CBT, PART, NB), jnp.float32),
            pltpu.VMEM((CBT, PART, NB), jnp.float32),
            pltpu.VMEM((CBT, PART, NB), jnp.float32),
            pltpu.VMEM((CBT, PART, NB), jnp.float32),
            pltpu.VMEM((CBT, PART, NB), jnp.float32),
            pltpu.VMEM((CBT, PART, NB), jnp.float32),
            pltpu.VMEM((CBT, PART, NB), jnp.float32),
            pltpu.VMEM((CBT, PART, NB), jnp.float32),
            pltpu.VMEM((CBT, PART, NB), jnp.float32),
            pltpu.VMEM((CBT, PART, NB), jnp.float32),
            pltpu.VMEM((CBT, PART, NB), jnp.float32),
            pltpu.VMEM((CBT, PART, NB), jnp.float32),
            pltpu.VMEM((CHUNKS, CHILDREN, ROW_SLOTS * PART, NB), jnp.float32),
            pltpu.VMEM((PARTS, CHILDREN, ROW_SLOTS, PART, NB), jnp.float32),
            pltpu.VMEM((NB, NB), jnp.float32),
            pltpu.VMEM((CHILDREN, NB, NB), jnp.float32),
            pltpu.VMEM((2, RING, NB, NB), jnp.float32),
            pltpu.VMEM((RING, NB, NB), jnp.float32),
            pltpu.VMEM((RING, NB, NB), jnp.float32),
            pltpu.VMEM((RING, NB, NB), jnp.float32),
            dma((PARTS * ROW_SLOTS,)), dma((12,)), dma((12,)), dma((16,)), dma((16,)),
            dma((CHUNKS * GROUPS,)), dma((CHUNKS * GROUPS,)), dma((CHUNKS,)),
            dma((CHUNKS * CHILDREN,)), dma((CHUNKS * CHILDREN,)), dma((CHUNKS,)),
            dma((1,)), dma((CHILDREN,)), dma((CHILDREN,)), dma((1,)), dma((GROUPS,)), dma((1,)),
            dma((GROUPS,)), dma((1,)), dma((GROUPS,)), dma((GROUPS,)),
            dma((2,)), dma((2,)), dma((RING,)), dma((RING,)), dma((RING,)), dma((RING,)),
        ],
        compiler_params=pltpu.CompilerParams(
            collective_id=0, has_side_effects=True, vmem_limit_bytes=60 * 2**20
        ),
        name="exchange",
    )(table, front, left, right, lead_block, diag, pivots)


def split(values):
    high = values.astype(jnp.bfloat16)
    return high, (values - high.astype(jnp.float32)).astype(jnp.bfloat16)


def update_kernel(table_ref, arrived_hbm, left_raw, right_panel,
                  packed, lower, diag, out_ref,
                  right, right_parts, total, arrived, arrive_sem):
    step = pl.program_id(0)

    def load(chunk):
        return pltpu.make_async_copy(
            arrived_hbm.at[chunk], arrived.at[chunk], arrive_sem.at[chunk]
        )

    @pl.when(step == 0)
    def _():
        for chunk in range(CHUNKS):
            load(chunk).start()

    child = lax.axis_index("child")
    group = lax.axis_index("grp")
    rows = lax.broadcasted_iota(jnp.int32, (NB, NB), 0)
    cols = lax.broadcasted_iota(jnp.int32, (NB, NB), 1)

    @pl.when(step == 0)
    def _():
        for b in range(TC):
            right[:, b * NB:(b + 1) * NB] = right_panel[b % 2, b // 2]
        right[...] = full_dot(lower[...], right[...])

        @pl.when(group == 0)
        def _():
            right[:, :NB] = jnp.zeros((NB, NB), jnp.float32)

        high, low = split(right[...])
        right_parts[0:NB] = high
        right_parts[NB:2 * NB] = low
        right_parts[2 * NB:] = high

    left = left_raw[...].reshape(STEP * NB, NB)
    high, low = split(left)
    left_parts = jnp.concatenate([high, high, low], axis=1)
    total[...] = -jnp.dot(left_parts, right_parts[...], preferred_element_type=jnp.float32)

    @pl.when(step == 0)
    def _():
        for chunk in range(CHUNKS):
            load(chunk).wait()

    def place(row, carry):
        a = step * STEP + row
        for k in range(CHILDREN):
            row_slot = table_ref[ROW_SLOT + k, a * CHILDREN + child]

            @pl.when(row_slot >= 0)
            def _():
                base = pl.multiple_of(row_slot * PART, PART)
                for b in range(TC):
                    col_slot = table_ref[COL_SLOT + k, b * GROUPS + group]

                    @pl.when(col_slot >= 0)
                    def _():
                        across = pl.ds(b * NB, NB)
                        for part in range(PARTS):
                            down = pl.ds(pl.multiple_of(row * NB, NB) + part * PART, PART)
                            tile = arrived[col_slot * PARTS + part, k, pl.ds(base, PART), :]
                            total[down, across] = total[down, across] + tile

        on_diag = (lax.rem(group, CHILDREN) == child) & (lax.rem(a, 2) == group // CHILDREN)

        @pl.when(on_diag)
        def _():
            across = pl.ds(pl.multiple_of((a // 2) * NB, NB), NB)
            down = pl.ds(pl.multiple_of(row * NB, NB), NB)
            entries = diag[pl.ds(a * CHILDREN + child, 1), :]
            total[down, across] = total[down, across] + jnp.where(rows == cols, entries, 0.0)

        return carry

    lax.fori_loop(0, STEP, place, 0)

    @pl.when(group == 0)
    def _():
        total[:, :NB] = left

    @pl.when((step == 0) & (child == 0))
    def _():
        total[:NB, :] = right[...]

        @pl.when(group == 0)
        def _():
            total[:NB, :NB] = packed[...]

    out_ref[0, :, 0, :] = total[...]


def update_front(table, arrived, left_raw, right_panel, packed, lower, diag):
    return pl.pallas_call(
        update_kernel,
        grid=(TR // STEP,),
        out_shape=jax.ShapeDtypeStruct((1, TR * NB, 1, TC * NB), jnp.float32),
        in_specs=[
            SMEM, ANY,
            pl.BlockSpec((STEP, NB, NB), lambda a: (a, 0, 0)),
            VMEM, VMEM, VMEM, VMEM,
        ],
        out_specs=pl.BlockSpec((1, STEP * NB, 1, TC * NB), lambda a: (0, a, 0, 0)),
        scratch_shapes=[
            pltpu.VMEM((NB, TC * NB), jnp.float32),
            pltpu.VMEM((3 * NB, TC * NB), jnp.bfloat16),
            pltpu.VMEM((STEP * NB, TC * NB), jnp.float32),
            pltpu.VMEM((CHUNKS, CHILDREN, ROW_SLOTS * PART, NB), jnp.float32),
            pltpu.SemaphoreType.DMA((CHUNKS,)),
        ],
        compiler_params=pltpu.CompilerParams(vmem_limit_bytes=60 * 2**20),
        name="update_front",
    )(table, arrived, left_raw, right_panel, packed, lower, diag)


def body(front_child, left_factor, right_factor, child_map, parent_diag, lead_block, pivots):
    diag = parent_diag.reshape(PT, NB)
    pivot_row = pivots.reshape(1, NB)
    table = slot_table(child_map)
    arrived, left_raw, right_panel, packed, lower, _ = exchange(
        table, front_child[0], left_factor[0], right_factor[0], lead_block, diag, pivot_row
    )
    return update_front(table, arrived, left_raw, right_panel, packed, lower, diag)


def solution(mesh):
    in_specs = (
        P("child", "grp", None),
        P("child", "grp", None),
        P("child", None, "grp"),
        P(),
        P(),
        P(),
        P(),
    )
    out_specs = P("child", None, "grp", None)
    return jax.shard_map(body, mesh=mesh, in_specs=in_specs, out_specs=out_specs, check_vma=False)
```
